128 devices in a mesh: fsdp: 8 (over y, core), seq: 16 (over z, x).
Axes of the slice: x: 4, y: 4, z: 4, core: 2. Of those that a mesh axis runs over, the one named last changes fastest.
Arguments:
- tokens: bfloat16 [8, 2048, 2048], P('fsdp', 'seq'), may hold values from -6 to 6
- cotangent: bfloat16 [8, 2048, 2048], P('fsdp', 'seq'), may hold values from -6 to 6
- doc_starts: int32 [8, 8], P('fsdp'), may hold values from 0 to 2047, as said below
- ln_gain: bfloat16 [2048], P(('fsdp', 'seq')), may hold values from 0.5 to 1.5
- ln_bias: bfloat16 [2048], P(('fsdp', 'seq')), may hold values from -0.625 to 0.625
- w_qkv: bfloat16 [2048, 6144], P('fsdp', 'seq'), may hold values from -0.125 to 0.125
- b_qkv: bfloat16 [6144], P(('fsdp', 'seq')), may hold values from -0.3125 to 0.3125
- w_out: bfloat16 [2048, 2048], P('seq', 'fsdp'), may hold values from -1.5 to 1.5
- b_out: bfloat16 [2048], P(('fsdp', 'seq')), may hold values from -1.25 to 1.25
- w_fc1: bfloat16 [2048, 8192], P('fsdp', 'seq'), may hold values from -0.125 to 0.125
- b_fc1: bfloat16 [8192], P(('fsdp', 'seq')), may hold values from -0.625 to 0.625
- w_fc2: bfloat16 [8192, 2048], P('seq', 'fsdp'), may hold values from -0.0625 to 0.0625
- b_fc2: bfloat16 [2048], P(('fsdp', 'seq')), may hold values from -1.25 to 1.25
Outputs:
- output: bfloat16 [8, 2048, 2048], P('fsdp', 'seq')
- input_grad: float32 [8, 2048, 2048], P('fsdp', 'seq')
- ln_gain_grad: float32 [2048], P(('fsdp', 'seq'))
- ln_bias_grad: float32 [2048], P(('fsdp', 'seq'))
- w_qkv_grad: float32 [2048, 6144], P('fsdp', 'seq')
- b_qkv_grad: float32 [6144], P(('fsdp', 'seq'))
- w_out_grad: float32 [2048, 2048], P('seq', 'fsdp')
- b_out_grad: float32 [2048], P(('fsdp', 'seq'))
- w_fc1_grad: float32 [2048, 8192], P('fsdp', 'seq')
- b_fc1_grad: float32 [8192], P(('fsdp', 'seq'))
- w_fc2_grad: float32 [8192, 2048], P('seq', 'fsdp')
- b_fc2_grad: float32 [2048], P(('fsdp', 'seq'))
The draws below stay inside these ranges and needn't reach their ends.
Inputs may be any that keep to these rules, and one draw needn't show every extreme that they name: `doc_starts`: each row rises strictly, begins with 0 and ends with 2047.
All inputs are finite; a program needn't handle non-finite values.
Results may differ from the reference program's by a relative error of at most 0.019.
Values may be sent and summed in bfloat16 or wider, within the bound.
No kernel may reach another device: no remote copies, remote signals or barrier semaphores. Data moves between devices by JAX's collectives and lax.ppermute only.
A program may use at most 448 MiB of HBM per device.

```python
import math
import jax
import jax.numpy as jnp
from jax import lax

D = 2048
HEADS = 32
HEAD_DIM = 64
ROT = 32
FF = 8192
TOK_DEV = 128
NDOC = 8
SEQ_LEN = 2048
GROUPS = 8


def draw_doc_starts(key, part):
    key = jax.random.fold_in(key, 11)
    pick_key, streams_key = jax.random.split(key)
    spanning = jax.random.randint(pick_key, (), 0, GROUPS)

    def one_stream(stream_key, stream_index):
        head_key, tail_key, spread_key = jax.random.split(stream_key, 3)
        early = jnp.sort(jax.random.permutation(head_key, jnp.arange(1, TOK_DEV, dtype=jnp.int32))[:4])
        late = jnp.sort(jax.random.permutation(tail_key, jnp.arange(SEQ_LEN - TOK_DEV + 1, SEQ_LEN - 1, dtype=jnp.int32))[:NDOC - 6])
        spread = jnp.sort(jax.random.permutation(spread_key, jnp.arange(1, SEQ_LEN - 1, dtype=jnp.int32))[:NDOC - 2])
        inner = jnp.where(stream_index == spanning, jnp.concatenate([early, late]), spread)
        final = jnp.full((1,), SEQ_LEN - 1, jnp.int32)
        return jnp.concatenate([jnp.zeros((1,), jnp.int32), inner, final])
    return jax.vmap(one_stream)(jax.random.split(streams_key, GROUPS), jnp.arange(GROUPS, dtype=jnp.int32))


def strengthened(values, key, source, target, parts, factor):
    def block_of(dim):
        return (jnp.arange(values.shape[dim]) // (values.shape[dim] // parts)).reshape((-1,) + (1,) * (values.ndim - 1 - dim))

    near = jax.random.permutation(key, parts)[block_of(target)]
    far = (block_of(target) + parts // 2) % parts
    return jnp.where((block_of(source) == near) | (block_of(source) == far), factor * values, values)


def steps_of(key, extent, shards, low, top_value):
    factor_of = 1.0
    for dim, blocks in shards:
        draws = jax.random.uniform(jax.random.fold_in(jax.random.fold_in(key, 6), dim), (blocks,), jnp.float32, low / len(shards), top_value / len(shards))
        factor_of = factor_of * jnp.repeat(jnp.exp(draws), extent[dim] // blocks).reshape((-1,) + (1,) * (len(extent) - 1 - dim))
    return factor_of


def scatter_about(key, dims, scale, most, cuts=(), kind=jnp.bfloat16):
    factor_of = steps_of(key, dims, cuts, -0.22, 0.18) if cuts else 1.0
    entries = jax.random.normal(key, dims, jnp.float32) * scale * factor_of
    return jnp.minimum(jnp.maximum(entries, -most), most).astype(kind)


def heavy_noise(own_key, extent, width, bound, cuts, heavy, kind=jnp.bfloat16):
    values = width * jax.random.normal(own_key, extent, jnp.float32)
    if cuts:
        values = values * steps_of(own_key, extent, cuts, -0.22, 0.18)
    return jnp.clip(strengthened(values, jax.random.fold_in(own_key, 3), *heavy), -bound, bound).astype(kind)


def setup_inputs(seed: int = 0) -> dict:
    arg_keys = jax.random.split(jax.random.key(seed), 14)
    return {
        "tokens": scatter_about(arg_keys[0], (GROUPS, SEQ_LEN, D), 1.0, 6.0, ((0, 8), (1, 16))),
        "cotangent": heavy_noise(arg_keys[1], (GROUPS, SEQ_LEN, D), 1.0, 6.0, ((0, 8), (1, 16)), (1, 2, 16, 2.0)),
        "doc_starts": draw_doc_starts(jax.random.fold_in(arg_keys[13], 71), 0),
        "ln_gain": jnp.clip(1.0 + 0.1 * jax.random.normal(arg_keys[3], (D,), jnp.float32), 0.5, 1.5).astype(jnp.bfloat16),
        "ln_bias": scatter_about(arg_keys[4], (D,), 0.1, 0.625, ((0, 128),)),
        "w_qkv": scatter_about(arg_keys[5], (D, 3 * D), D ** -0.5, 0.125, ((0, 8), (1, 16))),
        "b_qkv": scatter_about(arg_keys[6], (3 * D,), 0.05, 0.3125, ((0, 128),)),
        "w_out": scatter_about(arg_keys[7], (D, D), (max(D // 128, 1)) ** -0.5, 1.5, ((0, 16), (1, 8))),
        "b_out": scatter_about(arg_keys[8], (D,), 0.2, 1.25, ((0, 128),)),
        "w_fc1": scatter_about(arg_keys[9], (D, FF), D ** -0.5, 0.125, ((0, 8), (1, 16))),
        "b_fc1": scatter_about(arg_keys[10], (FF,), 0.1, 0.625, ((0, 128),)),
        "w_fc2": scatter_about(arg_keys[11], (FF, D), FF ** -0.5, 0.0625, ((0, 16), (1, 8))),
        "b_fc2": scatter_about(arg_keys[12], (D,), 0.2, 1.25, ((0, 128),)),
    }


@jax.custom_vjp
def low(v):
    return lax.optimization_barrier(v.astype(jnp.bfloat16)).astype(jnp.float32)

@jax.custom_vjp
def low_back(v):
    return v

def low_keep(v):
    return (low(v), None)

def low_pass(kept, grad):
    return (grad,)

def back_keep(v):
    return (v, None)

def back_low(kept, grad):
    return (low(grad),)
low.defvjp(low_keep, low_pass)
low_back.defvjp(back_keep, back_low)
norm_eps = 1e-05

def exact_dot(left, right):
    return jnp.dot(left, right, precision=lax.Precision.HIGHEST, preferred_element_type=jnp.float32)

def doc_tables(starts):
    token_index = jnp.arange(SEQ_LEN, dtype=jnp.int32)
    before = starts[None, :] <= token_index[:, None]
    segment = lax.optimization_barrier(jnp.sum(before.astype(jnp.int32), axis=1))
    first_start = lax.optimization_barrier(jnp.max(jnp.where(before, starts[None, :], 0), axis=1))
    return (segment, token_index - first_start)

def angle_tables(position):
    half_rot = ROT // 2
    frequency = jnp.exp(jnp.arange(half_rot, dtype=jnp.float32) * (-2.0 * math.log(10000.0) / ROT))
    phases = position.astype(jnp.float32)[:, None] * frequency[None, :]
    return (jnp.cos(phases), jnp.sin(phases))

def rotate(vectors, cosine, sine_table):
    half_rot = ROT // 2
    first_half = vectors[..., :half_rot]
    second_half = vectors[..., half_rot:ROT]
    cos_wide = cosine[:, None, :]
    sin_wide = sine_table[:, None, :]
    return jnp.concatenate([first_half * cos_wide - second_half * sin_wide, second_half * cos_wide + first_half * sin_wide, vectors[..., ROT:]], axis=-1)

def head_attention(q_head, k_head, v_head, allowed):
    raw_scores = low_back(exact_dot(q_head, k_head.T)) * HEAD_DIM ** (-0.5)
    masked = jnp.where(allowed, raw_scores, -1e+30)
    row_peak = lax.optimization_barrier(jnp.max(masked, axis=1, keepdims=True))
    exp_terms = jnp.exp(masked - row_peak)
    probabilities = exp_terms / lax.optimization_barrier(jnp.sum(exp_terms, axis=1, keepdims=True))
    return exact_dot(low(probabilities), v_head)

def forward_layer(inputs_wide, params, allowed, cosine, sine_table):
    ln_gain, ln_bias, w_qkv, b_qkv, w_out, b_out, w_fc1, b_fc1, w_fc2, b_fc2 = params
    mean_row = lax.optimization_barrier(jnp.mean(inputs_wide, axis=1, keepdims=True))
    centered = inputs_wide - mean_row
    variance = lax.optimization_barrier(jnp.mean(centered * centered, axis=1, keepdims=True))
    normed = low(centered * lax.rsqrt(variance + norm_eps) * ln_gain + ln_bias)
    projected = low_back(low(exact_dot(normed, w_qkv) + b_qkv)).reshape(SEQ_LEN, HEADS, 3, HEAD_DIM)
    queries = low(rotate(projected[:, :, 0], cosine, sine_table))
    keys_rot = low(rotate(projected[:, :, 1], cosine, sine_table))
    values = projected[:, :, 2]

    def one_head(items):
        return head_attention(items[0], items[1], items[2], allowed)
    per_head = lax.map(jax.checkpoint(one_head), (jnp.transpose(queries, (1, 0, 2)), jnp.transpose(keys_rot, (1, 0, 2)), jnp.transpose(values, (1, 0, 2))))
    attended = low_back(low(jnp.transpose(per_head, (1, 0, 2)).reshape(SEQ_LEN, HEADS * HEAD_DIM)))
    attn_out = exact_dot(attended, w_out) + b_out
    hidden_pre = low_back(exact_dot(normed, w_fc1) + b_fc1)
    activated = low(jax.nn.gelu(hidden_pre, approximate=True))
    mlp_out = exact_dot(activated, w_fc2) + b_fc2
    return inputs_wide + attn_out + mlp_out

def reference(tokens, cotangent, doc_starts, ln_gain, ln_bias, w_qkv, b_qkv, w_out, b_out, w_fc1, b_fc1, w_fc2, b_fc2):
    params = tuple((array.astype(jnp.float32) for array in (ln_gain, ln_bias, w_qkv, b_qkv, w_out, b_out, w_fc1, b_fc1, w_fc2, b_fc2)))

    def one_group(running, slices):
        stream_in, stream_grad, starts = slices
        segment, position = doc_tables(starts)
        token_index = jnp.arange(SEQ_LEN, dtype=jnp.int32)
        allowed = (segment[:, None] == segment[None, :]) & (token_index[None, :] <= token_index[:, None])
        cosine, sine_table = angle_tables(position)

        def layer_fn(inputs_wide, layer_params):
            return forward_layer(inputs_wide, layer_params, allowed, cosine, sine_table)
        result, pull_back = jax.vjp(layer_fn, stream_in.astype(jnp.float32), params)
        grad_input, grad_params = pull_back(stream_grad.astype(jnp.float32))
        new_running = tuple((total + piece for total, piece in zip(running, grad_params)))
        return (new_running, (result.astype(jnp.bfloat16), grad_input))
    start_totals = tuple((jnp.zeros(array.shape, jnp.float32) for array in params))
    totals, (output, input_grad) = lax.scan(one_group, start_totals, (tokens, cotangent, doc_starts))
    return (output, input_grad, totals[0], totals[1], totals[2], totals[3], totals[4], totals[5], totals[6], totals[7], totals[8], totals[9])
```

```python
import functools
import math

import jax
import jax.numpy as jnp
import numpy as np
from jax import lax
from jax.experimental import pallas as pl
from jax.experimental.pallas import tpu as pltpu
from jax.sharding import Mesh
from jax.sharding import PartitionSpec as P

BF = jnp.bfloat16
F32 = jnp.float32
EPS = 1e-05
VMEM_MIB = 60
D = 2048
LEN = 2048
ROWS = 512
TOK = 128
HALF = 64
QKV = 384
HID = 512
ATT = 128
PIECE = 256
FS = 8
NEG = -1e30


SMALL = pl.CostEstimate(flops=1, bytes_accessed=1, transcendentals=0)
LARGE = pl.CostEstimate(flops=100 * 2**30, bytes_accessed=320 * 2**20, transcendentals=0)


def params():
    return pltpu.CompilerParams(vmem_limit_bytes=VMEM_MIB * 2**20, dimension_semantics=("arbitrary",))


VM = pl.BlockSpec(memory_space=pltpu.VMEM)
SM = pl.BlockSpec(memory_space=pltpu.SMEM)
ANY = pl.BlockSpec(memory_space=pltpu.HBM)


def whole(shape):
    return pl.BlockSpec(shape, lambda i, *_: (0,) * len(shape))


def rows_of(width):
    return pl.BlockSpec((ROWS, width), lambda i, *_: (i, 0))


def piece_start(place_ref, block, piece):
    first = block < 4
    z_off = jnp.where(first, block, piece)
    x_off = jnp.where(first, piece, block - 4)
    seq = lax.rem(place_ref[0] + z_off, 4) * 4 + lax.rem(place_ref[1] + x_off, 4)
    return pl.multiple_of(seq * TOK + jnp.where(first, 0, HALF), HALF)


def gather_pieces(place_ref, ref, block):
    return jnp.concatenate(
        [ref[pl.ds(piece_start(place_ref, block, s), HALF), :] for s in range(4)], axis=0
    )


def turn(v, c, sa, sb):
    return v * c + pltpu.roll(v, 112, 1) * sa + pltpu.roll(v, 16, 1) * sb


def pack_body(*refs):
    ins, (w_ref, vec_ref, a_ref, b_ref), scr, sem = refs[:11], refs[11:15], refs[15:25], refs[25]
    copies = [pltpu.make_async_copy(ins[k], scr[k], sem.at[k]) for k in range(10)]
    copies += [
        pltpu.make_async_copy(ins[10].at[k * HALF : (k + 1) * HALF], ref, sem.at[10 + k])
        for k, ref in enumerate((a_ref, b_ref))
    ]
    for copy in copies:
        copy.start()
    for copy in copies[:10]:
        copy.wait()
    wq_ref, w1_ref, wo_ref, w2_ref = scr[:4]
    low = lax.broadcasted_iota(jnp.int32, (PIECE, 128), 1) < 64
    g0, g1, g2 = [wq_ref[:, k * 128 : (k + 1) * 128].astype(F32) for k in range(3)]
    w_ref[0, 0:256, :128] = jnp.where(low, g0, g1).astype(BF)
    w_ref[0, 0:256, 128:] = pltpu.roll(jnp.where(low, g2, g0), 64, 1).astype(BF)
    w_ref[0, 256:512, :128] = jnp.where(low, g1, g2).astype(BF)
    w_ref[0, 256:512, 128:] = w1_ref[:, :128]
    w_ref[0, 512:768] = w1_ref[:, 128:384]
    w_ref[1, 0:128, :128] = w1_ref[:128, 384:]
    w_ref[1, 0:128, 128:] = w1_ref[128:, 384:]
    w_ref[1, 128:256] = wo_ref[...]
    w_ref[1, 256:768] = w2_ref[...]
    for k, ref in enumerate(scr[4:]):
        vec_ref[k : k + 1, : ref.shape[1]] = ref[...].astype(F32)
    for copy in copies[10:]:
        copy.wait()


def pack(*arrays):
    flat = [a if a.ndim == 2 else a[None, :] for a in arrays]
    return pl.pallas_call(
        pack_body,
        in_specs=[ANY] * 11,
        out_specs=[VM, VM, VM, VM],
        out_shape=[
            jax.ShapeDtypeStruct((2, 768, PIECE), BF),
            jax.ShapeDtypeStruct((8, 128), F32),
            jax.ShapeDtypeStruct((HALF, D), BF),
            jax.ShapeDtypeStruct((HALF, D), BF),
        ],
        scratch_shapes=[pltpu.VMEM(a.shape, BF) for a in flat[:10]] + [pltpu.SemaphoreType.DMA((12,))],
        cost_estimate=SMALL,
        compiler_params=pltpu.CompilerParams(vmem_limit_bytes=VMEM_MIB * 2**20),
        name="pack",
    )(*flat)


def document_start(starts_ref, token):
    first = jnp.zeros(token.shape, jnp.int32)
    for n in range(starts_ref.shape[1]):
        begin = starts_ref[0, n]
        first = jnp.where(token >= begin, begin, first)
    return first


def angles_body(starts_ref, c_ref, sa_ref, sb_ref, start_ref):
    block = pl.program_id(0)
    shape = (ROWS, 128)
    token = block * ROWS + lax.broadcasted_iota(jnp.int32, shape, 0)
    lane = lax.rem(lax.broadcasted_iota(jnp.int32, shape, 1), 64)
    freq = jnp.exp(lax.rem(lane, 16).astype(F32) * (-2.0 * math.log(10000.0) / 32))
    phase = (token - document_start(starts_ref, token)).astype(F32) * freq
    sin = jnp.sin(phase)
    c_ref[...] = jnp.where(lane < 32, jnp.cos(phase), 1.0)
    sa_ref[...] = jnp.where(lane < 16, -sin, 0.0)
    sb_ref[...] = jnp.where((lane >= 16) & (lane < 32), sin, 0.0)
    here = block * ROWS + lax.broadcasted_iota(jnp.int32, (1, ROWS), 1)
    start_ref[...] = document_start(starts_ref, here)


def angles(starts):
    return pl.pallas_call(
        angles_body,
        grid=(LEN // ROWS,),
        in_specs=[SM],
        out_specs=[rows_of(128), rows_of(128), rows_of(128), pl.BlockSpec((1, ROWS), lambda i: (0, i))],
        out_shape=[jax.ShapeDtypeStruct((LEN, 128), F32)] * 3 + [jax.ShapeDtypeStruct((1, LEN), jnp.int32)],
        cost_estimate=SMALL,
        compiler_params=params(),
        name="angles",
    )(starts)


def unpack_last(w_ref, last_ref):
    for f in range(FS):
        for k in range(2):
            at = f * PIECE + k * 128
            last_ref[at : at + 128, :] = w_ref[f, 0, :, k * 128 : (k + 1) * 128]


W_FIRST = pl.BlockSpec((FS, 1, 768, PIECE), lambda *_: (0, 0, 0, 0))
W_LAST = pl.BlockSpec((FS, 1, 128, PIECE), lambda *_: (0, 1, 0, 0))
WIDTHS = (D, QKV, HID, HID)


ORDER = (0, 1, 3, 2)


def project_body(
    x_ref, gain_ref, bias_ref, w_ref, wl_ref, b_ref, c_ref, sa_ref, sb_ref,
    normed_ref, qkv_ref, act_ref, slope_ref, last_ref,
):
    @pl.when(pl.program_id(0) == 0)
    def _():
        unpack_last(wl_ref, last_ref)

    x = x_ref[...].astype(F32)
    centered = x - jnp.mean(x, axis=1, keepdims=True)
    inv = lax.rsqrt(jnp.mean(centered * centered, axis=1, keepdims=True) + EPS)
    normed_ref[...] = (centered * inv * gain_ref[...] + bias_ref[...]).astype(BF)

    def group(j):
        normed = normed_ref[...]
        if j == 3:
            return jnp.dot(normed, last_ref[...], preferred_element_type=F32) + b_ref[:, 768:]
        w = w_ref[:, 0, j * 256 : (j + 1) * 256].reshape(D, PIECE)
        return jnp.dot(normed, w, preferred_element_type=F32) + b_ref[:, j * 256 : (j + 1) * 256]

    c, sa, sb = c_ref[...], sa_ref[...], sb_ref[...]

    def hidden(h, cols):
        k0 = math.sqrt(2.0 / math.pi)
        h2 = h * h
        t = jnp.tanh(h * (k0 + (k0 * 0.044715) * h2))
        act_ref[:, cols] = (0.5 * h * (1.0 + t)).astype(BF)
        slope = 0.5 * (1.0 + t) + 0.5 * h * (1.0 - t * t) * (k0 + (3 * 0.044715 * k0) * h2)
        slope_ref[:, cols] = slope.astype(BF)

    qk = group(0).astype(BF).astype(F32)
    qkv_ref[:, 0:128] = (turn(qk[:, :128], c, sa, sb) * 0.125).astype(BF)
    qkv_ref[:, 128:256] = turn(qk[:, 128:], c, sa, sb).astype(BF)
    vh = group(1)
    qkv_ref[:, 256:384] = vh[:, :128].astype(BF)
    hidden(vh[:, 128:], slice(0, 128))
    hidden(group(2), slice(128, 384))
    hidden(group(3), slice(384, 512))


def project(x, gain, bias, w, b, tables):
    return pl.pallas_call(
        project_body,
        grid=(LEN // ROWS,),
        in_specs=[
            rows_of(D), whole((1, D)), whole((1, D)), W_FIRST, W_LAST, whole((1, QKV + HID)),
            rows_of(128), rows_of(128), rows_of(128),
        ],
        out_specs=[rows_of(D), rows_of(QKV), rows_of(HID), rows_of(HID)],
        out_shape=[
            jax.ShapeDtypeStruct((LEN, D), BF),
            jax.ShapeDtypeStruct((LEN, QKV), BF),
            jax.ShapeDtypeStruct((LEN, HID), BF),
            jax.ShapeDtypeStruct((LEN, HID), BF),
        ],
        scratch_shapes=[pltpu.VMEM((D, 128), BF)],
        cost_estimate=LARGE,
        compiler_params=params(),
        name="project",
    )(x, gain, bias, w, w, b, *tables)


AQ = 512
AK = 256
NQ = LEN // AQ


def padded_turned(ref, scr):
    row = lax.broadcasted_iota(jnp.int32, (128, AQ), 0)
    for i in range(NQ):
        cols = slice(i * AQ, (i + 1) * AQ)
        t = ref[cols, :].astype(F32).T
        scr[0, :, cols] = jnp.where(row < 64, t, 0.0).astype(BF)
        scr[1, :, cols] = jnp.where(row < 64, 0.0, t).astype(BF)


def padded(ref, scr):
    lane = lax.broadcasted_iota(jnp.int32, (AQ, 128), 1)
    for i in range(NQ):
        rows = slice(i * AQ, (i + 1) * AQ)
        v = ref[rows, :].astype(F32)
        scr[0, rows, :] = jnp.where(lane < 64, v, 0.0).astype(BF)
        scr[1, rows, :] = jnp.where(lane < 64, 0.0, v).astype(BF)


def fold(op, v):
    return op(v.reshape(AK // 8, 8, AQ), axis=0)


def attend_body(first_ref, qkv_ref, start_ref, att_ref, lse_ref, qt_scr, vt_scr, s_scr):
    padded_turned(qkv_ref.at[:, 0:128], qt_scr)
    for i in range(NQ):
        rows = slice(i * AQ, (i + 1) * AQ)
        vt_scr[:, rows] = qkv_ref[rows, 256:384].astype(F32).T.astype(BF)
    row = lax.broadcasted_iota(jnp.int32, (AK, AQ), 0)
    col = lax.broadcasted_iota(jnp.int32, (AK, AQ), 1)

    def q_block(i, _):
        cols = pl.ds(pl.multiple_of(i * AQ, AQ), AQ)
        start = start_ref[:, cols]
        qt = [qt_scr[h, :, cols] for h in range(2)]

        def scores(j, ok, peaks):
            rows = pl.ds(pl.multiple_of(j * AK, AK), AK)
            k = qkv_ref[rows, 128:256]
            new = []
            for h in range(2):
                s = jnp.dot(k, qt[h], preferred_element_type=F32)
                s = jnp.where(ok, s, NEG)
                s_scr[h, rows, :] = s
                new.append(jnp.maximum(peaks[h], fold(jnp.max, s)))
            return tuple(new)

        low = first_ref[i]
        peaks = (jnp.full((8, AQ), NEG, F32),) * 2
        for d in range(2):
            peaks = scores(2 * i + d, (row + (2 * i + d) * AK >= start) & (row + d * AK <= col), peaks)
        peaks = lax.fori_loop(low, 2 * i, lambda j, p: scores(j, row + j * AK >= start, p), peaks)
        peak = [jnp.max(p, axis=0, keepdims=True) for p in peaks]

        def values(j, state):
            rows = pl.ds(pl.multiple_of(j * AK, AK), AK)
            new = []
            for h in range(2):
                total, o = state[2 * h : 2 * h + 2]
                p = jnp.exp(s_scr[h, rows, :] - peak[h])
                total = total + fold(jnp.sum, p)
                o = o + jnp.dot(
                    vt_scr[64 * h : 64 * h + 64, rows], p.astype(BF), preferred_element_type=F32
                )
                new += [total, o]
            return tuple(new)

        state = (jnp.zeros((8, AQ), F32), jnp.zeros((64, AQ), F32)) * 2
        state = lax.fori_loop(low, 2 * i + 2, values, state)
        total = [jnp.sum(state[2 * h], axis=0, keepdims=True) for h in range(2)]
        both = jnp.concatenate([state[1] / total[0], state[3] / total[1]], axis=0)
        att_ref[cols, :] = both.T.astype(BF)
        for h in range(2):
            lse_ref[h : h + 1, cols] = peak[h] + jnp.log(total[h])
        return 0

    lax.fori_loop(0, NQ, q_block, 0)


def attend(first, qkv, start):
    return pl.pallas_call(
        attend_body,
        in_specs=[SM, VM, VM],
        out_specs=[VM, VM],
        out_shape=[
            jax.ShapeDtypeStruct((LEN, ATT), BF),
            jax.ShapeDtypeStruct((2, LEN), F32),
        ],
        scratch_shapes=[
            pltpu.VMEM((2, 128, LEN), BF),
            pltpu.VMEM((128, LEN), BF),
            pltpu.VMEM((2, LEN, AQ), F32),
        ],
        cost_estimate=LARGE,
        compiler_params=pltpu.CompilerParams(vmem_limit_bytes=VMEM_MIB * 2**20),
        name="attend",
    )(first, qkv, start)


def attend_back_body(
    first_ref, qkv_ref, att_ref, ga_ref, lse_ref, start_ref, c_ref, sa_ref, sb_ref,
    gqkv_ref, bsum_ref,
    q_scr, go_scr, qt_scr, got_scr, kt_scr, dl_scr, dk_scr, dv_scr,
):
    padded(qkv_ref.at[:, 0:128], q_scr)
    padded(ga_ref, go_scr)
    padded_turned(qkv_ref.at[:, 0:128], qt_scr)
    for i in range(NQ):
        rows = slice(i * AQ, (i + 1) * AQ)
        kt_scr[:, rows] = qkv_ref[rows, 128:256].astype(F32).T.astype(BF)
        got = ga_ref[rows, :].astype(F32).T
        prod = got * att_ref[rows, :].astype(F32).T
        row = lax.broadcasted_iota(jnp.int32, (128, AQ), 0)
        got_scr[0, :, rows] = jnp.where(row < 64, got, 0.0).astype(BF)
        got_scr[1, :, rows] = jnp.where(row < 64, 0.0, got).astype(BF)
        for h in range(2):
            dl_scr[h : h + 1, rows] = jnp.sum(prod[64 * h : 64 * h + 64], axis=0, keepdims=True)
    dk_scr[...] = jnp.zeros_like(dk_scr)
    dv_scr[...] = jnp.zeros_like(dv_scr)
    row = lax.broadcasted_iota(jnp.int32, (AK, AQ), 0)
    col = lax.broadcasted_iota(jnp.int32, (AK, AQ), 1)

    def q_block(i, bsum):
        cols = pl.ds(pl.multiple_of(i * AQ, AQ), AQ)
        start = start_ref[:, cols]
        lse = [lse_ref[h : h + 1, cols] for h in range(2)]
        dl = [dl_scr[h : h + 1, cols] for h in range(2)]

        def pair(j, ok, dq):
            rows = pl.ds(pl.multiple_of(j * AK, AK), AK)
            k = qkv_ref[rows, 128:256]
            v = qkv_ref[rows, 256:384]
            dv = dk = 0.0
            new = []
            for h in range(2):
                s = jnp.dot(k, qt_scr[h, :, cols], preferred_element_type=F32)
                dp = jnp.dot(v, got_scr[h, :, cols], preferred_element_type=F32)
                p = jnp.where(ok, jnp.exp(s - lse[h]), 0.0)
                ds = (p * (dp - dl[h])).astype(BF)
                dv += jnp.dot(p.astype(BF), go_scr[h, cols, :], preferred_element_type=F32)
                dk += jnp.dot(ds, q_scr[h, cols, :], preferred_element_type=F32)
                new.append(
                    dq[h]
                    + jnp.dot(kt_scr[64 * h : 64 * h + 64, rows], ds, preferred_element_type=F32)
                )
            dv_scr[rows, :] += dv
            dk_scr[rows, :] += dk
            return tuple(new)

        dq = (jnp.zeros((64, AQ), F32),) * 2
        for d in range(2):
            dq = pair(2 * i + d, (row + (2 * i + d) * AK >= start) & (row + d * AK <= col), dq)
        dq = lax.fori_loop(first_ref[i], 2 * i, lambda j, dq: pair(j, row + j * AK >= start, dq), dq)
        dq = (jnp.concatenate(dq, axis=0) * 0.125).T
        out = turn(dq, c_ref[cols, :], -sa_ref[cols, :], -sb_ref[cols, :]).astype(BF)
        gqkv_ref[cols, 0:128] = out
        return bsum + jnp.sum(out.astype(F32), axis=0, keepdims=True)

    bsum_ref[:, 0:128] = lax.fori_loop(0, NQ, q_block, jnp.zeros((1, 128), F32))

    def finish(i, total):
        rows = pl.ds(pl.multiple_of(i * AQ, AQ), AQ)
        dk = turn(dk_scr[rows, :], c_ref[rows, :], -sa_ref[rows, :], -sb_ref[rows, :])
        out = jnp.concatenate([dk, dv_scr[rows, :]], axis=1).astype(BF)
        gqkv_ref[rows, 128:384] = out
        return total + jnp.sum(out.astype(F32), axis=0, keepdims=True)

    bsum_ref[:, 128:384] = lax.fori_loop(0, NQ, finish, jnp.zeros((1, 256), F32))


def attend_back(first, qkv, att, ga, lse, start, tables):
    return pl.pallas_call(
        attend_back_body,
        in_specs=[SM] + [VM] * 8,
        out_specs=[VM, VM],
        out_shape=[
            jax.ShapeDtypeStruct((LEN, QKV), BF),
            jax.ShapeDtypeStruct((1, QKV), F32),
        ],
        scratch_shapes=[
            pltpu.VMEM((2, LEN, 128), BF),
            pltpu.VMEM((2, LEN, 128), BF),
            pltpu.VMEM((2, 128, LEN), BF),
            pltpu.VMEM((2, 128, LEN), BF),
            pltpu.VMEM((128, LEN), BF),
            pltpu.VMEM((2, LEN), F32),
            pltpu.VMEM((LEN, 128), F32),
            pltpu.VMEM((LEN, 128), F32),
        ],
        cost_estimate=LARGE,
        compiler_params=pltpu.CompilerParams(vmem_limit_bytes=VMEM_MIB * 2**20),
        name="attend_back",
    )(first, qkv, att, ga, lse, start, *tables)


def emit_body(att_ref, act_ref, w_ref, out_ref):
    both = jnp.concatenate([att_ref[...], act_ref[...]], axis=1)
    for f in range(FS):
        out_ref[:, f * PIECE : (f + 1) * PIECE] = jnp.dot(
            both, w_ref[f, 0, 128:], preferred_element_type=F32
        ).astype(BF)


def emit(att, act, w):
    return pl.pallas_call(
        emit_body,
        grid=(LEN // ROWS,),
        in_specs=[rows_of(ATT), rows_of(HID), pl.BlockSpec((FS, 1, 768, PIECE), lambda i, *_: (0, 1, 0, 0))],
        out_specs=rows_of(D),
        out_shape=jax.ShapeDtypeStruct((LEN, D), BF),
        cost_estimate=LARGE,
        compiler_params=params(),
        name="emit",
    )(att, act, w)


def emit_back_body(place_ref, *refs):
    a_refs, b_refs, (w_ref, slope_ref, ga_ref, gh_ref, bsum_ref, g_scr, sem) = refs[:5], refs[5:10], refs[10:]
    step = pl.program_id(0)
    slot = lax.rem(step, 2)
    turn_no = jnp.int32(ORDER[0])
    for k in range(1, 4):
        turn_no = jnp.where(step == k, ORDER[k], turn_no)

    def fetch(k):
        for side, side_refs in enumerate((a_refs, b_refs)):
            at = side * PIECE
            for ref in (side_refs[:1], side_refs[1:2], side_refs[4:], side_refs[2:4])[k]:
                pltpu.make_async_copy(
                    ref, g_scr.at[k % 2, at : at + ref.shape[0]], sem.at[k % 2, side]
                ).start()
                at += ref.shape[0]

    @pl.when(step == 0)
    def _():
        fetch(0)
        bsum_ref[...] = jnp.zeros_like(bsum_ref)

    for k in range(3):

        @pl.when(step == k)
        def _():
            fetch(k + 1)

    for side in range(2):
        pltpu.make_async_copy(
            a_refs[0], g_scr.at[slot, side * PIECE : (side + 1) * PIECE], sem.at[slot, side]
        ).wait()
    total = jnp.zeros((ROWS, ATT + HID), F32)
    for f in range(FS):
        total += lax.dot_general(
            g_scr[slot, :, f * PIECE : (f + 1) * PIECE], w_ref[f, 0, 128:], (((1,), (1,)), ((), ())),
            preferred_element_type=F32,
        )
    for m in range(8):
        rows = slice(m * HALF, (m + 1) * HALF)
        spot = pl.ds(piece_start(place_ref, turn_no + 4 * (m // 4), m % 4), HALF)
        ga_ref[spot, :] = total[rows, :ATT].astype(BF)
        gh = (total[rows, ATT:] * slope_ref[spot, :].astype(F32)).astype(BF)
        gh_ref[spot, :] = gh
        bsum_ref[...] += jnp.sum(gh.astype(F32), axis=0, keepdims=True)


def emit_back(place, g_a, g_b, w, slope):
    return pl.pallas_call(
        emit_back_body,
        grid=(4,),
        in_specs=[SM] + [ANY] * 10
        + [pl.BlockSpec((FS, 1, 768, PIECE), lambda i, *_: (0, 1, 0, 0)), whole((LEN, HID))],
        out_specs=[whole((LEN, ATT)), whole((LEN, HID)), whole((1, HID))],
        out_shape=[
            jax.ShapeDtypeStruct((LEN, ATT), BF),
            jax.ShapeDtypeStruct((LEN, HID), BF),
            jax.ShapeDtypeStruct((1, HID), F32),
        ],
        scratch_shapes=[pltpu.VMEM((2, ROWS, D), BF), pltpu.SemaphoreType.DMA((2, 2))],
        cost_estimate=LARGE,
        compiler_params=params(),
        name="emit_back",
    )(place, *g_a, *g_b, w, slope)


ALLW = QKV + ATT + 2 * HID
EXTRA = 16


def weight_grads_body(place_ref, att_ref, act_ref, gh_ref, gqkv_ref, normed_ref, *refs):
    g_refs, out_ref, turned = refs[:10], refs[10], refs[11]

    @pl.when(pl.program_id(0) == 0)
    def _():
        for block in range(8):
            rows = slice(block * PIECE, (block + 1) * PIECE)
            at = 0
            for ref, n in ((att_ref, ATT), (act_ref, HID)):
                turned[at : at + n, rows] = gather_pieces(place_ref, ref, jnp.int32(block)).T
                at += n
            for ref, n in ((gh_ref, HID), (gqkv_ref, QKV)):
                turned[at : at + n, rows] = ref[rows, :].T
                at += n

    cut = ATT + HID
    g = jnp.concatenate([ref[...] for ref in g_refs], axis=0)
    out_ref[0, :cut] = jnp.dot(turned[:cut], g, preferred_element_type=F32).astype(BF)
    out_ref[0, cut:ALLW] = jnp.dot(turned[cut:], normed_ref[...], preferred_element_type=F32).astype(BF)
    out_ref[0, ALLW:] = jnp.zeros((EXTRA, PIECE), BF)


def weight_grads(place, att, act, gh, gqkv, g_a, g_b, normed):
    return pl.pallas_call(
        weight_grads_body,
        grid=(FS,),
        in_specs=[
            SM, whole((LEN, ATT)), whole((LEN, HID)), whole((LEN, HID)), whole((LEN, QKV)),
            pl.BlockSpec((LEN, PIECE), lambda i: (0, i)),
        ]
        + [pl.BlockSpec((v.shape[0], PIECE), lambda i: (0, i)) for v in (*g_a, *g_b)],
        out_specs=pl.BlockSpec((1, ALLW + EXTRA, PIECE), lambda i: (i, 0, 0)),
        scratch_shapes=[pltpu.VMEM((ALLW, LEN), BF)],
        out_shape=jax.ShapeDtypeStruct((FS, ALLW + EXTRA, PIECE), BF),
        cost_estimate=LARGE,
        compiler_params=params(),
        name="weight_grads",
    )(place, att, act, gh, gqkv, normed, *g_a, *g_b)


def input_back_body(pairs, place_ref, gqkv_ref, gh_ref, w_ref, wl_ref, normed_ref, *refs):
    step = pl.program_id(0)
    sums_ref, last_ref, out_scr = refs[-3:]
    far = len(pairs) == 1
    got_refs, out_refs = ((), refs[:-3]) if far else (refs[:4], refs[4:-3])
    blocks = []
    for side in range(2):
        block = jnp.int32(pairs[0][side])
        for k in range(1, len(pairs)):
            block = jnp.where(step == k, pairs[k][side], block)
        blocks.append(block)

    def pieces(ref):
        return jnp.concatenate([gather_pieces(place_ref, ref, block) for block in blocks], axis=0)

    both = jnp.concatenate([pieces(gqkv_ref), pieces(gh_ref)], axis=1)
    normed = pieces(normed_ref)

    @pl.when(step == 0)
    def _():
        sums_ref[...] = jnp.zeros_like(sums_ref)
        unpack_last(wl_ref, last_ref)

    turned = (((1,), (1,)), ((), ()))
    for f in range(FS):
        cols = slice(f * PIECE, (f + 1) * PIECE)
        part = lax.dot_general(both[:, 768:], last_ref[cols, :], turned, preferred_element_type=F32)
        for j in range(3):
            part += lax.dot_general(
                both[:, j * 256 : (j + 1) * 256], w_ref[f, 0, j * 256 : (j + 1) * 256], turned,
                preferred_element_type=F32,
            )
        out_scr[:, cols] = part
        sums_ref[0:1, cols] += jnp.sum(part, axis=0, keepdims=True)
        sums_ref[1:2, cols] += jnp.sum(part * normed[:, cols].astype(F32), axis=0, keepdims=True)
    if far:
        for k in range(4):
            out_refs[k][...] = out_scr[k * 128 : (k + 1) * 128, :].astype(BF)
        return
    for k in range(3):

        @pl.when(step == k)
        def _():
            for side in range(2):
                for part in range(2):
                    at = side * PIECE + part * 128
                    v = out_scr[at : at + 128, :]
                    if k == part:
                        v += got_refs[2 * side + part][...].astype(F32)
                    out_refs[2 * k + side][part * 128 : (part + 1) * 128, :] = v.astype(BF)


def input_back(pairs, place, gqkv, gh, w, normed, got=()):
    n = len(pairs)
    outs = [(128, D)] * 4 if n == 1 else [(PIECE, D)] * 6
    return pl.pallas_call(
        functools.partial(input_back_body, pairs),
        grid_spec=pltpu.PrefetchScalarGridSpec(
            num_scalar_prefetch=1,
            grid=(n,),
            in_specs=[
                whole((LEN, QKV)), whole((LEN, HID)), W_FIRST, W_LAST, whole((LEN, D)),
            ]
            + [whole((128, D))] * len(got),
            out_specs=[whole(shape) for shape in outs] + [whole((2, D))],
            scratch_shapes=[pltpu.VMEM((D, 128), BF), pltpu.VMEM((2 * PIECE, D), F32)],
        ),
        out_shape=[jax.ShapeDtypeStruct(shape, BF) for shape in outs] + [jax.ShapeDtypeStruct((2, D), F32)],
        cost_estimate=LARGE,
        compiler_params=params(),
        name="input_back",
    )(place, gqkv, gh, w, w, normed, *got)


def shift(v, axis, by, n=4):
    return lax.ppermute(v, axis, [(i, (i + by) % n) for i in range(n)])


def ring_gather(own, axis):
    half = own.shape[0] // 2
    left = shift(own, axis, 1)
    right = shift(own, axis, -1)
    return [own, right, shift(left[:half], axis, 1), shift(right[half:], axis, -1), left]


def ring_place(pieces, axis):
    me = lax.axis_index(axis)
    out = jnp.zeros((4,) + pieces[0].shape, pieces[0].dtype)
    own, right, far_a, far_b, left = pieces
    for by, v in ((0, own), (1, right), (2, jnp.concatenate([far_a, far_b], axis=0)), (3, left)):
        out = lax.dynamic_update_index_in_dim(out, v, lax.rem(me + by, 4), 0)
    return out


def tie(v, *others):
    return lax.optimization_barrier((v,) + others)[0]


def plus(a, b):
    return (a.astype(F32) + b.astype(F32)).astype(BF)


def near_sum(own, right, left, axis):
    return own.astype(F32) + shift(right, axis, 1).astype(F32) + shift(left, axis, -1).astype(F32)


def ring_sum_first(parts, axis):
    own, right, far, left = parts
    got = [shift(far, axis, 2), shift(right, axis, 1), shift(left, axis, -1)]
    total = own.astype(F32)
    for v in got:
        total = total + v.astype(F32)
    return total, got[1]


def ring_sum(parts, axis):
    return ring_sum_first(parts, axis)[0]


def quarters(v):
    n = v.shape[0] // 4
    return [v[i * n : (i + 1) * n] for i in range(4)]


def small_gather(v, axes):
    for axis in axes:
        n = 2 if axis == "core" else 4
        me = lax.axis_index(axis)
        out = jnp.zeros((n,) + v.shape, v.dtype)
        out = lax.dynamic_update_index_in_dim(out, v, me, 0)
        for by in range(1, n):
            got = shift(v, axis, by, n)
            out = lax.dynamic_update_index_in_dim(out, got, lax.rem(me + n - by, n), 0)
        v = out
    return v


def small_sum(v, axes):
    for axis, n, dim in axes:
        me = lax.axis_index(axis)
        total = lax.dynamic_index_in_dim(v, me, dim, keepdims=False)
        for by in range(1, n):
            part = lax.dynamic_index_in_dim(v, lax.rem(me + by, n), dim, keepdims=False)
            total = total + shift(part, axis, by, n)
        v = total
    return v


def on_device(
    tokens, cotangent, doc_starts, ln_gain, ln_bias, w_qkv, b_qkv, w_out, b_out, w_fc1, b_fc1, w_fc2, b_fc2,
):
    own = tokens[0]
    own_grad = cotangent[0]
    z_me, x_me = lax.axis_index("z"), lax.axis_index("x")
    seq = z_me * 4 + x_me
    place = jnp.stack([z_me, x_me]).astype(jnp.int32)

    fsdp = ("y", "core")
    x = lax.all_gather(own, ("z", "x"), axis=0, tiled=True)
    w, vectors, own_a, own_b = pack(
        w_qkv, w_fc1, w_out, w_fc2, ln_gain, ln_bias, b_qkv, b_out, b_fc1, b_fc2, own_grad
    )
    vectors = small_gather(vectors, ("x", "z"))
    w = ring_place(ring_gather(w, "y"), "y")
    vectors = small_gather(vectors, ("y",))
    w, vectors, own_a, own_b = lax.optimization_barrier((w, vectors, own_a, own_b))
    w = small_gather(w, ("core",)).swapaxes(0, 1).reshape(FS, 2, 768, PIECE)
    vectors = small_gather(vectors, ("core",))
    *tables, start = angles(doc_starts)
    first = start[0, ::AQ] // AK
    a = jnp.concatenate(ring_gather(own_a, "x"), axis=0)
    b = jnp.concatenate(ring_gather(own_b, "z"), axis=0)
    a, b, x = lax.optimization_barrier((a, b, x))
    g_a = ring_gather(a, "z")
    g_b = ring_gather(b, "x")
    vectors = vectors.transpose(1, 0, 2, 3, 4, 5).reshape(128, 8, 128)

    sizes = [16, 16, 48, 16, 64, 16]
    gain, bias, bq, bo, b1, b2 = [vectors[:, k, :n].reshape(1, -1) for k, n in enumerate(sizes)]
    b_in = jnp.concatenate(
        [
            lax.dynamic_slice_in_dim(bq, seq * QKV, QKV, 1).reshape(2, 3, 64).transpose(1, 0, 2).reshape(1, QKV),
            lax.dynamic_slice_in_dim(b1, seq * HID, HID, 1),
        ],
        axis=1,
    )

    normed, qkv, act, slope = project(x, gain, bias, w, b_in, tables)
    att, lse = attend(first, qkv, start)
    out_part = emit(att, act, w)
    out_sum = lax.psum_scatter(out_part, ("z", "x"), scatter_dimension=0, tiled=True)
    output = (own.astype(F32) + out_sum.astype(F32) + bo + b2).astype(BF)

    ga, gh, b1_sum = emit_back(place, g_a, g_b, w, tie(slope, out_part))
    gqkv, bq_sum = attend_back(first, qkv, att, ga, lse, start, tables)
    bq_sum = bq_sum.reshape(3, 2, 64).transpose(1, 0, 2).reshape(1, QKV)
    far_a0, far_a1, far_b0, far_b1, sums_far = input_back(((2, 6),), place, gqkv, gh, w, normed)
    got = [shift(far_a0, "z", 1), shift(far_a1, "z", -1), shift(far_b0, "x", 1), shift(far_b1, "x", -1)]
    grads = weight_grads(place, att, act, gh, tie(gqkv, far_a0), g_a, g_b, normed)
    right_a, right_b, left_a, left_b, own_a, own_b, sums = input_back(
        ((1, 5), (3, 7), (0, 4)), place, gqkv, gh, w, tie(normed, grads), got
    )
    sums = sums + sums_far
    wide_grad = own_grad.astype(F32)
    bo_sum = jnp.sum(wide_grad, axis=0, keepdims=True)
    gain_sum = (sums[1:2] - bias * sums[0:1]) / gain
    bq_all = lax.dynamic_update_slice_in_dim(jnp.zeros((1, 16 * QKV), F32), bq_sum, seq * QKV, 1)
    b1_all = lax.dynamic_update_slice_in_dim(jnp.zeros((1, 16 * HID), F32), b1_sum, seq * HID, 1)
    packed = jnp.concatenate(
        [t.reshape(128, -1) for t in (gain_sum, sums[0:1], bq_all, bo_sum, b1_all)], axis=1
    )
    packed = packed.reshape(FS, 10, PIECE).astype(BF)
    grads = lax.dynamic_update_slice(grads, packed, (0, ALLW, 0))
    grads = lax.psum_scatter(tie(grads, out_sum, right_a), fsdp, scatter_dimension=0, tiled=True)[0].astype(F32)
    small = small_sum(grads[ALLW : ALLW + 10].reshape(4, 4, 160), (("z", 4, 0), ("x", 4, 0)))
    cut = ATT + HID
    grads_qkv, grads_fc1 = grads[cut + HID : ALLW], grads[cut : cut + HID]
    grads_qkv = grads_qkv.reshape(3, 2, 64, PIECE).transpose(1, 0, 2, 3).reshape(QKV, PIECE)

    a = near_sum(own_a, right_a, left_a, "z").astype(BF)
    b = near_sum(own_b, right_b, left_b, "x").astype(BF)
    a = ring_sum(quarters(a), "x")
    b = ring_sum(quarters(b), "z")
    dn = jnp.concatenate([a, b], axis=0)
    wide = own.astype(F32)
    centered = wide - jnp.mean(wide, axis=1, keepdims=True)
    inv = lax.rsqrt(jnp.mean(centered * centered, axis=1, keepdims=True) + EPS)
    unit = centered * inv
    e = dn * gain
    input_grad = wide_grad + inv * (
        e - jnp.mean(e, axis=1, keepdims=True) - unit * jnp.mean(e * unit, axis=1, keepdims=True)
    )

    return (
        output[None],
        input_grad[None],
        small[0:16],
        small[16:32],
        grads_qkv.T,
        small[32:80],
        grads[:ATT],
        small[80:96],
        grads_fc1.T,
        small[96:160],
        grads[ATT:cut],
        small[80:96],
    )


def solution(mesh):
    split = Mesh(mesh.devices.reshape(4, 2, 4, 4), ("y", "core", "z", "x"))
    f, s = ("y", "core"), ("z", "x")
    both = f + s
    in_specs = (
        P(f, s, None), P(f, s, None), P(f, None), P(both), P(both), P(f, s), P(both), P(s, f), P(both),
        P(f, s), P(both), P(s, f), P(both),
    )
    out_specs = (
        P(f, s, None), P(f, s, None), P(both), P(both), P(f, s), P(both), P(s, f), P(both), P(f, s),
        P(both), P(s, f), P(both),
    )
    return jax.shard_map(on_device, mesh=split, in_specs=in_specs, out_specs=out_specs, check_vma=False)
```

```python
import functools
import math

import jax
import jax.numpy as jnp
import numpy as np
from jax import lax
from jax.experimental import pallas as pl
from jax.experimental.pallas import tpu as pltpu
from jax.sharding import Mesh
from jax.sharding import PartitionSpec as P

BF = jnp.bfloat16
F32 = jnp.float32
EPS = 1e-05
D = 2048
LEN = 2048
ROWS = 512
TOK = 128
HALF = 64
WIDE = D // 2
QKV = 384
HID = 512
ATT = 128
PIECE = 256
FS = 8
NEG = -1e30


SMALL = pl.CostEstimate(flops=1, bytes_accessed=1, transcendentals=0)
LARGE = pl.CostEstimate(flops=100 * 2**30, bytes_accessed=320 * 2**20, transcendentals=0)


def params(mib):
    return pltpu.CompilerParams(vmem_limit_bytes=mib * 2**20, dimension_semantics=("arbitrary",))


VM = pl.BlockSpec(memory_space=pltpu.VMEM)
SM = pl.BlockSpec(memory_space=pltpu.SMEM)
ANY = pl.BlockSpec(memory_space=pl.ANY)
HBM = pl.BlockSpec(memory_space=pltpu.HBM)


def whole(shape):
    return pl.BlockSpec(shape, lambda i, *_: (0,) * len(shape))


def rows_of(width):
    return pl.BlockSpec((ROWS, width), lambda i, *_: (i, 0))


def piece_start(place_ref, block, piece):
    first = block < 4
    z_off = jnp.where(first, block, piece)
    x_off = jnp.where(first, piece, block - 4)
    seq = lax.rem(place_ref[0] + z_off, 4) * 4 + lax.rem(place_ref[1] + x_off, 4)
    return pl.multiple_of(seq * TOK + jnp.where(first, 0, HALF), HALF)


def gather_pieces(place_ref, ref, block):
    return jnp.concatenate(
        [ref[pl.ds(piece_start(place_ref, block, s), HALF), :] for s in range(4)], axis=0
    )


def turn(v, table, sign=1.0):
    lane = lax.broadcasted_iota(jnp.int32, v.shape, 1)
    other = pltpu.roll(table, 64, 1)
    cos = jnp.where(lane < 64, table, other)
    sin = jnp.where(lane < 64, other, table)
    swapped = jnp.where(lax.rem(lane, 64) < 16, pltpu.roll(v, 112, 1), pltpu.roll(v, 16, 1))
    return v * cos + swapped * (sign * sin)


def pack_body(*refs):
    ins, (w_ref, vec_ref, a_ref, b_ref), scr, sem = refs[:11], refs[11:15], refs[15:25], refs[25]
    copies = [pltpu.make_async_copy(ins[k], scr[k], sem.at[k]) for k in range(10)]
    copies += [
        pltpu.make_async_copy(ins[10].at[:, k * WIDE : (k + 1) * WIDE], ref, sem.at[10 + k])
        for k, ref in enumerate((a_ref, b_ref))
    ]
    for copy in copies:
        copy.start()
    for copy in copies[:10]:
        copy.wait()
    wq_ref, w1_ref, wo_ref, w2_ref = scr[:4]
    low = lax.broadcasted_iota(jnp.int32, (PIECE, 128), 1) < 64
    g0, g1, g2 = [wq_ref[:, k * 128 : (k + 1) * 128].astype(F32) for k in range(3)]
    w_ref[0, 0:256, :128] = jnp.where(low, g0, g1).astype(BF)
    w_ref[0, 0:256, 128:] = pltpu.roll(jnp.where(low, g2, g0), 64, 1).astype(BF)
    w_ref[0, 256:512, :128] = jnp.where(low, g1, g2).astype(BF)
    w_ref[0, 256:512, 128:] = w1_ref[:, :128]
    w_ref[0, 512:768] = w1_ref[:, 128:384]
    w_ref[1, 0:128, :128] = w1_ref[:128, 384:]
    w_ref[1, 0:128, 128:] = w1_ref[128:, 384:]
    w_ref[1, 128:256] = wo_ref[...]
    w_ref[1, 256:768] = w2_ref[...]
    for k, ref in enumerate(scr[4:]):
        vec_ref[k : k + 1, : ref.shape[1]] = ref[...].astype(F32)
    for copy in copies[10:]:
        copy.wait()


def pack(*arrays):
    flat = [a if a.ndim == 2 else a[None, :] for a in arrays]
    return pl.pallas_call(
        pack_body,
        in_specs=[ANY] * 11,
        out_specs=[VM, VM, VM, VM],
        out_shape=[
            jax.ShapeDtypeStruct((2, 768, PIECE), BF),
            jax.ShapeDtypeStruct((8, 128), F32),
            jax.ShapeDtypeStruct((TOK, WIDE), BF),
            jax.ShapeDtypeStruct((TOK, WIDE), BF),
        ],
        scratch_shapes=[pltpu.VMEM(a.shape, BF) for a in flat[:10]] + [pltpu.SemaphoreType.DMA((12,))],
        cost_estimate=SMALL,
        compiler_params=pltpu.CompilerParams(vmem_limit_bytes=58 * 2**20),
        name="pack",
    )(*flat)


def document_start(starts_ref, token):
    first = jnp.zeros(token.shape, jnp.int32)
    for n in range(starts_ref.shape[1]):
        begin = starts_ref[0, n]
        first = jnp.where(token >= begin, begin, first)
    return first


def angles_body(starts_ref, table_ref, start_ref):
    block = pl.program_id(0)
    shape = (ROWS, 128)
    token = block * ROWS + lax.broadcasted_iota(jnp.int32, shape, 0)
    wide = lax.broadcasted_iota(jnp.int32, shape, 1)
    lane = lax.rem(wide, 64)
    freq = jnp.exp(lax.rem(lane, 16).astype(F32) * (-2.0 * math.log(10000.0) / 32))
    phase = (token - document_start(starts_ref, token)).astype(F32) * freq
    sin = jnp.sin(phase)
    cos = jnp.where(lane < 32, jnp.cos(phase), 1.0)
    sin = jnp.where(lane < 16, -sin, jnp.where(lane < 32, sin, 0.0))
    table_ref[...] = jnp.where(wide < 64, cos, sin)
    here = block * ROWS + lax.broadcasted_iota(jnp.int32, (1, ROWS), 1)
    start_ref[...] = document_start(starts_ref, here)


def angles(starts):
    return pl.pallas_call(
        angles_body,
        grid=(LEN // ROWS,),
        in_specs=[SM],
        out_specs=[rows_of(128), pl.BlockSpec((1, ROWS), lambda i: (0, i))],
        out_shape=[jax.ShapeDtypeStruct((LEN, 128), F32), jax.ShapeDtypeStruct((1, LEN), jnp.int32)],
        cost_estimate=SMALL,
        compiler_params=params(58),
        name="angles",
    )(starts)


def unpack_last(w_ref, last_ref):
    for f in range(FS):
        for k in range(2):
            at = f * PIECE + k * 128
            last_ref[at : at + 128, :] = w_ref[f, 0, :, k * 128 : (k + 1) * 128]


W_FIRST = pl.BlockSpec((FS, 1, 768, PIECE), lambda *_: (0, 0, 0, 0))
W_LAST = pl.BlockSpec((FS, 1, 128, PIECE), lambda *_: (0, 1, 0, 0))
WIDTHS = (D, QKV, HID, HID)


ORDER = (0, 1, 3, 2)


ORDER = (0, 1, 3, 2)


def turn_of(i):
    return jnp.where(i == 3, 2, jnp.where(i == 2, 3, i))


def project_body(
    place_ref, a0_ref, a1_ref, a2_ref, a3_ref, a4_ref, b0_ref, b1_ref, b2_ref, b3_ref, b4_ref,
    gain_ref, bias_ref, w_ref, wl_ref, b_ref, table_ref,
    normed_ref, qkv_ref, act_ref, slope_ref, last_ref, x_scr,
):
    a_refs = ((a0_ref,), (a1_ref,), (a2_ref, a3_ref), (a4_ref,))

    def lay(k):
        z_at = lax.rem(place_ref[0] + ORDER[k], 4)
        at = 0
        for ref in a_refs[ORDER[k]]:
            n = ref.shape[0]
            x_scr[at : at + n, :, :WIDE] = ref[...]
            at += n
        for x_off, ref in ((0, b0_ref), (1, b1_ref), (3, b4_ref)):
            x_scr[lax.rem(place_ref[1] + x_off, 4), :, WIDE:] = ref[z_at]
        far = lax.rem(place_ref[1] + 2, 4)

        @pl.when(z_at < 2)
        def _():
            x_scr[far, :, WIDE:] = b2_ref[lax.rem(z_at, 2)]

        @pl.when(z_at >= 2)
        def _():
            x_scr[far, :, WIDE:] = b3_ref[lax.rem(z_at, 2)]

    for k in range(4):

        @pl.when(pl.program_id(0) == k)
        def _():
            lay(k)

    @pl.when(pl.program_id(0) == 0)
    def _():
        unpack_last(wl_ref, last_ref)

    x = x_scr[...].reshape(ROWS, D).astype(F32)
    centered = x - jnp.mean(x, axis=1, keepdims=True)
    inv = lax.rsqrt(jnp.mean(centered * centered, axis=1, keepdims=True) + EPS)
    normed_ref[...] = (centered * inv * gain_ref[...] + bias_ref[...]).astype(BF)

    def group(j):
        normed = normed_ref[...]
        if j == 3:
            return jnp.dot(normed, last_ref[...], preferred_element_type=F32) + b_ref[:, 768:]
        w = w_ref[:, 0, j * 256 : (j + 1) * 256].reshape(D, PIECE)
        return jnp.dot(normed, w, preferred_element_type=F32) + b_ref[:, j * 256 : (j + 1) * 256]

    table = table_ref[...]

    def hidden(h, cols):
        k0 = math.sqrt(2.0 / math.pi)
        h2 = h * h
        t = jnp.tanh(h * (k0 + (k0 * 0.044715) * h2))
        act_ref[:, cols] = (0.5 * h * (1.0 + t)).astype(BF)
        slope = 0.5 * (1.0 + t) + 0.5 * h * (1.0 - t * t) * (k0 + (3 * 0.044715 * k0) * h2)
        slope_ref[:, cols] = slope.astype(BF)

    qk = group(0).astype(BF).astype(F32)
    qkv_ref[:, 0:128] = (turn(qk[:, :128], table) * 0.125).astype(BF)
    qkv_ref[:, 128:256] = turn(qk[:, 128:], table).astype(BF)
    vh = group(1)
    qkv_ref[:, 256:384] = vh[:, :128].astype(BF)
    hidden(vh[:, 128:], slice(0, 128))
    hidden(group(2), slice(128, 384))
    hidden(group(3), slice(384, 512))


def turned_rows(width):
    return pl.BlockSpec((ROWS, width), lambda i, place: (lax.rem(place[0] + turn_of(i), 4), 0))


def project(place, x_a, x_b, gain, bias, w, b, table):
    return pl.pallas_call(
        project_body,
        grid_spec=pltpu.PrefetchScalarGridSpec(
            num_scalar_prefetch=1,
            grid=(4,),
            in_specs=[VM] * 10
            + [whole((1, D)), whole((1, D)), W_FIRST, W_LAST, whole((1, QKV + HID)), turned_rows(128)],
            out_specs=[turned_rows(D), turned_rows(QKV), turned_rows(HID), turned_rows(HID)],
            scratch_shapes=[
                pltpu.VMEM((D, 128), BF),
                pltpu.VMEM((4, TOK, D), BF),
            ],
        ),
        out_shape=[jax.ShapeDtypeStruct((LEN, width), BF) for width in (D, QKV, HID, HID)],
        cost_estimate=LARGE,
        compiler_params=params(34),
        name="project",
    )(place, *x_a, *x_b, gain, bias, w, w, b, table)


AQ = 512
AK = 256
NQ = LEN // AQ


def padded_turned(ref, scr):
    row = lax.broadcasted_iota(jnp.int32, (128, AQ), 0)
    for i in range(NQ):
        cols = slice(i * AQ, (i + 1) * AQ)
        t = ref[cols, :].astype(F32).T
        scr[0, :, cols] = jnp.where(row < 64, t, 0.0).astype(BF)
        scr[1, :, cols] = jnp.where(row < 64, 0.0, t).astype(BF)


def padded(ref, scr):
    lane = lax.broadcasted_iota(jnp.int32, (AQ, 128), 1)
    for i in range(NQ):
        rows = slice(i * AQ, (i + 1) * AQ)
        v = ref[rows, :].astype(F32)
        scr[0, rows, :] = jnp.where(lane < 64, v, 0.0).astype(BF)
        scr[1, rows, :] = jnp.where(lane < 64, 0.0, v).astype(BF)


def fold(op, v):
    return op(v.reshape(AK // 8, 8, AQ), axis=0)


def attend_body(first_ref, qkv_ref, start_ref, att_ref, lse_ref, qt_scr, vt_scr, s_scr):
    padded_turned(qkv_ref.at[:, 0:128], qt_scr)
    for i in range(NQ):
        rows = slice(i * AQ, (i + 1) * AQ)
        vt_scr[:, rows] = qkv_ref[rows, 256:384].astype(F32).T.astype(BF)
    row = lax.broadcasted_iota(jnp.int32, (AK, AQ), 0)
    col = lax.broadcasted_iota(jnp.int32, (AK, AQ), 1)

    def q_block(i, _):
        cols = pl.ds(pl.multiple_of(i * AQ, AQ), AQ)
        start = start_ref[:, cols]
        qt = [qt_scr[h, :, cols] for h in range(2)]

        def scores(j, ok, peaks):
            rows = pl.ds(pl.multiple_of(j * AK, AK), AK)
            k = qkv_ref[rows, 128:256]
            new = []
            for h in range(2):
                s = jnp.dot(k, qt[h], preferred_element_type=F32)
                s = jnp.where(ok, s, NEG)
                s_scr[h, rows, :] = s
                new.append(jnp.maximum(peaks[h], fold(jnp.max, s)))
            return tuple(new)

        low = first_ref[i]
        peaks = (jnp.full((8, AQ), NEG, F32),) * 2
        for d in range(2):
            peaks = scores(2 * i + d, (row + (2 * i + d) * AK >= start) & (row + d * AK <= col), peaks)
        peaks = lax.fori_loop(low, 2 * i, lambda j, p: scores(j, row + j * AK >= start, p), peaks)
        peak = [jnp.max(p, axis=0, keepdims=True) for p in peaks]

        def values(j, state):
            rows = pl.ds(pl.multiple_of(j * AK, AK), AK)
            new = []
            for h in range(2):
                total, o = state[2 * h : 2 * h + 2]
                p = jnp.exp(s_scr[h, rows, :] - peak[h])
                total = total + fold(jnp.sum, p)
                o = o + jnp.dot(
                    vt_scr[64 * h : 64 * h + 64, rows], p.astype(BF), preferred_element_type=F32
                )
                new += [total, o]
            return tuple(new)

        state = (jnp.zeros((8, AQ), F32), jnp.zeros((64, AQ), F32)) * 2
        state = lax.fori_loop(low, 2 * i + 2, values, state)
        total = [jnp.sum(state[2 * h], axis=0, keepdims=True) for h in range(2)]
        both = jnp.concatenate([state[1] / total[0], state[3] / total[1]], axis=0)
        att_ref[cols, :] = both.T.astype(BF)
        for h in range(2):
            lse_ref[h : h + 1, cols] = peak[h] + jnp.log(total[h])
        return 0

    lax.fori_loop(0, NQ, q_block, 0)


def attend(first, qkv, start):
    return pl.pallas_call(
        attend_body,
        in_specs=[SM, VM, VM],
        out_specs=[VM, VM],
        out_shape=[
            jax.ShapeDtypeStruct((LEN, ATT), BF),
            jax.ShapeDtypeStruct((2, LEN), F32),
        ],
        scratch_shapes=[
            pltpu.VMEM((2, 128, LEN), BF),
            pltpu.VMEM((128, LEN), BF),
            pltpu.VMEM((2, LEN, AQ), F32),
        ],
        cost_estimate=LARGE,
        compiler_params=pltpu.CompilerParams(vmem_limit_bytes=24 * 2**20),
        name="attend",
    )(first, qkv, start)


def attend_back_body(
    first_ref, qkv_ref, att_ref, ga_ref, lse_ref, start_ref, table_ref,
    gqkv_ref, bsum_ref,
    q_scr, go_scr, qt_scr, got_scr, kt_scr, dl_scr, dk_scr, dv_scr,
):
    padded(qkv_ref.at[:, 0:128], q_scr)
    padded(ga_ref, go_scr)
    padded_turned(qkv_ref.at[:, 0:128], qt_scr)
    for i in range(NQ):
        rows = slice(i * AQ, (i + 1) * AQ)
        kt_scr[:, rows] = qkv_ref[rows, 128:256].astype(F32).T.astype(BF)
        got = ga_ref[rows, :].astype(F32).T
        prod = got * att_ref[rows, :].astype(F32).T
        row = lax.broadcasted_iota(jnp.int32, (128, AQ), 0)
        got_scr[0, :, rows] = jnp.where(row < 64, got, 0.0).astype(BF)
        got_scr[1, :, rows] = jnp.where(row < 64, 0.0, got).astype(BF)
        for h in range(2):
            dl_scr[h : h + 1, rows] = jnp.sum(prod[64 * h : 64 * h + 64], axis=0, keepdims=True)
    dk_scr[...] = jnp.zeros_like(dk_scr)
    dv_scr[...] = jnp.zeros_like(dv_scr)
    row = lax.broadcasted_iota(jnp.int32, (AK, AQ), 0)
    col = lax.broadcasted_iota(jnp.int32, (AK, AQ), 1)

    def q_block(i, bsum):
        cols = pl.ds(pl.multiple_of(i * AQ, AQ), AQ)
        start = start_ref[:, cols]
        lse = [lse_ref[h : h + 1, cols] for h in range(2)]
        dl = [dl_scr[h : h + 1, cols] for h in range(2)]

        def pair(j, ok, dq):
            rows = pl.ds(pl.multiple_of(j * AK, AK), AK)
            k = qkv_ref[rows, 128:256]
            v = qkv_ref[rows, 256:384]
            dv = dk = 0.0
            new = []
            for h in range(2):
                s = jnp.dot(k, qt_scr[h, :, cols], preferred_element_type=F32)
                dp = jnp.dot(v, got_scr[h, :, cols], preferred_element_type=F32)
                p = jnp.where(ok, jnp.exp(s - lse[h]), 0.0)
                ds = (p * (dp - dl[h])).astype(BF)
                dv += jnp.dot(p.astype(BF), go_scr[h, cols, :], preferred_element_type=F32)
                dk += jnp.dot(ds, q_scr[h, cols, :], preferred_element_type=F32)
                new.append(
                    dq[h]
                    + jnp.dot(kt_scr[64 * h : 64 * h + 64, rows], ds, preferred_element_type=F32)
                )
            dv_scr[rows, :] += dv
            dk_scr[rows, :] += dk
            return tuple(new)

        dq = (jnp.zeros((64, AQ), F32),) * 2
        for d in range(2):
            dq = pair(2 * i + d, (row + (2 * i + d) * AK >= start) & (row + d * AK <= col), dq)
        dq = lax.fori_loop(first_ref[i], 2 * i, lambda j, dq: pair(j, row + j * AK >= start, dq), dq)
        dq = (jnp.concatenate(dq, axis=0) * 0.125).T
        out = turn(dq, table_ref[cols, :], -1.0).astype(BF)
        gqkv_ref[cols, 0:128] = out
        return bsum + jnp.sum(out.astype(F32), axis=0, keepdims=True)

    bsum_ref[:, 0:128] = lax.fori_loop(0, NQ, q_block, jnp.zeros((1, 128), F32))

    def finish(i, total):
        rows = pl.ds(pl.multiple_of(i * AQ, AQ), AQ)
        dk = turn(dk_scr[rows, :], table_ref[rows, :], -1.0)
        out = jnp.concatenate([dk, dv_scr[rows, :]], axis=1).astype(BF)
        gqkv_ref[rows, 128:384] = out
        return total + jnp.sum(out.astype(F32), axis=0, keepdims=True)

    bsum_ref[:, 128:384] = lax.fori_loop(0, NQ, finish, jnp.zeros((1, 256), F32))


def attend_back(first, qkv, att, ga, lse, start, table):
    return pl.pallas_call(
        attend_back_body,
        in_specs=[SM] + [VM] * 6,
        out_specs=[VM, VM],
        out_shape=[
            jax.ShapeDtypeStruct((LEN, QKV), BF),
            jax.ShapeDtypeStruct((1, QKV), F32),
        ],
        scratch_shapes=[
            pltpu.VMEM((2, LEN, 128), BF),
            pltpu.VMEM((2, LEN, 128), BF),
            pltpu.VMEM((2, 128, LEN), BF),
            pltpu.VMEM((2, 128, LEN), BF),
            pltpu.VMEM((128, LEN), BF),
            pltpu.VMEM((2, LEN), F32),
            pltpu.VMEM((LEN, 128), F32),
            pltpu.VMEM((LEN, 128), F32),
        ],
        cost_estimate=LARGE,
        compiler_params=pltpu.CompilerParams(vmem_limit_bytes=24 * 2**20),
        name="attend_back",
    )(first, qkv, att, ga, lse, start, table)


def emit_body(att_ref, act_ref, w_ref, out_ref):
    both = jnp.concatenate([att_ref[...], act_ref[...]], axis=1)
    for f in range(FS):
        out_ref[:, f * PIECE : (f + 1) * PIECE] = jnp.dot(
            both, w_ref[f, 0, 128:], preferred_element_type=F32
        ).astype(BF)


def emit(att, act, w):
    return pl.pallas_call(
        emit_body,
        grid=(LEN // ROWS,),
        in_specs=[rows_of(ATT), rows_of(HID), pl.BlockSpec((FS, 1, 768, PIECE), lambda i, *_: (0, 1, 0, 0))],
        out_specs=rows_of(D),
        out_shape=pltpu.HBM((LEN, D), BF),
        cost_estimate=LARGE,
        compiler_params=params(24),
        name="emit",
    )(att, act, in_hbm(w))


def emit_back_body(g_ref, w_ref, slope_ref, ga_ref, gh_ref, bsum_ref):
    total = jnp.zeros((ROWS, ATT + HID), F32)
    for f in range(FS):
        total += lax.dot_general(
            g_ref[:, f * PIECE : (f + 1) * PIECE], w_ref[f, 0, 128:], (((1,), (1,)), ((), ())),
            preferred_element_type=F32,
        )
    ga_ref[...] = total[:, :ATT].astype(BF)
    gh = (total[:, ATT:] * slope_ref[...].astype(F32)).astype(BF)
    gh_ref[...] = gh

    @pl.when(pl.program_id(0) == 0)
    def _():
        bsum_ref[...] = jnp.zeros_like(bsum_ref)

    bsum_ref[...] += jnp.sum(gh.astype(F32), axis=0, keepdims=True)


def emit_back(g, w, slope):
    return pl.pallas_call(
        emit_back_body,
        grid=(LEN // ROWS,),
        in_specs=[rows_of(D), pl.BlockSpec((FS, 1, 768, PIECE), lambda i: (0, 1, 0, 0)), rows_of(HID)],
        out_specs=[rows_of(ATT), rows_of(HID), whole((1, HID))],
        out_shape=[
            jax.ShapeDtypeStruct((LEN, ATT), BF),
            jax.ShapeDtypeStruct((LEN, HID), BF),
            jax.ShapeDtypeStruct((1, HID), F32),
        ],
        cost_estimate=LARGE,
        compiler_params=params(26),
        name="emit_back",
    )(in_hbm(g), in_hbm(w), slope)


ALLW = QKV + ATT + 2 * HID
EXTRA = 16


def weight_grads_body(att_ref, act_ref, gh_ref, gqkv_ref, g_ref, normed_ref, out_ref, turned):
    @pl.when(pl.program_id(0) == 0)
    def _():
        for block in range(8):
            rows = slice(block * PIECE, (block + 1) * PIECE)
            at = 0
            for ref, n in ((att_ref, ATT), (act_ref, HID), (gh_ref, HID), (gqkv_ref, QKV)):
                turned[at : at + n, rows] = ref[rows, :].T
                at += n

    cut = ATT + HID
    out_ref[0, :cut] = jnp.dot(turned[:cut], g_ref[...], preferred_element_type=F32).astype(BF)
    out_ref[0, cut:ALLW] = jnp.dot(turned[cut:], normed_ref[...], preferred_element_type=F32).astype(BF)
    out_ref[0, ALLW:] = jnp.zeros((EXTRA, PIECE), BF)


def column_piece():
    return pl.BlockSpec((LEN, PIECE), lambda i: (0, i))


def weight_grads(att, act, gh, gqkv, g, normed):
    return pl.pallas_call(
        weight_grads_body,
        grid=(FS,),
        in_specs=[
            whole((LEN, ATT)), whole((LEN, HID)), whole((LEN, HID)), whole((LEN, QKV)),
            column_piece(), column_piece(),
        ],
        out_specs=pl.BlockSpec((1, ALLW + EXTRA, PIECE), lambda i: (i, 0, 0)),
        scratch_shapes=[pltpu.VMEM((ALLW, LEN), BF)],
        out_shape=pltpu.HBM((FS, ALLW + EXTRA, PIECE), BF),
        cost_estimate=LARGE,
        compiler_params=params(34),
        name="weight_grads",
    )(att, act, gh, gqkv, in_hbm(g), in_hbm(normed))


def unpack_body(sums_ref, qkv_ref, out_ref, fc1_ref, fc2_ref, small_ref):
    out_ref[...] = sums_ref[0, :ATT].astype(F32)
    fc2_ref[...] = sums_ref[0, ATT : ATT + HID].astype(F32)
    fc1_ref[...] = sums_ref[0, ATT + HID : ATT + 2 * HID].astype(F32).T
    at = ATT + 2 * HID
    q, k, v = [sums_ref[0, at + n * 128 : at + (n + 1) * 128].astype(F32).T for n in range(3)]
    low = lax.broadcasted_iota(jnp.int32, (PIECE, 128), 1) < 64
    qkv_ref[:, 0:128] = jnp.where(low, q, pltpu.roll(k, 64, 1))
    qkv_ref[:, 128:256] = jnp.where(low, v, q)
    qkv_ref[:, 256:384] = jnp.where(low, pltpu.roll(k, 64, 1), v)
    small_ref[...] = sums_ref[0, ALLW:].astype(F32)


def unpack(sums):
    shapes = [(PIECE, QKV), (ATT, PIECE), (PIECE, HID), (HID, PIECE), (EXTRA, PIECE)]
    return pl.pallas_call(
        unpack_body,
        in_specs=[VM],
        out_specs=[VM] * 5,
        out_shape=[jax.ShapeDtypeStruct(shape, F32) for shape in shapes],
        cost_estimate=SMALL,
        compiler_params=pltpu.CompilerParams(vmem_limit_bytes=16 * 2**20),
        name="unpack",
    )(sums)


def block_of(pairs, step, side):
    block = jnp.int32(pairs[0][side])
    for k in range(1, len(pairs)):
        block = jnp.where(step == k, pairs[k][side], block)
    return block


def input_back_body(pairs, place_ref, gqkv_ref, gh_ref, w_ref, wl_ref, *refs):
    step = pl.program_id(0)
    normed_refs, refs = refs[:8], refs[8:]
    sums_ref, last_ref, out_scr = refs[-3:]
    far = len(pairs) == 1
    got_refs, out_refs = ((), refs[:-3]) if far else (refs[:4], refs[4:-3])
    blocks = [block_of(pairs, step, side) for side in range(2)]

    def pieces(ref):
        return jnp.concatenate([gather_pieces(place_ref, ref, block) for block in blocks], axis=0)

    both = jnp.concatenate([pieces(gqkv_ref), pieces(gh_ref)], axis=1)

    @pl.when(step == 0)
    def _():
        sums_ref[...] = jnp.zeros_like(sums_ref)
        unpack_last(wl_ref, last_ref)

    turned = (((1,), (1,)), ((), ()))
    for f in range(FS):
        cols = slice(f * PIECE, (f + 1) * PIECE)
        part = lax.dot_general(both[:, 768:], last_ref[cols, :], turned, preferred_element_type=F32)
        for j in range(3):
            part += lax.dot_general(
                both[:, j * 256 : (j + 1) * 256], w_ref[f, 0, j * 256 : (j + 1) * 256], turned,
                preferred_element_type=F32,
            )
        out_scr[:, cols] = part
        normed = jnp.concatenate([ref[0, 0, :, cols] for ref in normed_refs], axis=0).astype(F32)
        sums_ref[0:1, cols] += jnp.sum(part, axis=0, keepdims=True)
        sums_ref[1:2, cols] += jnp.sum(part * normed, axis=0, keepdims=True)
    if far:
        for k in range(4):
            out_refs[k][...] = out_scr[k * 128 : (k + 1) * 128, :].astype(BF)
        return
    for k in range(3):

        @pl.when(step == k)
        def _():
            for side in range(2):
                for part in range(2):
                    at = side * PIECE + part * 128
                    v = out_scr[at : at + 128, :]
                    if k == part:
                        v += got_refs[2 * side + part][...].astype(F32)
                    out_refs[2 * k + side][part * 128 : (part + 1) * 128, :] = v.astype(BF)


def piece_spec(pairs, m):
    def where_to(i, place_ref):
        start = piece_start(place_ref, block_of(pairs, i, m // 4), m % 4)
        return (start // TOK, m // 4, 0, 0)

    return pl.BlockSpec((1, 1, HALF, D), where_to)


def input_back(pairs, place, gqkv, gh, w, normed, got=()):
    n = len(pairs)
    outs = [(128, D)] * 4 if n == 1 else [(PIECE, D)] * 6
    return pl.pallas_call(
        functools.partial(input_back_body, pairs),
        grid_spec=pltpu.PrefetchScalarGridSpec(
            num_scalar_prefetch=1,
            grid=(n,),
            in_specs=[whole((LEN, QKV)), whole((LEN, HID)), W_FIRST, W_LAST]
            + [piece_spec(pairs, m) for m in range(8)]
            + [whole((128, D))] * len(got),
            out_specs=[whole(shape) for shape in outs] + [whole((2, D))],
            scratch_shapes=[pltpu.VMEM((D, 128), BF), pltpu.VMEM((2 * PIECE, D), F32)],
        ),
        out_shape=[pltpu.HBM(shape, BF) for shape in outs] + [jax.ShapeDtypeStruct((2, D), F32)],
        cost_estimate=LARGE,
        compiler_params=params(44),
        name="input_back",
    )(place, gqkv, gh, in_hbm(w), in_hbm(w), *[in_hbm(normed.reshape(16, 2, HALF, D))] * 8, *got)


def copy_body(moves, n_in, place_ref, *refs):
    ins, outs, sem = refs[:n_in], refs[n_in:-1], refs[-1]
    copies = [
        pltpu.make_async_copy(src(ins), dst(outs, place_ref), sem.at[k]) for k, (src, dst) in enumerate(moves)
    ]
    for copy in copies:
        copy.start()
    for copy in copies:
        copy.wait()


def copy_kernel(name, moves, place, ins, out_shapes):
    return pl.pallas_call(
        functools.partial(copy_body, moves, len(ins)),
        in_specs=[SM] + [ANY] * len(ins),
        out_specs=[VM] * len(out_shapes),
        out_shape=[jax.ShapeDtypeStruct(shape, BF) for shape in out_shapes],
        scratch_shapes=[pltpu.SemaphoreType.DMA((len(moves),))],
        cost_estimate=SMALL,
        compiler_params=pltpu.CompilerParams(vmem_limit_bytes=58 * 2**20),
        name=name,
    )(place, *ins)


def join(place, pieces_a, pieces_b):
    def move(k):
        axis = 1 - k // 4
        return (
            lambda ins: ins[k],
            lambda outs, place_ref: outs[k // 4].at[lax.rem(place_ref[axis] + k % 4, 4)],
        )

    return copy_kernel(
        "join", [move(k) for k in range(8)], place, [*pieces_a, *pieces_b], [(4, TOK, WIDE)] * 2
    )


def halves(place, left_a, right_a, left_b, right_b):
    def move(k):
        spot = slice(k % 2 * 2, k % 2 * 2 + 2)
        return (lambda ins: ins[k].at[spot], lambda outs, place_ref: outs[k])

    return copy_kernel(
        "halves", [move(k) for k in range(4)], place, [left_a, right_a, left_b, right_b], [(2, TOK, WIDE)] * 4
    )


def shift(v, axis, by, n=4):
    return lax.ppermute(v, axis, [(i, (i + by) % n) for i in range(n)])


def in_hbm(v):
    return pltpu.with_memory_space_constraint(v, pltpu.HBM)


def tie(v, *others):
    return lax.optimization_barrier((v,) + others)[0]


def plus(a, b):
    return (a.astype(F32) + b.astype(F32)).astype(BF)


def near_sum(own, right, left, axis):
    return own.astype(F32) + shift(right, axis, 1).astype(F32) + shift(left, axis, -1).astype(F32)


def ring_sum_first(parts, axis):
    own, right, far, left = parts
    got = [shift(far, axis, 2), shift(right, axis, 1), shift(left, axis, -1)]
    total = own.astype(F32)
    for v in got:
        total = total + v.astype(F32)
    return total, got[1]


def ring_sum(parts, axis):
    return ring_sum_first(parts, axis)[0]


def quarters(v):
    n = v.shape[0] // 4
    return [v[i * n : (i + 1) * n] for i in range(4)]


def small_gather(v, axes):
    for axis in axes:
        n = 2 if axis == "core" else 4
        me = lax.axis_index(axis)
        out = jnp.zeros((n,) + v.shape, v.dtype)
        out = lax.dynamic_update_index_in_dim(out, v, me, 0)
        for by in range(1, n):
            got = shift(v, axis, by, n)
            out = lax.dynamic_update_index_in_dim(out, got, lax.rem(me + n - by, n), 0)
        v = out
    return v


def small_sum(v, axes):
    for axis, n, dim in axes:
        me = lax.axis_index(axis)
        total = lax.dynamic_index_in_dim(v, me, dim, keepdims=False)
        for by in range(1, n):
            part = lax.dynamic_index_in_dim(v, lax.rem(me + by, n), dim, keepdims=False)
            total = total + shift(part, axis, by, n)
        v = total
    return v


def on_device(
    tokens, cotangent, doc_starts, ln_gain, ln_bias, w_qkv, b_qkv, w_out, b_out, w_fc1, b_fc1, w_fc2, b_fc2,
):
    own = tokens[0]
    own_grad = cotangent[0]
    z_me, x_me = lax.axis_index("z"), lax.axis_index("x")
    seq = z_me * 4 + x_me
    place = jnp.stack([z_me, x_me, lax.axis_index("core"), lax.axis_index("y")]).astype(jnp.int32)

    fsdp = ("y", "core")
    w, vectors, own_a, own_b = pack(
        w_qkv, w_fc1, w_out, w_fc2, ln_gain, ln_bias, b_qkv, b_out, b_fc1, b_fc2, own
    )
    w = lax.all_gather(w, fsdp, axis=0).reshape(FS, 2, 768, PIECE)
    vectors = small_gather(vectors, ("x", "z"))
    vectors, own_a, own_b = lax.optimization_barrier((vectors, own_a, own_b))
    a, b = join(
        place,
        [own_a] + [shift(own_a, "x", -by) for by in (1, 2, 3)],
        [own_b] + [shift(own_b, "z", -by) for by in (1, 2, 3)],
    )
    g = lax.all_gather(tie(own_grad, a), ("z", "x"), axis=0, tiled=True)
    left_a, right_a, left_b, right_b = shift(a, "z", 1), shift(a, "z", -1), shift(b, "x", 1), shift(b, "x", -1)
    far = halves(place, left_a, right_a, left_b, right_b)
    x_a = [a, right_a, shift(far[0], "z", 1), shift(far[1], "z", -1), left_a]
    x_b = [b, right_b, shift(far[2], "x", 1), shift(far[3], "x", -1), left_b]
    vectors = small_gather(vectors, ("y", "core"))
    table, start = angles(tie(doc_starts, far[0]))
    first = start[0, ::AQ] // AK
    vectors = vectors.transpose(1, 0, 2, 3, 4, 5).reshape(128, 8, 128)

    sizes = [16, 16, 48, 16, 64, 16]
    gain, bias, bq, bo, b1, b2 = [vectors[:, k, :n].reshape(1, -1) for k, n in enumerate(sizes)]
    b_in = jnp.concatenate(
        [
            lax.dynamic_slice_in_dim(bq, seq * QKV, QKV, 1).reshape(2, 3, 64).transpose(1, 0, 2).reshape(1, QKV),
            lax.dynamic_slice_in_dim(b1, seq * HID, HID, 1),
        ],
        axis=1,
    )

    normed, qkv, act, slope = project(place, x_a, x_b, gain, bias, w, b_in, table)
    att, lse = attend(first, qkv, start)
    out_part = emit(att, act, w)
    out_sum = lax.psum_scatter(out_part, ("z", "x"), scatter_dimension=0, tiled=True)
    output = (own.astype(F32) + out_sum.astype(F32) + bo + b2).astype(BF)

    ga, gh, b1_sum = emit_back(tie(g, out_part), w, slope)
    gqkv, bq_sum = attend_back(first, qkv, att, ga, lse, start, table)
    bq_sum = bq_sum.reshape(3, 2, 64).transpose(1, 0, 2).reshape(1, QKV)
    far_a0, far_a1, far_b0, far_b1, sums_far = input_back(((2, 6),), place, gqkv, gh, w, normed)
    got = [shift(far_a0, "z", 1), shift(far_a1, "z", -1), shift(far_b0, "x", 1), shift(far_b1, "x", -1)]
    grads = weight_grads(att, act, gh, tie(gqkv, far_a0), g, normed)
    right_a, right_b, left_a, left_b, own_a, own_b, sums = input_back(
        ((1, 5), (3, 7), (0, 4)), place, gqkv, gh, w, tie(normed, grads), got
    )
    sums = sums + sums_far
    wide_grad = own_grad.astype(F32)
    bo_sum = jnp.sum(wide_grad, axis=0, keepdims=True)
    gain_sum = (sums[1:2] - bias * sums[0:1]) / gain
    bq_all = lax.dynamic_update_slice_in_dim(jnp.zeros((1, 16 * QKV), F32), bq_sum, seq * QKV, 1)
    b1_all = lax.dynamic_update_slice_in_dim(jnp.zeros((1, 16 * HID), F32), b1_sum, seq * HID, 1)
    packed = jnp.concatenate(
        [t.reshape(128, -1) for t in (gain_sum, sums[0:1], bq_all, bo_sum, b1_all)], axis=1
    )
    packed = packed.reshape(FS, 10, PIECE).astype(BF)
    grads = lax.dynamic_update_slice(grads, packed, (0, ALLW, 0))
    grads = lax.psum_scatter(tie(grads, right_a), fsdp, scatter_dimension=0, tiled=True)
    grad_qkv, grad_out, grad_fc1, grad_fc2, small = unpack(grads)
    small = small_sum(small[:10].reshape(4, 4, 160), (("z", 4, 0), ("x", 4, 0)))

    a = near_sum(own_a, right_a, left_a, "z").astype(BF)
    b = near_sum(own_b, right_b, left_b, "x").astype(BF)
    a = ring_sum(quarters(a), "x")
    b = ring_sum(quarters(b), "z")
    dn = jnp.concatenate([a, b], axis=0)
    wide = own.astype(F32)
    centered = wide - jnp.mean(wide, axis=1, keepdims=True)
    inv = lax.rsqrt(jnp.mean(centered * centered, axis=1, keepdims=True) + EPS)
    unit = centered * inv
    e = dn * gain
    input_grad = wide_grad + inv * (
        e - jnp.mean(e, axis=1, keepdims=True) - unit * jnp.mean(e * unit, axis=1, keepdims=True)
    )

    return (
        output[None],
        input_grad[None],
        small[0:16],
        small[16:32],
        grad_qkv,
        small[32:80],
        grad_out,
        small[80:96],
        grad_fc1,
        small[96:160],
        grad_fc2,
        small[80:96],
    )


def solution(mesh):
    split = Mesh(mesh.devices.reshape(4, 2, 4, 4), ("y", "core", "z", "x"))
    f, s = ("y", "core"), ("z", "x")
    both = f + s
    in_specs = (
        P(f, s, None), P(f, s, None), P(f, None), P(both), P(both), P(f, s), P(both), P(s, f), P(both),
        P(f, s), P(both), P(s, f), P(both),
    )
    out_specs = (
        P(f, s, None), P(f, s, None), P(both), P(both), P(f, s), P(both), P(s, f), P(both), P(f, s),
        P(both), P(s, f), P(both),
    )
    return jax.shard_map(on_device, mesh=split, in_specs=in_specs, out_specs=out_specs, check_vma=False)
```

```python
import functools
import math

import jax
import jax.numpy as jnp
import numpy as np
from jax import lax
from jax.experimental import pallas as pl
from jax.experimental.pallas import tpu as pltpu
from jax.sharding import Mesh
from jax.sharding import PartitionSpec as P

BF = jnp.bfloat16
F32 = jnp.float32
EPS = 1e-05
D = 2048
LEN = 2048
ROWS = 512
TOK = 128
HALF = 64
WIDE = D // 2
QKV = 384
HID = 512
ATT = 128
PIECE = 256
FS = 8
NEG = -1e30


SMALL = pl.CostEstimate(flops=1, bytes_accessed=1, transcendentals=0)
LARGE = pl.CostEstimate(flops=100 * 2**30, bytes_accessed=320 * 2**20, transcendentals=0)


def params(mib):
    return pltpu.CompilerParams(vmem_limit_bytes=mib * 2**20, dimension_semantics=("arbitrary",))


VM = pl.BlockSpec(memory_space=pltpu.VMEM)
SM = pl.BlockSpec(memory_space=pltpu.SMEM)
ANY = pl.BlockSpec(memory_space=pl.ANY)
HBM = pl.BlockSpec(memory_space=pltpu.HBM)


def whole(shape):
    return pl.BlockSpec(shape, lambda i, *_: (0,) * len(shape))


def rows_of(width):
    return pl.BlockSpec((ROWS, width), lambda i, *_: (i, 0))


def piece_start(place_ref, block, piece):
    first = block < 4
    z_off = jnp.where(first, block, piece)
    x_off = jnp.where(first, piece, block - 4)
    seq = lax.rem(place_ref[0] + z_off, 4) * 4 + lax.rem(place_ref[1] + x_off, 4)
    return pl.multiple_of(seq * TOK + jnp.where(first, 0, HALF), HALF)


def gather_pieces(place_ref, ref, block):
    return jnp.concatenate(
        [ref[pl.ds(piece_start(place_ref, block, s), HALF), :] for s in range(4)], axis=0
    )


def turn(v, table, sign=1.0):
    lane = lax.broadcasted_iota(jnp.int32, v.shape, 1)
    other = pltpu.roll(table, 64, 1)
    cos = jnp.where(lane < 64, table, other)
    sin = jnp.where(lane < 64, other, table)
    swapped = jnp.where(lax.rem(lane, 64) < 16, pltpu.roll(v, 112, 1), pltpu.roll(v, 16, 1))
    return v * cos + swapped * (sign * sin)


def pack_body(*refs):
    ins, (w_ref, vec_ref, a_ref, b_ref), scr, sem = refs[:11], refs[11:15], refs[15:25], refs[25]
    copies = [pltpu.make_async_copy(ins[k], scr[k], sem.at[k]) for k in range(10)]
    copies += [
        pltpu.make_async_copy(ins[10].at[:, k * WIDE : (k + 1) * WIDE], ref, sem.at[10 + k])
        for k, ref in enumerate((a_ref, b_ref))
    ]
    for copy in copies:
        copy.start()
    for copy in copies[:10]:
        copy.wait()
    wq_ref, w1_ref, wo_ref, w2_ref = scr[:4]
    low = lax.broadcasted_iota(jnp.int32, (PIECE, 128), 1) < 64
    g0, g1, g2 = [wq_ref[:, k * 128 : (k + 1) * 128].astype(F32) for k in range(3)]
    w_ref[0, 0:256, :128] = jnp.where(low, g0, g1).astype(BF)
    w_ref[0, 0:256, 128:] = pltpu.roll(jnp.where(low, g2, g0), 64, 1).astype(BF)
    w_ref[0, 256:512, :128] = jnp.where(low, g1, g2).astype(BF)
    w_ref[0, 256:512, 128:] = w1_ref[:, :128]
    w_ref[0, 512:768] = w1_ref[:, 128:384]
    w_ref[1, 0:128, :128] = w1_ref[:128, 384:]
    w_ref[1, 0:128, 128:] = w1_ref[128:, 384:]
    w_ref[1, 128:256] = wo_ref[...]
    w_ref[1, 256:768] = w2_ref[...]
    for k, ref in enumerate(scr[4:]):
        vec_ref[k : k + 1, : ref.shape[1]] = ref[...].astype(F32)
    for copy in copies[10:]:
        copy.wait()


def pack(*arrays):
    flat = [a if a.ndim == 2 else a[None, :] for a in arrays]
    return pl.pallas_call(
        pack_body,
        in_specs=[ANY] * 11,
        out_specs=[VM, VM, VM, VM],
        out_shape=[
            jax.ShapeDtypeStruct((2, 768, PIECE), BF),
            jax.ShapeDtypeStruct((8, 128), F32),
            jax.ShapeDtypeStruct((TOK, WIDE), BF),
            jax.ShapeDtypeStruct((TOK, WIDE), BF),
        ],
        scratch_shapes=[pltpu.VMEM(a.shape, BF) for a in flat[:10]] + [pltpu.SemaphoreType.DMA((12,))],
        cost_estimate=SMALL,
        compiler_params=pltpu.CompilerParams(vmem_limit_bytes=58 * 2**20),
        name="pack",
    )(*flat)


def document_start(starts_ref, token):
    first = jnp.zeros(token.shape, jnp.int32)
    for n in range(starts_ref.shape[1]):
        begin = starts_ref[0, n]
        first = jnp.where(token >= begin, begin, first)
    return first


def angles_body(starts_ref, table_ref, start_ref):
    block = pl.program_id(0)
    shape = (ROWS, 128)
    token = block * ROWS + lax.broadcasted_iota(jnp.int32, shape, 0)
    wide = lax.broadcasted_iota(jnp.int32, shape, 1)
    lane = lax.rem(wide, 64)
    freq = jnp.exp(lax.rem(lane, 16).astype(F32) * (-2.0 * math.log(10000.0) / 32))
    phase = (token - document_start(starts_ref, token)).astype(F32) * freq
    sin = jnp.sin(phase)
    cos = jnp.where(lane < 32, jnp.cos(phase), 1.0)
    sin = jnp.where(lane < 16, -sin, jnp.where(lane < 32, sin, 0.0))
    table_ref[...] = jnp.where(wide < 64, cos, sin)
    here = block * ROWS + lax.broadcasted_iota(jnp.int32, (1, ROWS), 1)
    start_ref[...] = document_start(starts_ref, here)


def angles(starts):
    return pl.pallas_call(
        angles_body,
        grid=(LEN // ROWS,),
        in_specs=[SM],
        out_specs=[rows_of(128), pl.BlockSpec((1, ROWS), lambda i: (0, i))],
        out_shape=[jax.ShapeDtypeStruct((LEN, 128), F32), jax.ShapeDtypeStruct((1, LEN), jnp.int32)],
        cost_estimate=SMALL,
        compiler_params=params(58),
        name="angles",
    )(starts)


def unpack_last(w_ref, last_ref):
    for f in range(FS):
        for k in range(2):
            at = f * PIECE + k * 128
            last_ref[at : at + 128, :] = w_ref[f, 0, :, k * 128 : (k + 1) * 128]


W_FIRST = pl.BlockSpec((FS, 1, 768, PIECE), lambda *_: (0, 0, 0, 0))
W_LAST = pl.BlockSpec((FS, 1, 128, PIECE), lambda *_: (0, 1, 0, 0))
WIDTHS = (D, QKV, HID, HID)


ORDER = (0, 1, 3, 2)


ORDER = (0, 1, 3, 2)


def turn_of(i):
    return jnp.where(i == 3, 2, jnp.where(i == 2, 3, i))


def project_body(
    place_ref, a0_ref, a1_ref, a2_ref, a3_ref, a4_ref, b0_ref, b1_ref, b2_ref, b3_ref, b4_ref,
    gain_ref, bias_ref, w_ref, wl_ref, b_ref, table_ref,
    normed_ref, qkv_ref, act_ref, slope_ref, last_ref, x_scr, sem,
):
    step = pl.program_id(0)
    slot = lax.rem(step, 2)
    a_refs = ((a0_ref,), (a1_ref,), (a2_ref, a3_ref), (a4_ref,))

    def fetch(k, start):
        scr, sems = x_scr.at[k % 2], sem.at[k % 2]
        z_at = lax.rem(place_ref[0] + ORDER[k], 4)

        def go(src, dst, t):
            copy = pltpu.make_async_copy(src, dst, sems.at[t])
            copy.start() if start else copy.wait()

        at = 0
        for t, ref in enumerate(a_refs[ORDER[k]]):
            n = ref.shape[0]
            go(ref, scr.at[at : at + n, :, :WIDE], t)
            at += n
        for x_off, ref in ((0, b0_ref), (1, b1_ref), (3, b4_ref)):
            go(ref.at[z_at], scr.at[lax.rem(place_ref[1] + x_off, 4), :, WIDE:], 2 + x_off)
        far = scr.at[lax.rem(place_ref[1] + 2, 4), :, WIDE:]

        @pl.when(z_at < 2)
        def _():
            go(b2_ref.at[z_at], far, 4)

        @pl.when(z_at >= 2)
        def _():
            go(b3_ref.at[z_at - 2], far, 4)

    for k in range(4):

        @pl.when(step == k)
        def _():
            if k == 0:
                fetch(0, True)
            if k < 3:
                fetch(k + 1, True)
            fetch(k, False)

    @pl.when(pl.program_id(0) == 0)
    def _():
        unpack_last(wl_ref, last_ref)

    x = x_scr[slot].reshape(ROWS, D).astype(F32)
    centered = x - jnp.mean(x, axis=1, keepdims=True)
    inv = lax.rsqrt(jnp.mean(centered * centered, axis=1, keepdims=True) + EPS)
    normed_ref[...] = (centered * inv * gain_ref[...] + bias_ref[...]).astype(BF)

    def group(j):
        normed = normed_ref[...]
        if j == 3:
            return jnp.dot(normed, last_ref[...], preferred_element_type=F32) + b_ref[:, 768:]
        w = w_ref[:, 0, j * 256 : (j + 1) * 256].reshape(D, PIECE)
        return jnp.dot(normed, w, preferred_element_type=F32) + b_ref[:, j * 256 : (j + 1) * 256]

    table = table_ref[...]

    def hidden(h, cols):
        k0 = math.sqrt(2.0 / math.pi)
        h2 = h * h
        t = jnp.tanh(h * (k0 + (k0 * 0.044715) * h2))
        act_ref[:, cols] = (0.5 * h * (1.0 + t)).astype(BF)
        slope = 0.5 * (1.0 + t) + 0.5 * h * (1.0 - t * t) * (k0 + (3 * 0.044715 * k0) * h2)
        slope_ref[:, cols] = slope.astype(BF)

    qk = group(0).astype(BF).astype(F32)
    qkv_ref[:, 0:128] = (turn(qk[:, :128], table) * 0.125).astype(BF)
    qkv_ref[:, 128:256] = turn(qk[:, 128:], table).astype(BF)
    vh = group(1)
    qkv_ref[:, 256:384] = vh[:, :128].astype(BF)
    hidden(vh[:, 128:], slice(0, 128))
    hidden(group(2), slice(128, 384))
    hidden(group(3), slice(384, 512))


def turned_rows(width):
    return pl.BlockSpec((ROWS, width), lambda i, place: (lax.rem(place[0] + turn_of(i), 4), 0))


def project(place, x_a, x_b, gain, bias, w, b, table):
    return pl.pallas_call(
        project_body,
        grid_spec=pltpu.PrefetchScalarGridSpec(
            num_scalar_prefetch=1,
            grid=(4,),
            in_specs=[HBM] * 10
            + [whole((1, D)), whole((1, D)), W_FIRST, W_LAST, whole((1, QKV + HID)), turned_rows(128)],
            out_specs=[turned_rows(D), turned_rows(QKV), turned_rows(HID), turned_rows(HID)],
            scratch_shapes=[
                pltpu.VMEM((D, 128), BF),
                pltpu.VMEM((2, 4, TOK, D), BF),
                pltpu.SemaphoreType.DMA((2, 6)),
            ],
        ),
        out_shape=[jax.ShapeDtypeStruct((LEN, width), BF) for width in (D, QKV, HID, HID)],
        cost_estimate=LARGE,
        compiler_params=params(34),
        name="project",
    )(place, *map(in_hbm, (*x_a, *x_b)), gain, bias, w, w, b, in_hbm(table))


AQ = 512
AK = 256
NQ = LEN // AQ


def padded_turned(ref, scr):
    row = lax.broadcasted_iota(jnp.int32, (128, AQ), 0)
    for i in range(NQ):
        cols = slice(i * AQ, (i + 1) * AQ)
        t = ref[cols, :].astype(F32).T
        scr[0, :, cols] = jnp.where(row < 64, t, 0.0).astype(BF)
        scr[1, :, cols] = jnp.where(row < 64, 0.0, t).astype(BF)


def padded(ref, scr):
    lane = lax.broadcasted_iota(jnp.int32, (AQ, 128), 1)
    for i in range(NQ):
        rows = slice(i * AQ, (i + 1) * AQ)
        v = ref[rows, :].astype(F32)
        scr[0, rows, :] = jnp.where(lane < 64, v, 0.0).astype(BF)
        scr[1, rows, :] = jnp.where(lane < 64, 0.0, v).astype(BF)


def fold(op, v):
    return op(v.reshape(AK // 8, 8, AQ), axis=0)


def attend_body(first_ref, qkv_ref, start_ref, att_ref, lse_ref, qt_scr, vt_scr, s_scr):
    padded_turned(qkv_ref.at[:, 0:128], qt_scr)
    for i in range(NQ):
        rows = slice(i * AQ, (i + 1) * AQ)
        vt_scr[:, rows] = qkv_ref[rows, 256:384].astype(F32).T.astype(BF)
    row = lax.broadcasted_iota(jnp.int32, (AK, AQ), 0)
    col = lax.broadcasted_iota(jnp.int32, (AK, AQ), 1)

    def q_block(i, _):
        cols = pl.ds(pl.multiple_of(i * AQ, AQ), AQ)
        start = start_ref[:, cols]
        qt = [qt_scr[h, :, cols] for h in range(2)]

        def scores(j, ok, peaks):
            rows = pl.ds(pl.multiple_of(j * AK, AK), AK)
            k = qkv_ref[rows, 128:256]
            new = []
            for h in range(2):
                s = jnp.dot(k, qt[h], preferred_element_type=F32)
                s = jnp.where(ok, s, NEG)
                s_scr[h, rows, :] = s
                new.append(jnp.maximum(peaks[h], fold(jnp.max, s)))
            return tuple(new)

        low = first_ref[i]
        peaks = (jnp.full((8, AQ), NEG, F32),) * 2
        for d in range(2):
            peaks = scores(2 * i + d, (row + (2 * i + d) * AK >= start) & (row + d * AK <= col), peaks)
        peaks = lax.fori_loop(low, 2 * i, lambda j, p: scores(j, row + j * AK >= start, p), peaks)
        peak = [jnp.max(p, axis=0, keepdims=True) for p in peaks]

        def values(j, state):
            rows = pl.ds(pl.multiple_of(j * AK, AK), AK)
            new = []
            for h in range(2):
                total, o = state[2 * h : 2 * h + 2]
                p = jnp.exp(s_scr[h, rows, :] - peak[h])
                total = total + fold(jnp.sum, p)
                o = o + jnp.dot(
                    vt_scr[64 * h : 64 * h + 64, rows], p.astype(BF), preferred_element_type=F32
                )
                new += [total, o]
            return tuple(new)

        state = (jnp.zeros((8, AQ), F32), jnp.zeros((64, AQ), F32)) * 2
        state = lax.fori_loop(low, 2 * i + 2, values, state)
        total = [jnp.sum(state[2 * h], axis=0, keepdims=True) for h in range(2)]
        both = jnp.concatenate([state[1] / total[0], state[3] / total[1]], axis=0)
        att_ref[cols, :] = both.T.astype(BF)
        for h in range(2):
            lse_ref[h : h + 1, cols] = peak[h] + jnp.log(total[h])
        return 0

    lax.fori_loop(0, NQ, q_block, 0)


def attend(first, qkv, start):
    return pl.pallas_call(
        attend_body,
        in_specs=[SM, VM, VM],
        out_specs=[VM, VM],
        out_shape=[
            jax.ShapeDtypeStruct((LEN, ATT), BF),
            jax.ShapeDtypeStruct((2, LEN), F32),
        ],
        scratch_shapes=[
            pltpu.VMEM((2, 128, LEN), BF),
            pltpu.VMEM((128, LEN), BF),
            pltpu.VMEM((2, LEN, AQ), F32),
        ],
        cost_estimate=LARGE,
        compiler_params=pltpu.CompilerParams(vmem_limit_bytes=24 * 2**20),
        name="attend",
    )(first, qkv, start)


def attend_back_body(
    first_ref, qkv_ref, att_ref, ga_ref, lse_ref, start_ref, table_ref,
    gqkv_ref, bsum_ref,
    q_scr, go_scr, qt_scr, got_scr, kt_scr, dl_scr, dk_scr, dv_scr,
):
    padded(qkv_ref.at[:, 0:128], q_scr)
    padded(ga_ref, go_scr)
    padded_turned(qkv_ref.at[:, 0:128], qt_scr)
    for i in range(NQ):
        rows = slice(i * AQ, (i + 1) * AQ)
        kt_scr[:, rows] = qkv_ref[rows, 128:256].astype(F32).T.astype(BF)
        got = ga_ref[rows, :].astype(F32).T
        prod = got * att_ref[rows, :].astype(F32).T
        row = lax.broadcasted_iota(jnp.int32, (128, AQ), 0)
        got_scr[0, :, rows] = jnp.where(row < 64, got, 0.0).astype(BF)
        got_scr[1, :, rows] = jnp.where(row < 64, 0.0, got).astype(BF)
        for h in range(2):
            dl_scr[h : h + 1, rows] = jnp.sum(prod[64 * h : 64 * h + 64], axis=0, keepdims=True)
    dk_scr[...] = jnp.zeros_like(dk_scr)
    dv_scr[...] = jnp.zeros_like(dv_scr)
    row = lax.broadcasted_iota(jnp.int32, (AK, AQ), 0)
    col = lax.broadcasted_iota(jnp.int32, (AK, AQ), 1)

    def q_block(i, bsum):
        cols = pl.ds(pl.multiple_of(i * AQ, AQ), AQ)
        start = start_ref[:, cols]
        lse = [lse_ref[h : h + 1, cols] for h in range(2)]
        dl = [dl_scr[h : h + 1, cols] for h in range(2)]

        def pair(j, ok, dq):
            rows = pl.ds(pl.multiple_of(j * AK, AK), AK)
            k = qkv_ref[rows, 128:256]
            v = qkv_ref[rows, 256:384]
            dv = dk = 0.0
            new = []
            for h in range(2):
                s = jnp.dot(k, qt_scr[h, :, cols], preferred_element_type=F32)
                dp = jnp.dot(v, got_scr[h, :, cols], preferred_element_type=F32)
                p = jnp.where(ok, jnp.exp(s - lse[h]), 0.0)
                ds = (p * (dp - dl[h])).astype(BF)
                dv += jnp.dot(p.astype(BF), go_scr[h, cols, :], preferred_element_type=F32)
                dk += jnp.dot(ds, q_scr[h, cols, :], preferred_element_type=F32)
                new.append(
                    dq[h]
                    + jnp.dot(kt_scr[64 * h : 64 * h + 64, rows], ds, preferred_element_type=F32)
                )
            dv_scr[rows, :] += dv
            dk_scr[rows, :] += dk
            return tuple(new)

        dq = (jnp.zeros((64, AQ), F32),) * 2
        for d in range(2):
            dq = pair(2 * i + d, (row + (2 * i + d) * AK >= start) & (row + d * AK <= col), dq)
        dq = lax.fori_loop(first_ref[i], 2 * i, lambda j, dq: pair(j, row + j * AK >= start, dq), dq)
        dq = (jnp.concatenate(dq, axis=0) * 0.125).T
        out = turn(dq, table_ref[cols, :], -1.0).astype(BF)
        gqkv_ref[cols, 0:128] = out
        return bsum + jnp.sum(out.astype(F32), axis=0, keepdims=True)

    bsum_ref[:, 0:128] = lax.fori_loop(0, NQ, q_block, jnp.zeros((1, 128), F32))

    def finish(i, total):
        rows = pl.ds(pl.multiple_of(i * AQ, AQ), AQ)
        dk = turn(dk_scr[rows, :], table_ref[rows, :], -1.0)
        out = jnp.concatenate([dk, dv_scr[rows, :]], axis=1).astype(BF)
        gqkv_ref[rows, 128:384] = out
        return total + jnp.sum(out.astype(F32), axis=0, keepdims=True)

    bsum_ref[:, 128:384] = lax.fori_loop(0, NQ, finish, jnp.zeros((1, 256), F32))


def attend_back(first, qkv, att, ga, lse, start, table):
    return pl.pallas_call(
        attend_back_body,
        in_specs=[SM] + [VM] * 6,
        out_specs=[VM, VM],
        out_shape=[
            jax.ShapeDtypeStruct((LEN, QKV), BF),
            jax.ShapeDtypeStruct((1, QKV), F32),
        ],
        scratch_shapes=[
            pltpu.VMEM((2, LEN, 128), BF),
            pltpu.VMEM((2, LEN, 128), BF),
            pltpu.VMEM((2, 128, LEN), BF),
            pltpu.VMEM((2, 128, LEN), BF),
            pltpu.VMEM((128, LEN), BF),
            pltpu.VMEM((2, LEN), F32),
            pltpu.VMEM((LEN, 128), F32),
            pltpu.VMEM((LEN, 128), F32),
        ],
        cost_estimate=LARGE,
        compiler_params=pltpu.CompilerParams(vmem_limit_bytes=24 * 2**20),
        name="attend_back",
    )(first, qkv, att, ga, lse, start, table)


def emit_body(att_ref, act_ref, w_ref, out_ref):
    both = jnp.concatenate([att_ref[...], act_ref[...]], axis=1)
    for f in range(FS):
        out_ref[:, f * PIECE : (f + 1) * PIECE] = jnp.dot(
            both, w_ref[f, 0, 128:], preferred_element_type=F32
        ).astype(BF)


def emit(att, act, w):
    return pl.pallas_call(
        emit_body,
        grid=(LEN // ROWS,),
        in_specs=[rows_of(ATT), rows_of(HID), pl.BlockSpec((FS, 1, 768, PIECE), lambda i, *_: (0, 1, 0, 0))],
        out_specs=rows_of(D),
        out_shape=pltpu.HBM((LEN, D), BF),
        cost_estimate=LARGE,
        compiler_params=params(24),
        name="emit",
    )(att, act, w)


def emit_back_body(g_ref, w_ref, slope_ref, ga_ref, gh_ref, bsum_ref):
    total = jnp.zeros((ROWS, ATT + HID), F32)
    for f in range(FS):
        total += lax.dot_general(
            g_ref[:, f * PIECE : (f + 1) * PIECE], w_ref[f, 0, 128:], (((1,), (1,)), ((), ())),
            preferred_element_type=F32,
        )
    ga_ref[...] = total[:, :ATT].astype(BF)
    gh = (total[:, ATT:] * slope_ref[...].astype(F32)).astype(BF)
    gh_ref[...] = gh

    @pl.when(pl.program_id(0) == 0)
    def _():
        bsum_ref[...] = jnp.zeros_like(bsum_ref)

    bsum_ref[...] += jnp.sum(gh.astype(F32), axis=0, keepdims=True)


def emit_back(g, w, slope):
    return pl.pallas_call(
        emit_back_body,
        grid=(LEN // ROWS,),
        in_specs=[rows_of(D), pl.BlockSpec((FS, 1, 768, PIECE), lambda i: (0, 1, 0, 0)), rows_of(HID)],
        out_specs=[rows_of(ATT), rows_of(HID), whole((1, HID))],
        out_shape=[
            jax.ShapeDtypeStruct((LEN, ATT), BF),
            jax.ShapeDtypeStruct((LEN, HID), BF),
            jax.ShapeDtypeStruct((1, HID), F32),
        ],
        cost_estimate=LARGE,
        compiler_params=params(26),
        name="emit_back",
    )(in_hbm(g), in_hbm(w), slope)


ALLW = QKV + ATT + 2 * HID
EXTRA = 16


def weight_grads_body(att_ref, act_ref, gh_ref, gqkv_ref, g_ref, normed_ref, out_ref, turned):
    @pl.when(pl.program_id(0) == 0)
    def _():
        for block in range(8):
            rows = slice(block * PIECE, (block + 1) * PIECE)
            at = 0
            for ref, n in ((att_ref, ATT), (act_ref, HID), (gh_ref, HID), (gqkv_ref, QKV)):
                turned[at : at + n, rows] = ref[rows, :].T
                at += n

    cut = ATT + HID
    out_ref[0, :cut] = jnp.dot(turned[:cut], g_ref[...], preferred_element_type=F32).astype(BF)
    out_ref[0, cut:ALLW] = jnp.dot(turned[cut:], normed_ref[...], preferred_element_type=F32).astype(BF)
    out_ref[0, ALLW:] = jnp.zeros((EXTRA, PIECE), BF)


def column_piece():
    return pl.BlockSpec((LEN, PIECE), lambda i: (0, i))


def weight_grads(att, act, gh, gqkv, g, normed):
    return pl.pallas_call(
        weight_grads_body,
        grid=(FS,),
        in_specs=[
            whole((LEN, ATT)), whole((LEN, HID)), whole((LEN, HID)), whole((LEN, QKV)),
            column_piece(), column_piece(),
        ],
        out_specs=pl.BlockSpec((1, ALLW + EXTRA, PIECE), lambda i: (i, 0, 0)),
        scratch_shapes=[pltpu.VMEM((ALLW, LEN), BF)],
        out_shape=pltpu.HBM((FS, ALLW + EXTRA, PIECE), BF),
        cost_estimate=LARGE,
        compiler_params=params(34),
        name="weight_grads",
    )(att, act, gh, gqkv, in_hbm(g), in_hbm(normed))


def unpack_body(sums_ref, qkv_ref, out_ref, fc1_ref, fc2_ref, small_ref):
    out_ref[...] = sums_ref[0, :ATT].astype(F32)
    fc2_ref[...] = sums_ref[0, ATT : ATT + HID].astype(F32)
    fc1_ref[...] = sums_ref[0, ATT + HID : ATT + 2 * HID].astype(F32).T
    at = ATT + 2 * HID
    q, k, v = [sums_ref[0, at + n * 128 : at + (n + 1) * 128].astype(F32).T for n in range(3)]
    low = lax.broadcasted_iota(jnp.int32, (PIECE, 128), 1) < 64
    qkv_ref[:, 0:128] = jnp.where(low, q, pltpu.roll(k, 64, 1))
    qkv_ref[:, 128:256] = jnp.where(low, v, q)
    qkv_ref[:, 256:384] = jnp.where(low, pltpu.roll(k, 64, 1), v)
    small_ref[...] = sums_ref[0, ALLW:].astype(F32)


def unpack(sums):
    shapes = [(PIECE, QKV), (ATT, PIECE), (PIECE, HID), (HID, PIECE), (EXTRA, PIECE)]
    return pl.pallas_call(
        unpack_body,
        in_specs=[VM],
        out_specs=[VM] * 5,
        out_shape=[jax.ShapeDtypeStruct(shape, F32) for shape in shapes],
        cost_estimate=SMALL,
        compiler_params=pltpu.CompilerParams(vmem_limit_bytes=16 * 2**20),
        name="unpack",
    )(sums)


def block_of(pairs, step, side):
    block = jnp.int32(pairs[0][side])
    for k in range(1, len(pairs)):
        block = jnp.where(step == k, pairs[k][side], block)
    return block


def input_back_body(pairs, place_ref, gqkv_ref, gh_ref, w_ref, wl_ref, *refs):
    step = pl.program_id(0)
    normed_refs, refs = refs[:8], refs[8:]
    sums_ref, last_ref, out_scr = refs[-3:]
    far = len(pairs) == 1
    got_refs, out_refs = ((), refs[:-3]) if far else (refs[:4], refs[4:-3])
    blocks = [block_of(pairs, step, side) for side in range(2)]

    def pieces(ref):
        return jnp.concatenate([gather_pieces(place_ref, ref, block) for block in blocks], axis=0)

    both = jnp.concatenate([pieces(gqkv_ref), pieces(gh_ref)], axis=1)

    @pl.when(step == 0)
    def _():
        sums_ref[...] = jnp.zeros_like(sums_ref)
        unpack_last(wl_ref, last_ref)

    turned = (((1,), (1,)), ((), ()))
    for f in range(FS):
        cols = slice(f * PIECE, (f + 1) * PIECE)
        part = lax.dot_general(both[:, 768:], last_ref[cols, :], turned, preferred_element_type=F32)
        for j in range(3):
            part += lax.dot_general(
                both[:, j * 256 : (j + 1) * 256], w_ref[f, 0, j * 256 : (j + 1) * 256], turned,
                preferred_element_type=F32,
            )
        out_scr[:, cols] = part
        normed = jnp.concatenate([ref[0, 0, :, cols] for ref in normed_refs], axis=0).astype(F32)
        sums_ref[0:1, cols] += jnp.sum(part, axis=0, keepdims=True)
        sums_ref[1:2, cols] += jnp.sum(part * normed, axis=0, keepdims=True)
    if far:
        for k in range(4):
            out_refs[k][...] = out_scr[k * 128 : (k + 1) * 128, :].astype(BF)
        return
    for k in range(3):

        @pl.when(step == k)
        def _():
            for side in range(2):
                for part in range(2):
                    at = side * PIECE + part * 128
                    v = out_scr[at : at + 128, :]
                    if k == part:
                        v += got_refs[2 * side + part][...].astype(F32)
                    out_refs[2 * k + side][part * 128 : (part + 1) * 128, :] = v.astype(BF)


def piece_spec(pairs, m):
    def where_to(i, place_ref):
        start = piece_start(place_ref, block_of(pairs, i, m // 4), m % 4)
        return (start // TOK, m // 4, 0, 0)

    return pl.BlockSpec((1, 1, HALF, D), where_to)


def input_back(pairs, place, gqkv, gh, w, normed, got=()):
    n = len(pairs)
    outs = [(128, D)] * 4 if n == 1 else [(PIECE, D)] * 6
    return pl.pallas_call(
        functools.partial(input_back_body, pairs),
        grid_spec=pltpu.PrefetchScalarGridSpec(
            num_scalar_prefetch=1,
            grid=(n,),
            in_specs=[whole((LEN, QKV)), whole((LEN, HID)), W_FIRST, W_LAST]
            + [piece_spec(pairs, m) for m in range(8)]
            + [whole((128, D))] * len(got),
            out_specs=[whole(shape) for shape in outs] + [whole((2, D))],
            scratch_shapes=[pltpu.VMEM((D, 128), BF), pltpu.VMEM((2 * PIECE, D), F32)],
        ),
        out_shape=[pltpu.HBM(shape, BF) for shape in outs] + [jax.ShapeDtypeStruct((2, D), F32)],
        cost_estimate=LARGE,
        compiler_params=params(44),
        name="input_back",
    )(place, gqkv, gh, in_hbm(w), in_hbm(w), *[in_hbm(normed.reshape(16, 2, HALF, D))] * 8, *got)


def copy_body(moves, n_in, in_hbm_out, place_ref, *refs):
    n_out = len(refs) - n_in - 1
    if in_hbm_out:
        n_out //= 2
    ins, outs, sem = refs[:n_in], refs[n_in : n_in + n_out], refs[-1]
    to = refs[n_in + n_out : -1] if in_hbm_out else outs
    copies = [
        pltpu.make_async_copy(src(ins), dst(to, place_ref), sem.at[k]) for k, (src, dst) in enumerate(moves)
    ]
    for copy in copies:
        copy.start()
    for copy in copies:
        copy.wait()
    if in_hbm_out:
        copies = [pltpu.make_async_copy(scr, out, sem.at[k]) for k, (scr, out) in enumerate(zip(to, outs))]
        for copy in copies:
            copy.start()
        for copy in copies:
            copy.wait()


def copy_kernel(name, moves, place, ins, out_shapes, in_hbm_out=False):
    n = len(out_shapes)
    return pl.pallas_call(
        functools.partial(copy_body, moves, len(ins), in_hbm_out),
        in_specs=[SM] + [HBM if in_hbm_out else ANY] * len(ins),
        out_specs=[HBM if in_hbm_out else VM] * n,
        out_shape=[jax.ShapeDtypeStruct(shape, BF) for shape in out_shapes],
        scratch_shapes=[pltpu.VMEM(shape, BF) for shape in out_shapes if in_hbm_out]
        + [pltpu.SemaphoreType.DMA((len(moves),))],
        cost_estimate=SMALL,
        compiler_params=pltpu.CompilerParams(vmem_limit_bytes=58 * 2**20),
        name=name,
    )(place, *(map(in_hbm, ins) if in_hbm_out else ins))


def join(place, pieces_a, pieces_b):
    def move(k):
        axis = 1 - k // 4
        return (
            lambda ins: ins[k],
            lambda outs, place_ref: outs[k // 4].at[lax.rem(place_ref[axis] + k % 4, 4)],
        )

    moves = [move(k) for k in range(8)]
    return copy_kernel("join", moves, place, [*pieces_a, *pieces_b], [(4, TOK, WIDE)] * 2, True)


def halves(place, left_a, right_a, left_b, right_b):
    def move(k):
        spot = slice(k % 2 * 2, k % 2 * 2 + 2)
        return (lambda ins: ins[k].at[spot], lambda outs, place_ref: outs[k])

    moves = [move(k) for k in range(4)]
    return copy_kernel("halves", moves, place, [left_a, right_a, left_b, right_b], [(2, TOK, WIDE)] * 4, True)


def shift(v, axis, by, n=4):
    return lax.ppermute(v, axis, [(i, (i + by) % n) for i in range(n)])


def in_hbm(v):
    return pltpu.with_memory_space_constraint(v, pltpu.HBM)


def tie(v, *others):
    return lax.optimization_barrier((v,) + others)[0]


def plus(a, b):
    return (a.astype(F32) + b.astype(F32)).astype(BF)


def near_sum(own, right, left, axis):
    return own.astype(F32) + shift(right, axis, 1).astype(F32) + shift(left, axis, -1).astype(F32)


def ring_sum_first(parts, axis):
    own, right, far, left = parts
    got = [shift(far, axis, 2), shift(right, axis, 1), shift(left, axis, -1)]
    total = own.astype(F32)
    for v in got:
        total = total + v.astype(F32)
    return total, got[1]


def ring_sum(parts, axis):
    return ring_sum_first(parts, axis)[0]


def quarters(v):
    n = v.shape[0] // 4
    return [v[i * n : (i + 1) * n] for i in range(4)]


def small_gather(v, axes):
    for axis in axes:
        n = 2 if axis == "core" else 4
        me = lax.axis_index(axis)
        out = jnp.zeros((n,) + v.shape, v.dtype)
        out = lax.dynamic_update_index_in_dim(out, v, me, 0)
        for by in range(1, n):
            got = shift(v, axis, by, n)
            out = lax.dynamic_update_index_in_dim(out, got, lax.rem(me + n - by, n), 0)
        v = out
    return v


def small_sum(v, axes):
    for axis, n, dim in axes:
        me = lax.axis_index(axis)
        total = lax.dynamic_index_in_dim(v, me, dim, keepdims=False)
        for by in range(1, n):
            part = lax.dynamic_index_in_dim(v, lax.rem(me + by, n), dim, keepdims=False)
            total = total + shift(part, axis, by, n)
        v = total
    return v


def on_device(
    tokens, cotangent, doc_starts, ln_gain, ln_bias, w_qkv, b_qkv, w_out, b_out, w_fc1, b_fc1, w_fc2, b_fc2,
):
    own = tokens[0]
    own_grad = cotangent[0]
    z_me, x_me = lax.axis_index("z"), lax.axis_index("x")
    seq = z_me * 4 + x_me
    place = jnp.stack([z_me, x_me, lax.axis_index("core"), lax.axis_index("y")]).astype(jnp.int32)

    fsdp = ("y", "core")
    w, vectors, own_a, own_b = pack(
        w_qkv, w_fc1, w_out, w_fc2, ln_gain, ln_bias, b_qkv, b_out, b_fc1, b_fc2, own
    )
    w = lax.all_gather(w, fsdp, axis=0).reshape(FS, 2, 768, PIECE)
    vectors = small_gather(vectors, ("x", "z"))
    vectors, own_a, own_b = lax.optimization_barrier((vectors, own_a, own_b))
    a, b = join(
        place,
        [own_a] + [shift(own_a, "x", -by) for by in (1, 2, 3)],
        [own_b] + [shift(own_b, "z", -by) for by in (1, 2, 3)],
    )
    g = lax.all_gather(tie(own_grad, a), ("z", "x"), axis=0, tiled=True)
    left_a, right_a, left_b, right_b = shift(a, "z", 1), shift(a, "z", -1), shift(b, "x", 1), shift(b, "x", -1)
    far = halves(place, left_a, right_a, left_b, right_b)
    x_a = [a, right_a, shift(far[0], "z", 1), shift(far[1], "z", -1), left_a]
    x_b = [b, right_b, shift(far[2], "x", 1), shift(far[3], "x", -1), left_b]
    vectors = small_gather(vectors, ("y", "core"))
    table, start = angles(tie(doc_starts, far[0]))
    first = start[0, ::AQ] // AK
    vectors = vectors.transpose(1, 0, 2, 3, 4, 5).reshape(128, 8, 128)

    sizes = [16, 16, 48, 16, 64, 16]
    gain, bias, bq, bo, b1, b2 = [vectors[:, k, :n].reshape(1, -1) for k, n in enumerate(sizes)]
    b_in = jnp.concatenate(
        [
            lax.dynamic_slice_in_dim(bq, seq * QKV, QKV, 1).reshape(2, 3, 64).transpose(1, 0, 2).reshape(1, QKV),
            lax.dynamic_slice_in_dim(b1, seq * HID, HID, 1),
        ],
        axis=1,
    )

    normed, qkv, act, slope = project(place, x_a, x_b, gain, bias, w, b_in, table)
    att, lse = attend(first, qkv, start)
    out_part = emit(att, act, w)
    out_sum = lax.psum_scatter(out_part, ("z", "x"), scatter_dimension=0, tiled=True)
    output = (own.astype(F32) + out_sum.astype(F32) + bo + b2).astype(BF)

    ga, gh, b1_sum = emit_back(tie(g, out_part), w, slope)
    gqkv, bq_sum = attend_back(first, qkv, att, ga, lse, start, table)
    bq_sum = bq_sum.reshape(3, 2, 64).transpose(1, 0, 2).reshape(1, QKV)
    far_a0, far_a1, far_b0, far_b1, sums_far = input_back(((2, 6),), place, gqkv, gh, w, normed)
    got = [shift(far_a0, "z", 1), shift(far_a1, "z", -1), shift(far_b0, "x", 1), shift(far_b1, "x", -1)]
    grads = weight_grads(att, act, gh, tie(gqkv, far_a0), g, normed)
    right_a, right_b, left_a, left_b, own_a, own_b, sums = input_back(
        ((1, 5), (3, 7), (0, 4)), place, gqkv, gh, w, tie(normed, grads), got
    )
    sums = sums + sums_far
    wide_grad = own_grad.astype(F32)
    bo_sum = jnp.sum(wide_grad, axis=0, keepdims=True)
    gain_sum = (sums[1:2] - bias * sums[0:1]) / gain
    bq_all = lax.dynamic_update_slice_in_dim(jnp.zeros((1, 16 * QKV), F32), bq_sum, seq * QKV, 1)
    b1_all = lax.dynamic_update_slice_in_dim(jnp.zeros((1, 16 * HID), F32), b1_sum, seq * HID, 1)
    packed = jnp.concatenate(
        [t.reshape(128, -1) for t in (gain_sum, sums[0:1], bq_all, bo_sum, b1_all)], axis=1
    )
    small = small_sum(packed.reshape(4, 2, 4, 4, -1), (("z", 4, 2), ("x", 4, 2)))
    small, right_a, right_b, left_a, left_b = lax.optimization_barrier((small, right_a, right_b, left_a, left_b))
    small = small.reshape(FS, 1, 160).astype(BF)
    grads = lax.dynamic_update_slice(grads, small, (0, ALLW, 0))
    grads = lax.psum_scatter(grads, fsdp, scatter_dimension=0, tiled=True)
    grad_qkv, grad_out, grad_fc1, grad_fc2, small = unpack(grads)
    small = small[0, :160]

    a = near_sum(own_a, right_a, left_a, "z").astype(BF)
    b = near_sum(own_b, right_b, left_b, "x").astype(BF)
    a = ring_sum(quarters(a), "x")
    b = ring_sum(quarters(b), "z")
    dn = jnp.concatenate([a, b], axis=0)
    wide = own.astype(F32)
    centered = wide - jnp.mean(wide, axis=1, keepdims=True)
    inv = lax.rsqrt(jnp.mean(centered * centered, axis=1, keepdims=True) + EPS)
    unit = centered * inv
    e = dn * gain
    input_grad = wide_grad + inv * (
        e - jnp.mean(e, axis=1, keepdims=True) - unit * jnp.mean(e * unit, axis=1, keepdims=True)
    )

    return (
        output[None],
        input_grad[None],
        small[0:16],
        small[16:32],
        grad_qkv,
        small[32:80],
        grad_out,
        small[80:96],
        grad_fc1,
        small[96:160],
        grad_fc2,
        small[80:96],
    )


def solution(mesh):
    split = Mesh(mesh.devices.reshape(4, 2, 4, 4), ("y", "core", "z", "x"))
    f, s = ("y", "core"), ("z", "x")
    both = f + s
    in_specs = (
        P(f, s, None), P(f, s, None), P(f, None), P(both), P(both), P(f, s), P(both), P(s, f), P(both),
        P(f, s), P(both), P(s, f), P(both),
    )
    out_specs = (
        P(f, s, None), P(f, s, None), P(both), P(both), P(f, s), P(both), P(s, f), P(both), P(f, s),
        P(both), P(s, f), P(both),
    )
    return jax.shard_map(on_device, mesh=split, in_specs=in_specs, out_specs=out_specs, check_vma=False)
```

```python
import functools
import math

import jax
import jax.numpy as jnp
import numpy as np
from jax import lax
from jax.experimental import pallas as pl
from jax.experimental.pallas import tpu as pltpu
from jax.sharding import Mesh
from jax.sharding import PartitionSpec as P

BF = jnp.bfloat16
F32 = jnp.float32
EPS = 1e-05
D = 2048
LEN = 2048
ROWS = 512
TOK = 128
HALF = 64
WIDE = D // 2
QKV = 384
HID = 512
ATT = 128
PIECE = 256
FS = 8
NEG = -1e30


SMALL = pl.CostEstimate(flops=1, bytes_accessed=1, transcendentals=0)
LARGE = pl.CostEstimate(flops=100 * 2**30, bytes_accessed=320 * 2**20, transcendentals=0)


def params(mib):
    return pltpu.CompilerParams(vmem_limit_bytes=mib * 2**20, dimension_semantics=("arbitrary",))


VM = pl.BlockSpec(memory_space=pltpu.VMEM)
SM = pl.BlockSpec(memory_space=pltpu.SMEM)
ANY = pl.BlockSpec(memory_space=pl.ANY)
HBM = pl.BlockSpec(memory_space=pltpu.HBM)


def whole(shape):
    return pl.BlockSpec(shape, lambda i, *_: (0,) * len(shape))


def rows_of(width):
    return pl.BlockSpec((ROWS, width), lambda i, *_: (i, 0))


def piece_start(place_ref, block, piece):
    first = block < 4
    z_off = jnp.where(first, block, piece)
    x_off = jnp.where(first, piece, block - 4)
    seq = lax.rem(place_ref[0] + z_off, 4) * 4 + lax.rem(place_ref[1] + x_off, 4)
    return pl.multiple_of(seq * TOK + jnp.where(first, 0, HALF), HALF)


def gather_pieces(place_ref, ref, block):
    return jnp.concatenate(
        [ref[pl.ds(piece_start(place_ref, block, s), HALF), :] for s in range(4)], axis=0
    )


def turn(v, table, sign=1.0):
    lane = lax.broadcasted_iota(jnp.int32, v.shape, 1)
    other = pltpu.roll(table, 64, 1)
    cos = jnp.where(lane < 64, table, other)
    sin = jnp.where(lane < 64, other, table)
    swapped = jnp.where(lax.rem(lane, 64) < 16, pltpu.roll(v, 112, 1), pltpu.roll(v, 16, 1))
    return v * cos + swapped * (sign * sin)


def pack_body(*refs):
    ins, (w_ref, vec_ref, a_ref, b_ref), scr, sem = refs[:11], refs[11:15], refs[15:25], refs[25]
    copies = [pltpu.make_async_copy(ins[k], scr[k], sem.at[k]) for k in range(10)]
    copies += [
        pltpu.make_async_copy(ins[10].at[:, k * WIDE : (k + 1) * WIDE], ref, sem.at[10 + k])
        for k, ref in enumerate((a_ref, b_ref))
    ]
    for copy in copies:
        copy.start()
    for copy in copies[:10]:
        copy.wait()
    wq_ref, w1_ref, wo_ref, w2_ref = scr[:4]
    low = lax.broadcasted_iota(jnp.int32, (PIECE, 128), 1) < 64
    g0, g1, g2 = [wq_ref[:, k * 128 : (k + 1) * 128].astype(F32) for k in range(3)]
    w_ref[0, 0:256, :128] = jnp.where(low, g0, g1).astype(BF)
    w_ref[0, 0:256, 128:] = pltpu.roll(jnp.where(low, g2, g0), 64, 1).astype(BF)
    w_ref[0, 256:512, :128] = jnp.where(low, g1, g2).astype(BF)
    w_ref[0, 256:512, 128:] = w1_ref[:, :128]
    w_ref[0, 512:768] = w1_ref[:, 128:384]
    w_ref[1, 0:128, :128] = w1_ref[:128, 384:]
    w_ref[1, 0:128, 128:] = w1_ref[128:, 384:]
    w_ref[1, 128:256] = wo_ref[...]
    w_ref[1, 256:768] = w2_ref[...]
    for k, ref in enumerate(scr[4:]):
        vec_ref[k : k + 1, : ref.shape[1]] = ref[...].astype(F32)
    for copy in copies[10:]:
        copy.wait()


def pack(*arrays):
    flat = [a if a.ndim == 2 else a[None, :] for a in arrays]
    return pl.pallas_call(
        pack_body,
        in_specs=[ANY] * 11,
        out_specs=[VM, VM, VM, VM],
        out_shape=[
            jax.ShapeDtypeStruct((2, 768, PIECE), BF),
            jax.ShapeDtypeStruct((8, 128), F32),
            jax.ShapeDtypeStruct((TOK, WIDE), BF),
            jax.ShapeDtypeStruct((TOK, WIDE), BF),
        ],
        scratch_shapes=[pltpu.VMEM(a.shape, BF) for a in flat[:10]] + [pltpu.SemaphoreType.DMA((12,))],
        cost_estimate=SMALL,
        compiler_params=pltpu.CompilerParams(vmem_limit_bytes=58 * 2**20),
        name="pack",
    )(*flat)


def document_start(starts_ref, token):
    first = jnp.zeros(token.shape, jnp.int32)
    for n in range(starts_ref.shape[1]):
        begin = starts_ref[0, n]
        first = jnp.where(token >= begin, begin, first)
    return first


def angles_body(starts_ref, table_ref, start_ref, bounds_ref):
    block = pl.program_id(0)

    @pl.when(block == 0)
    def _():
        for i in range(LEN // ROWS):
            for k, token in enumerate((i * ROWS, (i + 1) * ROWS - 1)):
                begin = jnp.int32(0)
                for n in range(starts_ref.shape[1]):
                    begin = jnp.where(starts_ref[0, n] <= token, starts_ref[0, n], begin)
                bounds_ref[k * (LEN // ROWS) + i] = lax.div(begin + k * (AK - 1), AK)

    shape = (ROWS, 128)
    token = block * ROWS + lax.broadcasted_iota(jnp.int32, shape, 0)
    wide = lax.broadcasted_iota(jnp.int32, shape, 1)
    lane = lax.rem(wide, 64)
    freq = jnp.exp(lax.rem(lane, 16).astype(F32) * (-2.0 * math.log(10000.0) / 32))
    phase = (token - document_start(starts_ref, token)).astype(F32) * freq
    sin = jnp.sin(phase)
    cos = jnp.where(lane < 32, jnp.cos(phase), 1.0)
    sin = jnp.where(lane < 16, -sin, jnp.where(lane < 32, sin, 0.0))
    table_ref[...] = jnp.where(wide < 64, cos, sin)
    here = block * ROWS + lax.broadcasted_iota(jnp.int32, (1, ROWS), 1)
    start_ref[...] = document_start(starts_ref, here)


def angles(starts):
    return pl.pallas_call(
        angles_body,
        grid=(LEN // ROWS,),
        in_specs=[SM],
        out_specs=[rows_of(128), pl.BlockSpec((1, ROWS), lambda i: (0, i)), SM],
        out_shape=[
            jax.ShapeDtypeStruct((LEN, 128), F32),
            jax.ShapeDtypeStruct((1, LEN), jnp.int32),
            jax.ShapeDtypeStruct((2 * (LEN // ROWS),), jnp.int32),
        ],
        cost_estimate=SMALL,
        compiler_params=params(58),
        name="angles",
    )(starts)


def unpack_last(w_ref, last_ref):
    for f in range(FS):
        for k in range(2):
            at = f * PIECE + k * 128
            last_ref[at : at + 128, :] = w_ref[f, 0, :, k * 128 : (k + 1) * 128]


W_FIRST = pl.BlockSpec((FS, 1, 768, PIECE), lambda *_: (0, 0, 0, 0))
W_LAST = pl.BlockSpec((FS, 1, 128, PIECE), lambda *_: (0, 1, 0, 0))
WIDTHS = (D, QKV, HID, HID)


ORDER = (0, 1, 3, 2)


ORDER = (0, 1, 3, 2)


def turn_of(i):
    return jnp.where(i == 3, 2, jnp.where(i == 2, 3, i))


def project_body(
    place_ref, a0_ref, a1_ref, a2_ref, a3_ref, a4_ref, b0_ref, b1_ref, b2_ref, b3_ref, b4_ref,
    gain_ref, bias_ref, w_ref, wl_ref, b_ref, table_ref,
    normed_ref, qkv_ref, act_ref, slope_ref, last_ref, x_scr, sem,
):
    step = pl.program_id(0)
    slot = lax.rem(step, 2)
    a_refs = ((a0_ref,), (a1_ref,), (a2_ref, a3_ref), (a4_ref,))

    def fetch(k, start):
        scr, sems = x_scr.at[k % 2], sem.at[k % 2]
        z_at = lax.rem(place_ref[0] + ORDER[k], 4)

        def go(src, dst, t):
            copy = pltpu.make_async_copy(src, dst, sems.at[t])
            copy.start() if start else copy.wait()

        at = 0
        for t, ref in enumerate(a_refs[ORDER[k]]):
            n = ref.shape[0]
            go(ref, scr.at[at : at + n, :, :WIDE], t)
            at += n
        for x_off, ref in ((0, b0_ref), (1, b1_ref), (3, b4_ref)):
            go(ref.at[z_at], scr.at[lax.rem(place_ref[1] + x_off, 4), :, WIDE:], 2 + x_off)
        far = scr.at[lax.rem(place_ref[1] + 2, 4), :, WIDE:]

        @pl.when(z_at < 2)
        def _():
            go(b2_ref.at[z_at], far, 4)

        @pl.when(z_at >= 2)
        def _():
            go(b3_ref.at[z_at - 2], far, 4)

    for k in range(4):

        @pl.when(step == k)
        def _():
            if k == 0:
                fetch(0, True)
            if k < 3:
                fetch(k + 1, True)
            fetch(k, False)

    @pl.when(pl.program_id(0) == 0)
    def _():
        unpack_last(wl_ref, last_ref)

    x = x_scr[slot].reshape(ROWS, D).astype(F32)
    centered = x - jnp.mean(x, axis=1, keepdims=True)
    inv = lax.rsqrt(jnp.mean(centered * centered, axis=1, keepdims=True) + EPS)
    normed_ref[...] = (centered * inv * gain_ref[...] + bias_ref[...]).astype(BF)

    def group(j):
        normed = normed_ref[...]
        if j == 3:
            return jnp.dot(normed, last_ref[...], preferred_element_type=F32) + b_ref[:, 768:]
        w = w_ref[:, 0, j * 256 : (j + 1) * 256].reshape(D, PIECE)
        return jnp.dot(normed, w, preferred_element_type=F32) + b_ref[:, j * 256 : (j + 1) * 256]

    table = table_ref[...]

    def hidden(h, cols):
        k0 = math.sqrt(2.0 / math.pi)
        h2 = h * h
        t = jnp.tanh(h * (k0 + (k0 * 0.044715) * h2))
        act_ref[:, cols] = (0.5 * h * (1.0 + t)).astype(BF)
        slope = 0.5 * (1.0 + t) + 0.5 * h * (1.0 - t * t) * (k0 + (3 * 0.044715 * k0) * h2)
        slope_ref[:, cols] = slope.astype(BF)

    qk = group(0).astype(BF).astype(F32)
    qkv_ref[:, 0:128] = (turn(qk[:, :128], table) * 0.125).astype(BF)
    qkv_ref[:, 128:256] = turn(qk[:, 128:], table).astype(BF)
    vh = group(1)
    qkv_ref[:, 256:384] = vh[:, :128].astype(BF)
    hidden(vh[:, 128:], slice(0, 128))
    hidden(group(2), slice(128, 384))
    hidden(group(3), slice(384, 512))


def turned_rows(width):
    return pl.BlockSpec((ROWS, width), lambda i, place: (lax.rem(place[0] + turn_of(i), 4), 0))


def project(place, x_a, x_b, gain, bias, w, b, table):
    return pl.pallas_call(
        project_body,
        grid_spec=pltpu.PrefetchScalarGridSpec(
            num_scalar_prefetch=1,
            grid=(4,),
            in_specs=[HBM] * 10
            + [whole((1, D)), whole((1, D)), W_FIRST, W_LAST, whole((1, QKV + HID)), turned_rows(128)],
            out_specs=[turned_rows(D), turned_rows(QKV), turned_rows(HID), turned_rows(HID)],
            scratch_shapes=[
                pltpu.VMEM((D, 128), BF),
                pltpu.VMEM((2, 4, TOK, D), BF),
                pltpu.SemaphoreType.DMA((2, 6)),
            ],
        ),
        out_shape=[jax.ShapeDtypeStruct((LEN, width), BF) for width in (D, QKV, HID, HID)],
        cost_estimate=LARGE,
        compiler_params=params(34),
        name="project",
    )(place, *map(in_hbm, (*x_a, *x_b)), gain, bias, w, w, b, in_hbm(table))


AQ = 512
AK = 256
NQ = LEN // AQ


def padded_turned(ref, scr):
    row = lax.broadcasted_iota(jnp.int32, (128, AQ), 0)
    for i in range(NQ):
        cols = slice(i * AQ, (i + 1) * AQ)
        t = ref[cols, :].astype(F32).T
        scr[0, :, cols] = jnp.where(row < 64, t, 0.0).astype(BF)
        scr[1, :, cols] = jnp.where(row < 64, 0.0, t).astype(BF)


def padded(ref, scr):
    lane = lax.broadcasted_iota(jnp.int32, (AQ, 128), 1)
    for i in range(NQ):
        rows = slice(i * AQ, (i + 1) * AQ)
        v = ref[rows, :].astype(F32)
        scr[0, rows, :] = jnp.where(lane < 64, v, 0.0).astype(BF)
        scr[1, rows, :] = jnp.where(lane < 64, 0.0, v).astype(BF)


def fold(op, v):
    return op(v.reshape(AK // 8, 8, v.shape[1]), axis=0)


def key_bounds(bounds_ref, i):
    low = bounds_ref[i]
    return low, jnp.clip(bounds_ref[NQ + i], low, 2 * i)


def right_half(old, new):
    return jnp.concatenate([old[:, :AK], new], axis=1)


def attend_body(first_ref, qkv_ref, start_ref, att_ref, lse_ref, qt_scr, vt_scr, s_scr):
    padded_turned(qkv_ref.at[:, 0:128], qt_scr)
    for i in range(NQ):
        rows = slice(i * AQ, (i + 1) * AQ)
        vt_scr[:, rows] = qkv_ref[rows, 256:384].astype(F32).T.astype(BF)
    row = lax.broadcasted_iota(jnp.int32, (AK, AQ), 0)
    col = lax.broadcasted_iota(jnp.int32, (AK, AQ), 1)

    def q_block(i, _):
        cols = pl.ds(pl.multiple_of(i * AQ, AQ), AQ)
        start = start_ref[:, cols]
        qt = [qt_scr[h, :, cols] for h in range(2)]

        def scores(j, ok, peaks):
            rows = pl.ds(pl.multiple_of(j * AK, AK), AK)
            k = qkv_ref[rows, 128:256]
            new = []
            for h in range(2):
                s = jnp.dot(k, qt[h], preferred_element_type=F32)
                if ok is not None:
                    s = jnp.where(ok, s, NEG)
                s_scr[h, rows, :] = s
                new.append(jnp.maximum(peaks[h], fold(jnp.max, s)))
            return tuple(new)

        low, mid = key_bounds(first_ref, i)
        peaks = (jnp.full((8, AQ), NEG, F32),) * 2
        peaks = scores(2 * i, (row + 2 * i * AK >= start) & (row <= col), peaks)
        last = pl.ds(pl.multiple_of((2 * i + 1) * AK, AK), AK)
        corner = (row[:, :AK] + (2 * i + 1) * AK >= start[:, AK:]) & (row[:, :AK] <= col[:, :AK])
        new = []
        for h in range(2):
            s = jnp.dot(qkv_ref[last, 128:256], qt[h][:, AK:], preferred_element_type=F32)
            s = jnp.where(corner, s, NEG)
            s_scr[h, last, AK:] = s
            new.append(right_half(peaks[h], jnp.maximum(peaks[h][:, AK:], fold(jnp.max, s))))
        peaks = lax.fori_loop(low, mid, lambda j, p: scores(j, row + j * AK >= start, p), tuple(new))
        peaks = lax.fori_loop(mid, 2 * i, lambda j, p: scores(j, None, p), peaks)
        peak = [jnp.max(p, axis=0, keepdims=True) for p in peaks]

        def values(j, state):
            rows = pl.ds(pl.multiple_of(j * AK, AK), AK)
            new = []
            for h in range(2):
                total, o = state[2 * h : 2 * h + 2]
                p = jnp.exp(s_scr[h, rows, :] - peak[h])
                total = total + fold(jnp.sum, p)
                o = o + jnp.dot(
                    vt_scr[64 * h : 64 * h + 64, rows], p.astype(BF), preferred_element_type=F32
                )
                new += [total, o]
            return tuple(new)

        state = (jnp.zeros((8, AQ), F32), jnp.zeros((64, AQ), F32)) * 2
        state = list(lax.fori_loop(low, 2 * i + 1, values, state))
        for h in range(2):
            total, o = state[2 * h : 2 * h + 2]
            p = jnp.exp(s_scr[h, last, AK:] - peak[h][:, AK:])
            more = jnp.dot(vt_scr[64 * h : 64 * h + 64, last], p.astype(BF), preferred_element_type=F32)
            state[2 * h] = right_half(total, total[:, AK:] + fold(jnp.sum, p))
            state[2 * h + 1] = right_half(o, o[:, AK:] + more)
        total = [jnp.sum(state[2 * h], axis=0, keepdims=True) for h in range(2)]
        both = jnp.concatenate([state[1] / total[0], state[3] / total[1]], axis=0)
        att_ref[cols, :] = both.T.astype(BF)
        for h in range(2):
            lse_ref[h : h + 1, cols] = peak[h] + jnp.log(total[h])
        return 0

    lax.fori_loop(0, NQ, q_block, 0)


def attend(first, qkv, start):
    return pl.pallas_call(
        attend_body,
        in_specs=[SM, VM, VM],
        out_specs=[VM, VM],
        out_shape=[
            jax.ShapeDtypeStruct((LEN, ATT), BF),
            jax.ShapeDtypeStruct((2, LEN), F32),
        ],
        scratch_shapes=[
            pltpu.VMEM((2, 128, LEN), BF),
            pltpu.VMEM((128, LEN), BF),
            pltpu.VMEM((2, LEN, AQ), F32),
        ],
        cost_estimate=LARGE,
        compiler_params=pltpu.CompilerParams(vmem_limit_bytes=24 * 2**20),
        name="attend",
    )(first, qkv, start)


def attend_back_body(
    first_ref, qkv_ref, att_ref, ga_ref, lse_ref, start_ref, table_ref,
    gqkv_ref, bsum_ref,
    q_scr, go_scr, qt_scr, got_scr, kt_scr, dl_scr, dk_scr, dv_scr,
):
    padded(qkv_ref.at[:, 0:128], q_scr)
    padded(ga_ref, go_scr)
    padded_turned(qkv_ref.at[:, 0:128], qt_scr)
    for i in range(NQ):
        rows = slice(i * AQ, (i + 1) * AQ)
        kt_scr[:, rows] = qkv_ref[rows, 128:256].astype(F32).T.astype(BF)
        got = ga_ref[rows, :].astype(F32).T
        prod = got * att_ref[rows, :].astype(F32).T
        row = lax.broadcasted_iota(jnp.int32, (128, AQ), 0)
        got_scr[0, :, rows] = jnp.where(row < 64, got, 0.0).astype(BF)
        got_scr[1, :, rows] = jnp.where(row < 64, 0.0, got).astype(BF)
        for h in range(2):
            dl_scr[h : h + 1, rows] = jnp.sum(prod[64 * h : 64 * h + 64], axis=0, keepdims=True)
    dk_scr[...] = jnp.zeros_like(dk_scr)
    dv_scr[...] = jnp.zeros_like(dv_scr)
    row = lax.broadcasted_iota(jnp.int32, (AK, AQ), 0)
    col = lax.broadcasted_iota(jnp.int32, (AK, AQ), 1)

    def q_block(i, bsum):
        cols = pl.ds(pl.multiple_of(i * AQ, AQ), AQ)
        start = start_ref[:, cols]
        lse = [lse_ref[h : h + 1, cols] for h in range(2)]
        dl = [dl_scr[h : h + 1, cols] for h in range(2)]

        def pair(j, ok, dq, half=False):
            rows = pl.ds(pl.multiple_of(j * AK, AK), AK)
            mine = pl.ds(pl.multiple_of(i * AQ + AK, AK), AK) if half else cols
            part = slice(AK, None) if half else slice(None)
            k = qkv_ref[rows, 128:256]
            v = qkv_ref[rows, 256:384]
            dv = dk = 0.0
            new = []
            for h in range(2):
                s = jnp.dot(k, qt_scr[h, :, mine], preferred_element_type=F32)
                dp = jnp.dot(v, got_scr[h, :, mine], preferred_element_type=F32)
                p = jnp.exp(s - lse[h][:, part])
                if ok is not None:
                    p = jnp.where(ok, p, 0.0)
                ds = (p * (dp - dl[h][:, part])).astype(BF)
                dv += jnp.dot(p.astype(BF), go_scr[h, mine, :], preferred_element_type=F32)
                dk += jnp.dot(ds, q_scr[h, mine, :], preferred_element_type=F32)
                more = jnp.dot(kt_scr[64 * h : 64 * h + 64, rows], ds, preferred_element_type=F32)
                new.append(right_half(dq[h], dq[h][:, AK:] + more) if half else dq[h] + more)
            dv_scr[rows, :] += dv
            dk_scr[rows, :] += dk
            return tuple(new)

        low, mid = key_bounds(first_ref, i)
        dq = (jnp.zeros((64, AQ), F32),) * 2
        dq = pair(2 * i, (row + 2 * i * AK >= start) & (row <= col), dq)
        corner = (row[:, :AK] + (2 * i + 1) * AK >= start[:, AK:]) & (row[:, :AK] <= col[:, :AK])
        dq = pair(2 * i + 1, corner, dq, half=True)
        dq = lax.fori_loop(low, mid, lambda j, dq: pair(j, row + j * AK >= start, dq), dq)
        dq = lax.fori_loop(mid, 2 * i, lambda j, dq: pair(j, None, dq), dq)
        dq = (jnp.concatenate(dq, axis=0) * 0.125).T
        out = turn(dq, table_ref[cols, :], -1.0).astype(BF)
        gqkv_ref[cols, 0:128] = out
        return bsum + jnp.sum(out.astype(F32), axis=0, keepdims=True)

    bsum_ref[:, 0:128] = lax.fori_loop(0, NQ, q_block, jnp.zeros((1, 128), F32))

    def finish(i, total):
        rows = pl.ds(pl.multiple_of(i * AQ, AQ), AQ)
        dk = turn(dk_scr[rows, :], table_ref[rows, :], -1.0)
        out = jnp.concatenate([dk, dv_scr[rows, :]], axis=1).astype(BF)
        gqkv_ref[rows, 128:384] = out
        return total + jnp.sum(out.astype(F32), axis=0, keepdims=True)

    bsum_ref[:, 128:384] = lax.fori_loop(0, NQ, finish, jnp.zeros((1, 256), F32))


def attend_back(first, qkv, att, ga, lse, start, table):
    return pl.pallas_call(
        attend_back_body,
        in_specs=[SM] + [VM] * 6,
        out_specs=[VM, VM],
        out_shape=[
            jax.ShapeDtypeStruct((LEN, QKV), BF),
            jax.ShapeDtypeStruct((1, QKV), F32),
        ],
        scratch_shapes=[
            pltpu.VMEM((2, LEN, 128), BF),
            pltpu.VMEM((2, LEN, 128), BF),
            pltpu.VMEM((2, 128, LEN), BF),
            pltpu.VMEM((2, 128, LEN), BF),
            pltpu.VMEM((128, LEN), BF),
            pltpu.VMEM((2, LEN), F32),
            pltpu.VMEM((LEN, 128), F32),
            pltpu.VMEM((LEN, 128), F32),
        ],
        cost_estimate=LARGE,
        compiler_params=pltpu.CompilerParams(vmem_limit_bytes=24 * 2**20),
        name="attend_back",
    )(first, qkv, att, ga, lse, start, table)


def emit_body(att_ref, act_ref, w_ref, out_ref):
    both = jnp.concatenate([att_ref[...], act_ref[...]], axis=1)
    for f in range(FS):
        out_ref[:, f * PIECE : (f + 1) * PIECE] = jnp.dot(
            both, w_ref[f, 0, 128:], preferred_element_type=F32
        ).astype(BF)


def emit(att, act, w):
    return pl.pallas_call(
        emit_body,
        grid=(LEN // ROWS,),
        in_specs=[rows_of(ATT), rows_of(HID), pl.BlockSpec((FS, 1, 768, PIECE), lambda i, *_: (0, 1, 0, 0))],
        out_specs=rows_of(D),
        out_shape=pltpu.HBM((LEN, D), BF),
        cost_estimate=LARGE,
        compiler_params=params(24),
        name="emit",
    )(att, act, w)


def emit_back_body(g_ref, w_ref, slope_ref, ga_ref, gh_ref, bsum_ref):
    total = jnp.zeros((ROWS, ATT + HID), F32)
    for f in range(FS):
        total += lax.dot_general(
            g_ref[:, f * PIECE : (f + 1) * PIECE], w_ref[f, 0, 128:], (((1,), (1,)), ((), ())),
            preferred_element_type=F32,
        )
    ga_ref[...] = total[:, :ATT].astype(BF)
    gh = (total[:, ATT:] * slope_ref[...].astype(F32)).astype(BF)
    gh_ref[...] = gh

    @pl.when(pl.program_id(0) == 0)
    def _():
        bsum_ref[...] = jnp.zeros_like(bsum_ref)

    bsum_ref[...] += jnp.sum(gh.astype(F32), axis=0, keepdims=True)


def emit_back(g, w, slope):
    return pl.pallas_call(
        emit_back_body,
        grid=(LEN // ROWS,),
        in_specs=[rows_of(D), pl.BlockSpec((FS, 1, 768, PIECE), lambda i: (0, 1, 0, 0)), rows_of(HID)],
        out_specs=[rows_of(ATT), rows_of(HID), whole((1, HID))],
        out_shape=[
            jax.ShapeDtypeStruct((LEN, ATT), BF),
            jax.ShapeDtypeStruct((LEN, HID), BF),
            jax.ShapeDtypeStruct((1, HID), F32),
        ],
        cost_estimate=LARGE,
        compiler_params=params(26),
        name="emit_back",
    )(in_hbm(g), in_hbm(w), slope)


ALLW = QKV + ATT + 2 * HID
EXTRA = 16


def weight_grads_body(att_ref, act_ref, gh_ref, gqkv_ref, g_ref, normed_ref, out_ref, turned):
    @pl.when(pl.program_id(0) == 0)
    def _():
        for block in range(8):
            rows = slice(block * PIECE, (block + 1) * PIECE)
            at = 0
            for ref, n in ((att_ref, ATT), (act_ref, HID), (gh_ref, HID), (gqkv_ref, QKV)):
                turned[at : at + n, rows] = ref[rows, :].T
                at += n

    cut = ATT + HID
    out_ref[0, :cut] = jnp.dot(turned[:cut], g_ref[...], preferred_element_type=F32).astype(BF)
    out_ref[0, cut:ALLW] = jnp.dot(turned[cut:], normed_ref[...], preferred_element_type=F32).astype(BF)
    out_ref[0, ALLW:] = jnp.zeros((EXTRA, PIECE), BF)


def column_piece():
    return pl.BlockSpec((LEN, PIECE), lambda i: (0, i))


def weight_grads(att, act, gh, gqkv, g, normed):
    return pl.pallas_call(
        weight_grads_body,
        grid=(FS,),
        in_specs=[
            whole((LEN, ATT)), whole((LEN, HID)), whole((LEN, HID)), whole((LEN, QKV)),
            column_piece(), column_piece(),
        ],
        out_specs=pl.BlockSpec((1, ALLW + EXTRA, PIECE), lambda i: (i, 0, 0)),
        scratch_shapes=[pltpu.VMEM((ALLW, LEN), BF)],
        out_shape=pltpu.HBM((FS, ALLW + EXTRA, PIECE), BF),
        cost_estimate=LARGE,
        compiler_params=params(34),
        name="weight_grads",
    )(att, act, gh, gqkv, in_hbm(g), in_hbm(normed))


def unpack_body(sums_ref, qkv_ref, out_ref, fc1_ref, fc2_ref, small_ref):
    out_ref[...] = sums_ref[0, :ATT].astype(F32)
    fc2_ref[...] = sums_ref[0, ATT : ATT + HID].astype(F32)
    fc1_ref[...] = sums_ref[0, ATT + HID : ATT + 2 * HID].astype(F32).T
    at = ATT + 2 * HID
    q, k, v = [sums_ref[0, at + n * 128 : at + (n + 1) * 128].astype(F32).T for n in range(3)]
    low = lax.broadcasted_iota(jnp.int32, (PIECE, 128), 1) < 64
    qkv_ref[:, 0:128] = jnp.where(low, q, pltpu.roll(k, 64, 1))
    qkv_ref[:, 128:256] = jnp.where(low, v, q)
    qkv_ref[:, 256:384] = jnp.where(low, pltpu.roll(k, 64, 1), v)
    small_ref[...] = sums_ref[0, ALLW:].astype(F32)


def unpack(sums):
    shapes = [(PIECE, QKV), (ATT, PIECE), (PIECE, HID), (HID, PIECE), (EXTRA, PIECE)]
    return pl.pallas_call(
        unpack_body,
        in_specs=[VM],
        out_specs=[VM] * 5,
        out_shape=[jax.ShapeDtypeStruct(shape, F32) for shape in shapes],
        cost_estimate=SMALL,
        compiler_params=pltpu.CompilerParams(vmem_limit_bytes=16 * 2**20),
        name="unpack",
    )(sums)


def block_of(pairs, step, side):
    block = jnp.int32(pairs[0][side])
    for k in range(1, len(pairs)):
        block = jnp.where(step == k, pairs[k][side], block)
    return block


def input_back_body(pairs, place_ref, gqkv_ref, gh_ref, w_ref, wl_ref, *refs):
    step = pl.program_id(0)
    normed_refs, refs = refs[:8], refs[8:]
    sums_ref, last_ref, out_scr = refs[-3:]
    far = len(pairs) == 1
    got_refs, out_refs = ((), refs[:-3]) if far else (refs[:4], refs[4:-3])
    blocks = [block_of(pairs, step, side) for side in range(2)]

    def pieces(ref):
        return jnp.concatenate([gather_pieces(place_ref, ref, block) for block in blocks], axis=0)

    both = jnp.concatenate([pieces(gqkv_ref), pieces(gh_ref)], axis=1)

    @pl.when(step == 0)
    def _():
        sums_ref[...] = jnp.zeros_like(sums_ref)
        unpack_last(wl_ref, last_ref)

    turned = (((1,), (1,)), ((), ()))
    for f in range(FS):
        cols = slice(f * PIECE, (f + 1) * PIECE)
        part = lax.dot_general(both[:, 768:], last_ref[cols, :], turned, preferred_element_type=F32)
        for j in range(3):
            part += lax.dot_general(
                both[:, j * 256 : (j + 1) * 256], w_ref[f, 0, j * 256 : (j + 1) * 256], turned,
                preferred_element_type=F32,
            )
        out_scr[:, cols] = part
        normed = jnp.concatenate([ref[0, 0, :, cols] for ref in normed_refs], axis=0).astype(F32)
        sums_ref[0:1, cols] += jnp.sum(part, axis=0, keepdims=True)
        sums_ref[1:2, cols] += jnp.sum(part * normed, axis=0, keepdims=True)
    if far:
        for k in range(4):
            out_refs[k][...] = out_scr[k * 128 : (k + 1) * 128, :].astype(BF)
        return
    for k in range(3):

        @pl.when(step == k)
        def _():
            for side in range(2):
                for part in range(2):
                    at = side * PIECE + part * 128
                    v = out_scr[at : at + 128, :]
                    if k == part:
                        v += got_refs[2 * side + part][...].astype(F32)
                    out_refs[2 * k + side][part * 128 : (part + 1) * 128, :] = v.astype(BF)


def piece_spec(pairs, m):
    def where_to(i, place_ref):
        start = piece_start(place_ref, block_of(pairs, i, m // 4), m % 4)
        return (start // TOK, m // 4, 0, 0)

    return pl.BlockSpec((1, 1, HALF, D), where_to)


def input_back(pairs, place, gqkv, gh, w, normed, got=()):
    n = len(pairs)
    outs = [(128, D)] * 4 if n == 1 else [(PIECE, D)] * 6
    return pl.pallas_call(
        functools.partial(input_back_body, pairs),
        grid_spec=pltpu.PrefetchScalarGridSpec(
            num_scalar_prefetch=1,
            grid=(n,),
            in_specs=[whole((LEN, QKV)), whole((LEN, HID)), W_FIRST, W_LAST]
            + [piece_spec(pairs, m) for m in range(8)]
            + [whole((128, D))] * len(got),
            out_specs=[whole(shape) for shape in outs] + [whole((2, D))],
            scratch_shapes=[pltpu.VMEM((D, 128), BF), pltpu.VMEM((2 * PIECE, D), F32)],
        ),
        out_shape=[pltpu.HBM(shape, BF) for shape in outs] + [jax.ShapeDtypeStruct((2, D), F32)],
        cost_estimate=LARGE,
        compiler_params=params(44),
        name="input_back",
    )(place, gqkv, gh, in_hbm(w), in_hbm(w), *[in_hbm(normed.reshape(16, 2, HALF, D))] * 8, *got)


def copy_body(moves, n_in, in_hbm_out, place_ref, *refs):
    n_out = len(refs) - n_in - 1
    if in_hbm_out:
        n_out //= 2
    ins, outs, sem = refs[:n_in], refs[n_in : n_in + n_out], refs[-1]
    to = refs[n_in + n_out : -1] if in_hbm_out else outs
    copies = [
        pltpu.make_async_copy(src(ins), dst(to, place_ref), sem.at[k]) for k, (src, dst) in enumerate(moves)
    ]
    for copy in copies:
        copy.start()
    for copy in copies:
        copy.wait()
    if in_hbm_out:
        copies = [pltpu.make_async_copy(scr, out, sem.at[k]) for k, (scr, out) in enumerate(zip(to, outs))]
        for copy in copies:
            copy.start()
        for copy in copies:
            copy.wait()


def copy_kernel(name, moves, place, ins, out_shapes, in_hbm_out=False):
    n = len(out_shapes)
    return pl.pallas_call(
        functools.partial(copy_body, moves, len(ins), in_hbm_out),
        in_specs=[SM] + [HBM if in_hbm_out else ANY] * len(ins),
        out_specs=[HBM if in_hbm_out else VM] * n,
        out_shape=[jax.ShapeDtypeStruct(shape, BF) for shape in out_shapes],
        scratch_shapes=[pltpu.VMEM(shape, BF) for shape in out_shapes if in_hbm_out]
        + [pltpu.SemaphoreType.DMA((len(moves),))],
        cost_estimate=SMALL,
        compiler_params=pltpu.CompilerParams(vmem_limit_bytes=58 * 2**20),
        name=name,
    )(place, *(map(in_hbm, ins) if in_hbm_out else ins))


def join(place, pieces_a, pieces_b):
    def move(k):
        axis = 1 - k // 4
        return (
            lambda ins: ins[k],
            lambda outs, place_ref: outs[k // 4].at[lax.rem(place_ref[axis] + k % 4, 4)],
        )

    moves = [move(k) for k in range(8)]
    return copy_kernel("join", moves, place, [*pieces_a, *pieces_b], [(4, TOK, WIDE)] * 2, True)


def halves(place, left_a, right_a, left_b, right_b):
    def move(k):
        spot = slice(k % 2 * 2, k % 2 * 2 + 2)
        return (lambda ins: ins[k].at[spot], lambda outs, place_ref: outs[k])

    moves = [move(k) for k in range(4)]
    return copy_kernel("halves", moves, place, [left_a, right_a, left_b, right_b], [(2, TOK, WIDE)] * 4, True)


def shift(v, axis, by, n=4):
    return lax.ppermute(v, axis, [(i, (i + by) % n) for i in range(n)])


def in_hbm(v):
    return pltpu.with_memory_space_constraint(v, pltpu.HBM)


def tie(v, *others):
    return lax.optimization_barrier((v,) + others)[0]


def plus(a, b):
    return (a.astype(F32) + b.astype(F32)).astype(BF)


def near_sum(own, right, left, axis):
    return own.astype(F32) + shift(right, axis, 1).astype(F32) + shift(left, axis, -1).astype(F32)


def ring_sum_first(parts, axis):
    own, right, far, left = parts
    got = [shift(far, axis, 2), shift(right, axis, 1), shift(left, axis, -1)]
    total = own.astype(F32)
    for v in got:
        total = total + v.astype(F32)
    return total, got[1]


def ring_sum(parts, axis):
    return ring_sum_first(parts, axis)[0]


def quarters(v):
    n = v.shape[0] // 4
    return [v[i * n : (i + 1) * n] for i in range(4)]


def small_gather(v, axes):
    for axis in axes:
        n = 2 if axis == "core" else 4
        me = lax.axis_index(axis)
        out = jnp.zeros((n,) + v.shape, v.dtype)
        out = lax.dynamic_update_index_in_dim(out, v, me, 0)
        for by in range(1, n):
            got = shift(v, axis, by, n)
            out = lax.dynamic_update_index_in_dim(out, got, lax.rem(me + n - by, n), 0)
        v = out
    return v


def small_sum(v, axes):
    for axis, n, dim in axes:
        me = lax.axis_index(axis)
        total = lax.dynamic_index_in_dim(v, me, dim, keepdims=False)
        for by in range(1, n):
            part = lax.dynamic_index_in_dim(v, lax.rem(me + by, n), dim, keepdims=False)
            total = total + shift(part, axis, by, n)
        v = total
    return v


def on_device(
    tokens, cotangent, doc_starts, ln_gain, ln_bias, w_qkv, b_qkv, w_out, b_out, w_fc1, b_fc1, w_fc2, b_fc2,
):
    own = tokens[0]
    own_grad = cotangent[0]
    z_me, x_me = lax.axis_index("z"), lax.axis_index("x")
    seq = z_me * 4 + x_me
    place = jnp.stack([z_me, x_me, lax.axis_index("core"), lax.axis_index("y")]).astype(jnp.int32)

    fsdp = ("y", "core")
    w, vectors, own_a, own_b = pack(
        w_qkv, w_fc1, w_out, w_fc2, ln_gain, ln_bias, b_qkv, b_out, b_fc1, b_fc2, own
    )
    w = lax.all_gather(w, fsdp, axis=0).reshape(FS, 2, 768, PIECE)
    vectors = small_gather(vectors, ("x", "z"))
    vectors, own_a, own_b = lax.optimization_barrier((vectors, own_a, own_b))
    a, b = join(
        place,
        [own_a] + [shift(own_a, "x", -by) for by in (1, 2, 3)],
        [own_b] + [shift(own_b, "z", -by) for by in (1, 2, 3)],
    )
    g = lax.all_gather(tie(own_grad, a), ("z", "x"), axis=0, tiled=True)
    left_a, right_a, left_b, right_b = shift(a, "z", 1), shift(a, "z", -1), shift(b, "x", 1), shift(b, "x", -1)
    far = halves(place, left_a, right_a, left_b, right_b)
    x_a = [a, right_a, shift(far[0], "z", 1), shift(far[1], "z", -1), left_a]
    x_b = [b, right_b, shift(far[2], "x", 1), shift(far[3], "x", -1), left_b]
    vectors = small_gather(vectors, ("y", "core"))
    table, start, first = angles(tie(doc_starts, far[0]))
    vectors = vectors.transpose(1, 0, 2, 3, 4, 5).reshape(128, 8, 128)

    sizes = [16, 16, 48, 16, 64, 16]
    gain, bias, bq, bo, b1, b2 = [vectors[:, k, :n].reshape(1, -1) for k, n in enumerate(sizes)]
    b_in = jnp.concatenate(
        [
            lax.dynamic_slice_in_dim(bq, seq * QKV, QKV, 1).reshape(2, 3, 64).transpose(1, 0, 2).reshape(1, QKV),
            lax.dynamic_slice_in_dim(b1, seq * HID, HID, 1),
        ],
        axis=1,
    )

    normed, qkv, act, slope = project(place, x_a, x_b, gain, bias, w, b_in, table)
    att, lse = attend(first, qkv, start)
    out_part = emit(att, act, w)
    out_sum = lax.psum_scatter(out_part, ("z", "x"), scatter_dimension=0, tiled=True)
    output = (own.astype(F32) + out_sum.astype(F32) + bo + b2).astype(BF)

    ga, gh, b1_sum = emit_back(tie(g, out_part), w, slope)
    gqkv, bq_sum = attend_back(first, qkv, att, ga, lse, start, table)
    bq_sum = bq_sum.reshape(3, 2, 64).transpose(1, 0, 2).reshape(1, QKV)
    far_a0, far_a1, far_b0, far_b1, sums_far = input_back(((2, 6),), place, gqkv, gh, w, normed)
    got = [shift(far_a0, "z", 1), shift(far_a1, "z", -1), shift(far_b0, "x", 1), shift(far_b1, "x", -1)]
    grads = weight_grads(att, act, gh, tie(gqkv, far_a0), g, normed)
    right_a, right_b, left_a, left_b, own_a, own_b, sums = input_back(
        ((1, 5), (3, 7), (0, 4)), place, gqkv, gh, w, tie(normed, grads), got
    )
    sums = sums + sums_far
    wide_grad = own_grad.astype(F32)
    bo_sum = jnp.sum(wide_grad, axis=0, keepdims=True)
    gain_sum = (sums[1:2] - bias * sums[0:1]) / gain
    bq_all = lax.dynamic_update_slice_in_dim(jnp.zeros((1, 16 * QKV), F32), bq_sum, seq * QKV, 1)
    b1_all = lax.dynamic_update_slice_in_dim(jnp.zeros((1, 16 * HID), F32), b1_sum, seq * HID, 1)
    packed = jnp.concatenate(
        [t.reshape(128, -1) for t in (gain_sum, sums[0:1], bq_all, bo_sum, b1_all)], axis=1
    )
    small = small_sum(packed.reshape(4, 2, 4, 4, -1), (("z", 4, 2), ("x", 4, 2)))
    small, right_a, right_b, left_a, left_b = lax.optimization_barrier((small, right_a, right_b, left_a, left_b))
    small = small.reshape(FS, 1, 160).astype(BF)
    grads = lax.dynamic_update_slice(grads, small, (0, ALLW, 0))
    grads = lax.psum_scatter(grads, fsdp, scatter_dimension=0, tiled=True)
    grad_qkv, grad_out, grad_fc1, grad_fc2, small = unpack(grads)
    small = small[0, :160]

    a = near_sum(own_a, right_a, left_a, "z").astype(BF)
    b = near_sum(own_b, right_b, left_b, "x").astype(BF)
    a = ring_sum(quarters(a), "x")
    b = ring_sum(quarters(b), "z")
    dn = jnp.concatenate([a, b], axis=0)
    wide = own.astype(F32)
    centered = wide - jnp.mean(wide, axis=1, keepdims=True)
    inv = lax.rsqrt(jnp.mean(centered * centered, axis=1, keepdims=True) + EPS)
    unit = centered * inv
    e = dn * gain
    input_grad = wide_grad + inv * (
        e - jnp.mean(e, axis=1, keepdims=True) - unit * jnp.mean(e * unit, axis=1, keepdims=True)
    )

    return (
        output[None],
        input_grad[None],
        small[0:16],
        small[16:32],
        grad_qkv,
        small[32:80],
        grad_out,
        small[80:96],
        grad_fc1,
        small[96:160],
        grad_fc2,
        small[80:96],
    )


def solution(mesh):
    split = Mesh(mesh.devices.reshape(4, 2, 4, 4), ("y", "core", "z", "x"))
    f, s = ("y", "core"), ("z", "x")
    both = f + s
    in_specs = (
        P(f, s, None), P(f, s, None), P(f, None), P(both), P(both), P(f, s), P(both), P(s, f), P(both),
        P(f, s), P(both), P(s, f), P(both),
    )
    out_specs = (
        P(f, s, None), P(f, s, None), P(both), P(both), P(f, s), P(both), P(s, f), P(both), P(f, s),
        P(both), P(s, f), P(both),
    )
    return jax.shard_map(on_device, mesh=split, in_specs=in_specs, out_specs=out_specs, check_vma=False)
```

```python
import functools
import math

import jax
import jax.numpy as jnp
import numpy as np
from jax import lax
from jax.experimental import pallas as pl
from jax.experimental.pallas import tpu as pltpu
from jax.sharding import Mesh
from jax.sharding import PartitionSpec as P

BF = jnp.bfloat16
F32 = jnp.float32
EPS = 1e-05
D = 2048
LEN = 2048
ROWS = 512
TOK = 128
HALF = 64
WIDE = D // 2
QKV = 384
HID = 512
ATT = 128
PIECE = 256
FS = 8
NEG = -1e30


SMALL = pl.CostEstimate(flops=1, bytes_accessed=1, transcendentals=0)
LARGE = pl.CostEstimate(flops=100 * 2**30, bytes_accessed=320 * 2**20, transcendentals=0)


def params(mib):
    return pltpu.CompilerParams(vmem_limit_bytes=mib * 2**20, dimension_semantics=("arbitrary",))


VM = pl.BlockSpec(memory_space=pltpu.VMEM)
SM = pl.BlockSpec(memory_space=pltpu.SMEM)
ANY = pl.BlockSpec(memory_space=pl.ANY)
HBM = pl.BlockSpec(memory_space=pltpu.HBM)


def whole(shape):
    return pl.BlockSpec(shape, lambda i, *_: (0,) * len(shape))


def rows_of(width):
    return pl.BlockSpec((ROWS, width), lambda i, *_: (i, 0))


def piece_start(place_ref, block, piece):
    first = block < 4
    z_off = jnp.where(first, block, piece)
    x_off = jnp.where(first, piece, block - 4)
    seq = lax.rem(place_ref[0] + z_off, 4) * 4 + lax.rem(place_ref[1] + x_off, 4)
    return pl.multiple_of(seq * TOK + jnp.where(first, 0, HALF), HALF)


def gather_pieces(place_ref, ref, block):
    return jnp.concatenate(
        [ref[pl.ds(piece_start(place_ref, block, s), HALF), :] for s in range(4)], axis=0
    )


def turn(v, table, sign=1.0):
    lane = lax.broadcasted_iota(jnp.int32, v.shape, 1)
    other = pltpu.roll(table, 64, 1)
    cos = jnp.where(lane < 64, table, other)
    sin = jnp.where(lane < 64, other, table)
    swapped = jnp.where(lax.rem(lane, 64) < 16, pltpu.roll(v, 112, 1), pltpu.roll(v, 16, 1))
    return v * cos + swapped * (sign * sin)


def pack_body(*refs):
    ins, (w_ref, vec_ref, a_ref, b_ref), scr, sem = refs[:11], refs[11:15], refs[15:25], refs[25]
    copies = [pltpu.make_async_copy(ins[k], scr[k], sem.at[k]) for k in range(10)]
    copies += [
        pltpu.make_async_copy(ins[10].at[:, k * WIDE : (k + 1) * WIDE], ref, sem.at[10 + k])
        for k, ref in enumerate((a_ref, b_ref))
    ]
    for copy in copies:
        copy.start()
    for copy in copies[:10]:
        copy.wait()
    wq_ref, w1_ref, wo_ref, w2_ref = scr[:4]
    low = lax.broadcasted_iota(jnp.int32, (PIECE, 128), 1) < 64
    g0, g1, g2 = [wq_ref[:, k * 128 : (k + 1) * 128].astype(F32) for k in range(3)]
    w_ref[0, 0:256, :128] = jnp.where(low, g0, g1).astype(BF)
    w_ref[0, 0:256, 128:] = pltpu.roll(jnp.where(low, g2, g0), 64, 1).astype(BF)
    w_ref[0, 256:512, :128] = jnp.where(low, g1, g2).astype(BF)
    w_ref[0, 256:512, 128:] = w1_ref[:, :128]
    w_ref[0, 512:768] = w1_ref[:, 128:384]
    w_ref[1, 0:128, :128] = w1_ref[:128, 384:]
    w_ref[1, 0:128, 128:] = w1_ref[128:, 384:]
    w_ref[1, 128:256] = wo_ref[...]
    w_ref[1, 256:768] = w2_ref[...]
    for k, ref in enumerate(scr[4:]):
        vec_ref[k : k + 1, : ref.shape[1]] = ref[...].astype(F32)
    for copy in copies[10:]:
        copy.wait()


def pack(*arrays):
    flat = [a if a.ndim == 2 else a[None, :] for a in arrays]
    return pl.pallas_call(
        pack_body,
        in_specs=[ANY] * 11,
        out_specs=[VM, VM, VM, VM],
        out_shape=[
            jax.ShapeDtypeStruct((2, 768, PIECE), BF),
            jax.ShapeDtypeStruct((8, 128), F32),
            jax.ShapeDtypeStruct((TOK, WIDE), BF),
            jax.ShapeDtypeStruct((TOK, WIDE), BF),
        ],
        scratch_shapes=[pltpu.VMEM(a.shape, BF) for a in flat[:10]] + [pltpu.SemaphoreType.DMA((12,))],
        cost_estimate=SMALL,
        compiler_params=pltpu.CompilerParams(vmem_limit_bytes=58 * 2**20),
        name="pack",
    )(*flat)


def document_start(starts_ref, token):
    first = jnp.zeros(token.shape, jnp.int32)
    for n in range(starts_ref.shape[1]):
        begin = starts_ref[0, n]
        first = jnp.where(token >= begin, begin, first)
    return first


def angles_body(starts_ref, table_ref, start_ref, bounds_ref):
    block = pl.program_id(0)

    @pl.when(block == 0)
    def _():
        for i in range(LEN // ROWS):
            for k, token in enumerate((i * ROWS, (i + 1) * ROWS - 1)):
                begin = jnp.int32(0)
                for n in range(starts_ref.shape[1]):
                    begin = jnp.where(starts_ref[0, n] <= token, starts_ref[0, n], begin)
                bounds_ref[k * (LEN // ROWS) + i] = lax.div(begin + k * (AK - 1), AK)

    shape = (ROWS, 128)
    token = block * ROWS + lax.broadcasted_iota(jnp.int32, shape, 0)
    wide = lax.broadcasted_iota(jnp.int32, shape, 1)
    lane = lax.rem(wide, 64)
    freq = jnp.exp(lax.rem(lane, 16).astype(F32) * (-2.0 * math.log(10000.0) / 32))
    phase = (token - document_start(starts_ref, token)).astype(F32) * freq
    sin = jnp.sin(phase)
    cos = jnp.where(lane < 32, jnp.cos(phase), 1.0)
    sin = jnp.where(lane < 16, -sin, jnp.where(lane < 32, sin, 0.0))
    table_ref[...] = jnp.where(wide < 64, cos, sin)
    here = block * ROWS + lax.broadcasted_iota(jnp.int32, (1, ROWS), 1)
    start_ref[...] = document_start(starts_ref, here)


def angles(starts):
    return pl.pallas_call(
        angles_body,
        grid=(LEN // ROWS,),
        in_specs=[SM],
        out_specs=[rows_of(128), pl.BlockSpec((1, ROWS), lambda i: (0, i)), SM],
        out_shape=[
            jax.ShapeDtypeStruct((LEN, 128), F32),
            jax.ShapeDtypeStruct((1, LEN), jnp.int32),
            jax.ShapeDtypeStruct((2 * (LEN // ROWS),), jnp.int32),
        ],
        cost_estimate=SMALL,
        compiler_params=params(58),
        name="angles",
    )(starts)


def unpack_last(w_ref, last_ref):
    for f in range(FS):
        for k in range(2):
            at = f * PIECE + k * 128
            last_ref[at : at + 128, :] = w_ref[f, 0, :, k * 128 : (k + 1) * 128]


W_FIRST = pl.BlockSpec((FS, 1, 768, PIECE), lambda *_: (0, 0, 0, 0))
W_LAST = pl.BlockSpec((FS, 1, 128, PIECE), lambda *_: (0, 1, 0, 0))
WIDTHS = (D, QKV, HID, HID)


ORDER = (0, 1, 3, 2)


ORDER = (0, 1, 3, 2)


def turn_of(i):
    return jnp.where(i == 3, 2, jnp.where(i == 2, 3, i))


def project_body(
    place_ref, a0_ref, a1_ref, a2_ref, a3_ref, a4_ref, b0_ref, b1_ref, b2_ref, b3_ref, b4_ref,
    gain_ref, bias_ref, w_ref, wl_ref, b_ref, table_ref,
    normed_ref, qkv_ref, act_ref, slope_ref, last_ref, x_scr, sem,
):
    step = pl.program_id(0)
    slot = lax.rem(step, 2)
    a_refs = ((a0_ref,), (a1_ref,), (a2_ref, a3_ref), (a4_ref,))

    def fetch(k, start):
        scr, sems = x_scr.at[k % 2], sem.at[k % 2]
        z_at = lax.rem(place_ref[0] + ORDER[k], 4)

        def go(src, dst, t):
            copy = pltpu.make_async_copy(src, dst, sems.at[t])
            copy.start() if start else copy.wait()

        at = 0
        for t, ref in enumerate(a_refs[ORDER[k]]):
            n = ref.shape[0]
            go(ref, scr.at[at : at + n, :, :WIDE], t)
            at += n
        for x_off, ref in ((0, b0_ref), (1, b1_ref), (3, b4_ref)):
            go(ref.at[z_at], scr.at[lax.rem(place_ref[1] + x_off, 4), :, WIDE:], 2 + x_off)
        far = scr.at[lax.rem(place_ref[1] + 2, 4), :, WIDE:]

        @pl.when(z_at < 2)
        def _():
            go(b2_ref.at[z_at], far, 4)

        @pl.when(z_at >= 2)
        def _():
            go(b3_ref.at[z_at - 2], far, 4)

    for k in range(4):

        @pl.when(step == k)
        def _():
            if k == 0:
                fetch(0, True)
            if k < 3:
                fetch(k + 1, True)
            fetch(k, False)

    @pl.when(pl.program_id(0) == 0)
    def _():
        unpack_last(wl_ref, last_ref)

    x = x_scr[slot].reshape(ROWS, D).astype(F32)
    centered = x - jnp.mean(x, axis=1, keepdims=True)
    inv = lax.rsqrt(jnp.mean(centered * centered, axis=1, keepdims=True) + EPS)
    normed_ref[...] = (centered * inv * gain_ref[...] + bias_ref[...]).astype(BF)

    def group(j):
        normed = normed_ref[...]
        if j == 3:
            return jnp.dot(normed, last_ref[...], preferred_element_type=F32) + b_ref[:, 768:]
        w = w_ref[:, 0, j * 256 : (j + 1) * 256].reshape(D, PIECE)
        return jnp.dot(normed, w, preferred_element_type=F32) + b_ref[:, j * 256 : (j + 1) * 256]

    table = table_ref[...]

    def hidden(h, cols):
        k0 = math.sqrt(2.0 / math.pi)
        h2 = h * h
        t = jnp.tanh(h * (k0 + (k0 * 0.044715) * h2))
        act_ref[:, cols] = (0.5 * h * (1.0 + t)).astype(BF)
        slope = 0.5 * (1.0 + t) + 0.5 * h * (1.0 - t * t) * (k0 + (3 * 0.044715 * k0) * h2)
        slope_ref[:, cols] = slope.astype(BF)

    qk = group(0).astype(BF).astype(F32)
    qkv_ref[:, 0:128] = (turn(qk[:, :128], table) * 0.125).astype(BF)
    qkv_ref[:, 128:256] = turn(qk[:, 128:], table).astype(BF)
    vh = group(1)
    qkv_ref[:, 256:384] = vh[:, :128].astype(BF)
    hidden(vh[:, 128:], slice(0, 128))
    hidden(group(2), slice(128, 384))
    hidden(group(3), slice(384, 512))


def turned_rows(width):
    return pl.BlockSpec((ROWS, width), lambda i, place: (lax.rem(place[0] + turn_of(i), 4), 0))


def project(place, x_a, x_b, gain, bias, w, b, table):
    return pl.pallas_call(
        project_body,
        grid_spec=pltpu.PrefetchScalarGridSpec(
            num_scalar_prefetch=1,
            grid=(4,),
            in_specs=[HBM] * 10
            + [whole((1, D)), whole((1, D)), W_FIRST, W_LAST, whole((1, QKV + HID)), turned_rows(128)],
            out_specs=[turned_rows(D), turned_rows(QKV), turned_rows(HID), turned_rows(HID)],
            scratch_shapes=[
                pltpu.VMEM((D, 128), BF),
                pltpu.VMEM((2, 4, TOK, D), BF),
                pltpu.SemaphoreType.DMA((2, 6)),
            ],
        ),
        out_shape=[jax.ShapeDtypeStruct((LEN, width), BF) for width in (D, QKV, HID, HID)],
        cost_estimate=LARGE,
        compiler_params=params(34),
        name="project",
    )(place, *map(in_hbm, (*x_a, *x_b)), gain, bias, in_hbm(w), in_hbm(w), b, in_hbm(table))


AQ = 512
AK = 256
NQ = LEN // AQ


def padded_turned(ref, scr):
    row = lax.broadcasted_iota(jnp.int32, (128, AQ), 0)
    for i in range(NQ):
        cols = slice(i * AQ, (i + 1) * AQ)
        t = ref[cols, :].astype(F32).T
        scr[0, :, cols] = jnp.where(row < 64, t, 0.0).astype(BF)
        scr[1, :, cols] = jnp.where(row < 64, 0.0, t).astype(BF)


def padded(ref, scr):
    lane = lax.broadcasted_iota(jnp.int32, (AQ, 128), 1)
    for i in range(NQ):
        rows = slice(i * AQ, (i + 1) * AQ)
        v = ref[rows, :].astype(F32)
        scr[0, rows, :] = jnp.where(lane < 64, v, 0.0).astype(BF)
        scr[1, rows, :] = jnp.where(lane < 64, 0.0, v).astype(BF)


def fold(op, v):
    return op(v.reshape(AK // 8, 8, v.shape[1]), axis=0)


def key_bounds(bounds_ref, i):
    low = bounds_ref[i]
    return low, jnp.clip(bounds_ref[NQ + i], low, 2 * i)


def right_half(old, new):
    return jnp.concatenate([old[:, :AK], new], axis=1)


def attend_body(first_ref, qkv_ref, start_ref, att_ref, lse_ref, qt_scr, vt_scr, s_scr):
    padded_turned(qkv_ref.at[:, 0:128], qt_scr)
    for i in range(NQ):
        rows = slice(i * AQ, (i + 1) * AQ)
        vt_scr[:, rows] = qkv_ref[rows, 256:384].astype(F32).T.astype(BF)
    row = lax.broadcasted_iota(jnp.int32, (AK, AQ), 0)
    col = lax.broadcasted_iota(jnp.int32, (AK, AQ), 1)

    def q_block(i, _):
        cols = pl.ds(pl.multiple_of(i * AQ, AQ), AQ)
        start = start_ref[:, cols]
        qt = [qt_scr[h, :, cols] for h in range(2)]

        def scores(j, ok, peaks):
            rows = pl.ds(pl.multiple_of(j * AK, AK), AK)
            k = qkv_ref[rows, 128:256]
            new = []
            for h in range(2):
                s = jnp.dot(k, qt[h], preferred_element_type=F32)
                if ok is not None:
                    s = jnp.where(ok, s, NEG)
                s_scr[h, rows, :] = s
                new.append(jnp.maximum(peaks[h], fold(jnp.max, s)))
            return tuple(new)

        low, mid = key_bounds(first_ref, i)
        peaks = (jnp.full((8, AQ), NEG, F32),) * 2
        peaks = scores(2 * i, (row + 2 * i * AK >= start) & (row <= col), peaks)
        last = pl.ds(pl.multiple_of((2 * i + 1) * AK, AK), AK)
        corner = (row[:, :AK] + (2 * i + 1) * AK >= start[:, AK:]) & (row[:, :AK] <= col[:, :AK])
        new = []
        for h in range(2):
            s = jnp.dot(qkv_ref[last, 128:256], qt[h][:, AK:], preferred_element_type=F32)
            s = jnp.where(corner, s, NEG)
            s_scr[h, last, AK:] = s
            new.append(right_half(peaks[h], jnp.maximum(peaks[h][:, AK:], fold(jnp.max, s))))
        peaks = lax.fori_loop(low, mid, lambda j, p: scores(j, row + j * AK >= start, p), tuple(new))
        peaks = lax.fori_loop(mid, 2 * i, lambda j, p: scores(j, None, p), peaks)
        peak = [jnp.max(p, axis=0, keepdims=True) for p in peaks]

        def values(j, state):
            rows = pl.ds(pl.multiple_of(j * AK, AK), AK)
            new = []
            for h in range(2):
                total, o = state[2 * h : 2 * h + 2]
                p = jnp.exp(s_scr[h, rows, :] - peak[h])
                total = total + fold(jnp.sum, p)
                o = o + jnp.dot(
                    vt_scr[64 * h : 64 * h + 64, rows], p.astype(BF), preferred_element_type=F32
                )
                new += [total, o]
            return tuple(new)

        state = (jnp.zeros((8, AQ), F32), jnp.zeros((64, AQ), F32)) * 2
        state = list(lax.fori_loop(low, 2 * i + 1, values, state))
        for h in range(2):
            total, o = state[2 * h : 2 * h + 2]
            p = jnp.exp(s_scr[h, last, AK:] - peak[h][:, AK:])
            more = jnp.dot(vt_scr[64 * h : 64 * h + 64, last], p.astype(BF), preferred_element_type=F32)
            state[2 * h] = right_half(total, total[:, AK:] + fold(jnp.sum, p))
            state[2 * h + 1] = right_half(o, o[:, AK:] + more)
        total = [jnp.sum(state[2 * h], axis=0, keepdims=True) for h in range(2)]
        both = jnp.concatenate([state[1] / total[0], state[3] / total[1]], axis=0)
        att_ref[cols, :] = both.T.astype(BF)
        for h in range(2):
            lse_ref[h : h + 1, cols] = peak[h] + jnp.log(total[h])
        return 0

    lax.fori_loop(0, NQ, q_block, 0)


def attend(first, qkv, start):
    return pl.pallas_call(
        attend_body,
        in_specs=[SM, VM, VM],
        out_specs=[VM, VM],
        out_shape=[
            jax.ShapeDtypeStruct((LEN, ATT), BF),
            jax.ShapeDtypeStruct((2, LEN), F32),
        ],
        scratch_shapes=[
            pltpu.VMEM((2, 128, LEN), BF),
            pltpu.VMEM((128, LEN), BF),
            pltpu.VMEM((2, LEN, AQ), F32),
        ],
        cost_estimate=LARGE,
        compiler_params=pltpu.CompilerParams(vmem_limit_bytes=24 * 2**20),
        name="attend",
    )(first, qkv, start)


def attend_back_body(
    first_ref, qkv_ref, att_ref, ga_ref, lse_ref, start_ref, table_ref,
    gqkv_ref, bsum_ref,
    q_scr, go_scr, qt_scr, got_scr, kt_scr, dl_scr, dk_scr, dv_scr,
):
    padded(qkv_ref.at[:, 0:128], q_scr)
    padded(ga_ref, go_scr)
    padded_turned(qkv_ref.at[:, 0:128], qt_scr)
    for i in range(NQ):
        rows = slice(i * AQ, (i + 1) * AQ)
        kt_scr[:, rows] = qkv_ref[rows, 128:256].astype(F32).T.astype(BF)
        got = ga_ref[rows, :].astype(F32).T
        prod = got * att_ref[rows, :].astype(F32).T
        row = lax.broadcasted_iota(jnp.int32, (128, AQ), 0)
        got_scr[0, :, rows] = jnp.where(row < 64, got, 0.0).astype(BF)
        got_scr[1, :, rows] = jnp.where(row < 64, 0.0, got).astype(BF)
        for h in range(2):
            dl_scr[h : h + 1, rows] = jnp.sum(prod[64 * h : 64 * h + 64], axis=0, keepdims=True)
    dk_scr[...] = jnp.zeros_like(dk_scr)
    dv_scr[...] = jnp.zeros_like(dv_scr)
    row = lax.broadcasted_iota(jnp.int32, (AK, AQ), 0)
    col = lax.broadcasted_iota(jnp.int32, (AK, AQ), 1)

    def q_block(i, bsum):
        cols = pl.ds(pl.multiple_of(i * AQ, AQ), AQ)
        start = start_ref[:, cols]
        lse = [lse_ref[h : h + 1, cols] for h in range(2)]
        dl = [dl_scr[h : h + 1, cols] for h in range(2)]

        def pair(j, ok, dq, half=False):
            rows = pl.ds(pl.multiple_of(j * AK, AK), AK)
            mine = pl.ds(pl.multiple_of(i * AQ + AK, AK), AK) if half else cols
            part = slice(AK, None) if half else slice(None)
            k = qkv_ref[rows, 128:256]
            v = qkv_ref[rows, 256:384]
            dv = dk = 0.0
            new = []
            for h in range(2):
                s = jnp.dot(k, qt_scr[h, :, mine], preferred_element_type=F32)
                dp = jnp.dot(v, got_scr[h, :, mine], preferred_element_type=F32)
                p = jnp.exp(s - lse[h][:, part])
                if ok is not None:
                    p = jnp.where(ok, p, 0.0)
                ds = (p * (dp - dl[h][:, part])).astype(BF)
                dv += jnp.dot(p.astype(BF), go_scr[h, mine, :], preferred_element_type=F32)
                dk += jnp.dot(ds, q_scr[h, mine, :], preferred_element_type=F32)
                more = jnp.dot(kt_scr[64 * h : 64 * h + 64, rows], ds, preferred_element_type=F32)
                new.append(right_half(dq[h], dq[h][:, AK:] + more) if half else dq[h] + more)
            dv_scr[rows, :] += dv
            dk_scr[rows, :] += dk
            return tuple(new)

        low, mid = key_bounds(first_ref, i)
        dq = (jnp.zeros((64, AQ), F32),) * 2
        dq = pair(2 * i, (row + 2 * i * AK >= start) & (row <= col), dq)
        corner = (row[:, :AK] + (2 * i + 1) * AK >= start[:, AK:]) & (row[:, :AK] <= col[:, :AK])
        dq = pair(2 * i + 1, corner, dq, half=True)
        dq = lax.fori_loop(low, mid, lambda j, dq: pair(j, row + j * AK >= start, dq), dq)
        dq = lax.fori_loop(mid, 2 * i, lambda j, dq: pair(j, None, dq), dq)
        dq = (jnp.concatenate(dq, axis=0) * 0.125).T
        out = turn(dq, table_ref[cols, :], -1.0).astype(BF)
        gqkv_ref[cols, 0:128] = out
        return bsum + jnp.sum(out.astype(F32), axis=0, keepdims=True)

    bsum_ref[:, 0:128] = lax.fori_loop(0, NQ, q_block, jnp.zeros((1, 128), F32))

    def finish(i, total):
        rows = pl.ds(pl.multiple_of(i * AQ, AQ), AQ)
        dk = turn(dk_scr[rows, :], table_ref[rows, :], -1.0)
        out = jnp.concatenate([dk, dv_scr[rows, :]], axis=1).astype(BF)
        gqkv_ref[rows, 128:384] = out
        return total + jnp.sum(out.astype(F32), axis=0, keepdims=True)

    bsum_ref[:, 128:384] = lax.fori_loop(0, NQ, finish, jnp.zeros((1, 256), F32))


def attend_back(first, qkv, att, ga, lse, start, table):
    return pl.pallas_call(
        attend_back_body,
        in_specs=[SM] + [VM] * 6,
        out_specs=[VM, VM],
        out_shape=[
            jax.ShapeDtypeStruct((LEN, QKV), BF),
            jax.ShapeDtypeStruct((1, QKV), F32),
        ],
        scratch_shapes=[
            pltpu.VMEM((2, LEN, 128), BF),
            pltpu.VMEM((2, LEN, 128), BF),
            pltpu.VMEM((2, 128, LEN), BF),
            pltpu.VMEM((2, 128, LEN), BF),
            pltpu.VMEM((128, LEN), BF),
            pltpu.VMEM((2, LEN), F32),
            pltpu.VMEM((LEN, 128), F32),
            pltpu.VMEM((LEN, 128), F32),
        ],
        cost_estimate=LARGE,
        compiler_params=pltpu.CompilerParams(vmem_limit_bytes=24 * 2**20),
        name="attend_back",
    )(first, qkv, att, ga, lse, start, table)


def emit_body(att_ref, act_ref, w_ref, out_ref):
    both = jnp.concatenate([att_ref[...], act_ref[...]], axis=1)
    for f in range(FS):
        out_ref[:, f * PIECE : (f + 1) * PIECE] = jnp.dot(
            both, w_ref[f, 0, 128:], preferred_element_type=F32
        ).astype(BF)


def emit(att, act, w):
    return pl.pallas_call(
        emit_body,
        grid=(LEN // ROWS,),
        in_specs=[rows_of(ATT), rows_of(HID), pl.BlockSpec((FS, 1, 768, PIECE), lambda i, *_: (0, 1, 0, 0))],
        out_specs=rows_of(D),
        out_shape=pltpu.HBM((LEN, D), BF),
        cost_estimate=LARGE,
        compiler_params=params(24),
        name="emit",
    )(att, act, w)


def emit_back_body(g_ref, w_ref, slope_ref, ga_ref, gh_ref, bsum_ref):
    total = jnp.zeros((ROWS, ATT + HID), F32)
    for f in range(FS):
        total += lax.dot_general(
            g_ref[:, f * PIECE : (f + 1) * PIECE], w_ref[f, 0, 128:], (((1,), (1,)), ((), ())),
            preferred_element_type=F32,
        )
    ga_ref[...] = total[:, :ATT].astype(BF)
    gh = (total[:, ATT:] * slope_ref[...].astype(F32)).astype(BF)
    gh_ref[...] = gh

    @pl.when(pl.program_id(0) == 0)
    def _():
        bsum_ref[...] = jnp.zeros_like(bsum_ref)

    bsum_ref[...] += jnp.sum(gh.astype(F32), axis=0, keepdims=True)


def emit_back(g, w, slope):
    return pl.pallas_call(
        emit_back_body,
        grid=(LEN // ROWS,),
        in_specs=[rows_of(D), pl.BlockSpec((FS, 1, 768, PIECE), lambda i: (0, 1, 0, 0)), rows_of(HID)],
        out_specs=[rows_of(ATT), rows_of(HID), whole((1, HID))],
        out_shape=[
            jax.ShapeDtypeStruct((LEN, ATT), BF),
            jax.ShapeDtypeStruct((LEN, HID), BF),
            jax.ShapeDtypeStruct((1, HID), F32),
        ],
        cost_estimate=LARGE,
        compiler_params=params(26),
        name="emit_back",
    )(in_hbm(g), in_hbm(w), slope)


ALLW = QKV + ATT + 2 * HID
EXTRA = 16


def weight_grads_body(att_ref, act_ref, gh_ref, gqkv_ref, g_ref, normed_ref, out_ref, turned):
    @pl.when(pl.program_id(0) == 0)
    def _():
        for block in range(8):
            rows = slice(block * PIECE, (block + 1) * PIECE)
            at = 0
            for ref, n in ((att_ref, ATT), (act_ref, HID), (gh_ref, HID), (gqkv_ref, QKV)):
                turned[at : at + n, rows] = ref[rows, :].T
                at += n

    cut = ATT + HID
    out_ref[0, :cut] = jnp.dot(turned[:cut], g_ref[...], preferred_element_type=F32).astype(BF)
    out_ref[0, cut:ALLW] = jnp.dot(turned[cut:], normed_ref[...], preferred_element_type=F32).astype(BF)
    out_ref[0, ALLW:] = jnp.zeros((EXTRA, PIECE), BF)


def column_piece():
    return pl.BlockSpec((LEN, PIECE), lambda i: (0, i))


def weight_grads(att, act, gh, gqkv, g, normed):
    return pl.pallas_call(
        weight_grads_body,
        grid=(FS,),
        in_specs=[
            whole((LEN, ATT)), whole((LEN, HID)), whole((LEN, HID)), whole((LEN, QKV)),
            column_piece(), column_piece(),
        ],
        out_specs=pl.BlockSpec((1, ALLW + EXTRA, PIECE), lambda i: (i, 0, 0)),
        scratch_shapes=[pltpu.VMEM((ALLW, LEN), BF)],
        out_shape=pltpu.HBM((FS, ALLW + EXTRA, PIECE), BF),
        cost_estimate=LARGE,
        compiler_params=params(34),
        name="weight_grads",
    )(att, act, gh, gqkv, in_hbm(g), in_hbm(normed))


def unpack_body(sums_ref, qkv_ref, out_ref, fc1_ref, fc2_ref, small_ref):
    out_ref[...] = sums_ref[0, :ATT].astype(F32)
    fc2_ref[...] = sums_ref[0, ATT : ATT + HID].astype(F32)
    fc1_ref[...] = sums_ref[0, ATT + HID : ATT + 2 * HID].astype(F32).T
    at = ATT + 2 * HID
    q, k, v = [sums_ref[0, at + n * 128 : at + (n + 1) * 128].astype(F32).T for n in range(3)]
    low = lax.broadcasted_iota(jnp.int32, (PIECE, 128), 1) < 64
    qkv_ref[:, 0:128] = jnp.where(low, q, pltpu.roll(k, 64, 1))
    qkv_ref[:, 128:256] = jnp.where(low, v, q)
    qkv_ref[:, 256:384] = jnp.where(low, pltpu.roll(k, 64, 1), v)
    small_ref[...] = sums_ref[0, ALLW:].astype(F32)


def unpack(sums):
    shapes = [(PIECE, QKV), (ATT, PIECE), (PIECE, HID), (HID, PIECE), (EXTRA, PIECE)]
    return pl.pallas_call(
        unpack_body,
        in_specs=[VM],
        out_specs=[VM] * 5,
        out_shape=[jax.ShapeDtypeStruct(shape, F32) for shape in shapes],
        cost_estimate=SMALL,
        compiler_params=pltpu.CompilerParams(vmem_limit_bytes=16 * 2**20),
        name="unpack",
    )(sums)


def block_of(pairs, step, side):
    block = jnp.int32(pairs[0][side])
    for k in range(1, len(pairs)):
        block = jnp.where(step == k, pairs[k][side], block)
    return block


def input_back_body(pairs, place_ref, gqkv_ref, gh_ref, w_ref, wl_ref, *refs):
    step = pl.program_id(0)
    normed_refs, refs = refs[:8], refs[8:]
    sums_ref, last_ref, out_scr = refs[-3:]
    far = len(pairs) == 1
    got_refs, out_refs = ((), refs[:-3]) if far else (refs[:4], refs[4:-3])
    blocks = [block_of(pairs, step, side) for side in range(2)]

    def pieces(ref):
        return jnp.concatenate([gather_pieces(place_ref, ref, block) for block in blocks], axis=0)

    both = jnp.concatenate([pieces(gqkv_ref), pieces(gh_ref)], axis=1)

    @pl.when(step == 0)
    def _():
        sums_ref[...] = jnp.zeros_like(sums_ref)
        unpack_last(wl_ref, last_ref)

    turned = (((1,), (1,)), ((), ()))
    for f in range(FS):
        cols = slice(f * PIECE, (f + 1) * PIECE)
        part = lax.dot_general(both[:, 768:], last_ref[cols, :], turned, preferred_element_type=F32)
        for j in range(3):
            part += lax.dot_general(
                both[:, j * 256 : (j + 1) * 256], w_ref[f, 0, j * 256 : (j + 1) * 256], turned,
                preferred_element_type=F32,
            )
        out_scr[:, cols] = part
        normed = jnp.concatenate([ref[0, 0, :, cols] for ref in normed_refs], axis=0).astype(F32)
        sums_ref[0:1, cols] += jnp.sum(part, axis=0, keepdims=True)
        sums_ref[1:2, cols] += jnp.sum(part * normed, axis=0, keepdims=True)
    if far:
        for k in range(4):
            out_refs[k][...] = out_scr[k * 128 : (k + 1) * 128, :].astype(BF)
        return
    for k in range(3):

        @pl.when(step == k)
        def _():
            for side in range(2):
                for part in range(2):
                    at = side * PIECE + part * 128
                    v = out_scr[at : at + 128, :]
                    if k == part:
                        v += got_refs[2 * side + part][...].astype(F32)
                    out_refs[2 * k + side][part * 128 : (part + 1) * 128, :] = v.astype(BF)


def piece_spec(pairs, m):
    def where_to(i, place_ref):
        start = piece_start(place_ref, block_of(pairs, i, m // 4), m % 4)
        return (start // TOK, m // 4, 0, 0)

    return pl.BlockSpec((1, 1, HALF, D), where_to)


def input_back(pairs, place, gqkv, gh, w, normed, got=()):
    n = len(pairs)
    outs = [(128, D)] * 4 if n == 1 else [(PIECE, D)] * 6
    return pl.pallas_call(
        functools.partial(input_back_body, pairs),
        grid_spec=pltpu.PrefetchScalarGridSpec(
            num_scalar_prefetch=1,
            grid=(n,),
            in_specs=[whole((LEN, QKV)), whole((LEN, HID)), W_FIRST, W_LAST]
            + [piece_spec(pairs, m) for m in range(8)]
            + [whole((128, D))] * len(got),
            out_specs=[whole(shape) for shape in outs] + [whole((2, D))],
            scratch_shapes=[pltpu.VMEM((D, 128), BF), pltpu.VMEM((2 * PIECE, D), F32)],
        ),
        out_shape=[pltpu.HBM(shape, BF) for shape in outs] + [jax.ShapeDtypeStruct((2, D), F32)],
        cost_estimate=LARGE,
        compiler_params=params(44),
        name="input_back",
    )(place, gqkv, gh, in_hbm(w), in_hbm(w), *[in_hbm(normed.reshape(16, 2, HALF, D))] * 8, *got)


def copy_body(moves, n_in, in_hbm_out, place_ref, *refs):
    n_out = len(refs) - n_in - 1
    if in_hbm_out:
        n_out //= 2
    ins, outs, sem = refs[:n_in], refs[n_in : n_in + n_out], refs[-1]
    to = refs[n_in + n_out : -1] if in_hbm_out else outs
    copies = [
        pltpu.make_async_copy(src(ins), dst(to, place_ref), sem.at[k]) for k, (src, dst) in enumerate(moves)
    ]
    for copy in copies:
        copy.start()
    for copy in copies:
        copy.wait()
    if in_hbm_out:
        copies = [pltpu.make_async_copy(scr, out, sem.at[k]) for k, (scr, out) in enumerate(zip(to, outs))]
        for copy in copies:
            copy.start()
        for copy in copies:
            copy.wait()


def copy_kernel(name, moves, place, ins, out_shapes, in_hbm_out=False):
    n = len(out_shapes)
    return pl.pallas_call(
        functools.partial(copy_body, moves, len(ins), in_hbm_out),
        in_specs=[SM] + [HBM if in_hbm_out else ANY] * len(ins),
        out_specs=[HBM if in_hbm_out else VM] * n,
        out_shape=[jax.ShapeDtypeStruct(shape, BF) for shape in out_shapes],
        scratch_shapes=[pltpu.VMEM(shape, BF) for shape in out_shapes if in_hbm_out]
        + [pltpu.SemaphoreType.DMA((len(moves),))],
        cost_estimate=SMALL,
        compiler_params=pltpu.CompilerParams(vmem_limit_bytes=58 * 2**20),
        name=name,
    )(place, *(map(in_hbm, ins) if in_hbm_out else ins))


def join(place, pieces_a, pieces_b):
    def move(k):
        axis = 1 - k // 4
        return (
            lambda ins: ins[k],
            lambda outs, place_ref: outs[k // 4].at[lax.rem(place_ref[axis] + k % 4, 4)],
        )

    moves = [move(k) for k in range(8)]
    return copy_kernel("join", moves, place, [*pieces_a, *pieces_b], [(4, TOK, WIDE)] * 2, True)


def halves(place, left_a, right_a, left_b, right_b):
    def move(k):
        spot = slice(k % 2 * 2, k % 2 * 2 + 2)
        return (lambda ins: ins[k].at[spot], lambda outs, place_ref: outs[k])

    moves = [move(k) for k in range(4)]
    return copy_kernel("halves", moves, place, [left_a, right_a, left_b, right_b], [(2, TOK, WIDE)] * 4, True)


def shift(v, axis, by, n=4):
    return lax.ppermute(v, axis, [(i, (i + by) % n) for i in range(n)])


def in_hbm(v):
    return pltpu.with_memory_space_constraint(v, pltpu.HBM)


def tie(v, *others):
    return lax.optimization_barrier((v,) + others)[0]


def plus(a, b):
    return (a.astype(F32) + b.astype(F32)).astype(BF)


def near_sum(own, right, left, axis):
    return own.astype(F32) + shift(right, axis, 1).astype(F32) + shift(left, axis, -1).astype(F32)


def ring_sum_first(parts, axis):
    own, right, far, left = parts
    got = [shift(far, axis, 2), shift(right, axis, 1), shift(left, axis, -1)]
    total = own.astype(F32)
    for v in got:
        total = total + v.astype(F32)
    return total, got[1]


def ring_sum(parts, axis):
    return ring_sum_first(parts, axis)[0]


def quarters(v):
    n = v.shape[0] // 4
    return [v[i * n : (i + 1) * n] for i in range(4)]


def small_gather(v, axes):
    for axis in axes:
        n = 2 if axis == "core" else 4
        me = lax.axis_index(axis)
        out = jnp.zeros((n,) + v.shape, v.dtype)
        out = lax.dynamic_update_index_in_dim(out, v, me, 0)
        for by in range(1, n):
            got = shift(v, axis, by, n)
            out = lax.dynamic_update_index_in_dim(out, got, lax.rem(me + n - by, n), 0)
        v = out
    return v


def small_sum(v, axes):
    for axis, n, dim in axes:
        me = lax.axis_index(axis)
        total = lax.dynamic_index_in_dim(v, me, dim, keepdims=False)
        for by in range(1, n):
            part = lax.dynamic_index_in_dim(v, lax.rem(me + by, n), dim, keepdims=False)
            total = total + shift(part, axis, by, n)
        v = total
    return v


def on_device(
    tokens, cotangent, doc_starts, ln_gain, ln_bias, w_qkv, b_qkv, w_out, b_out, w_fc1, b_fc1, w_fc2, b_fc2,
):
    own = tokens[0]
    own_grad = cotangent[0]
    z_me, x_me = lax.axis_index("z"), lax.axis_index("x")
    seq = z_me * 4 + x_me
    place = jnp.stack([z_me, x_me, lax.axis_index("core"), lax.axis_index("y")]).astype(jnp.int32)

    fsdp = ("y", "core")
    w, vectors, own_a, own_b = pack(
        w_qkv, w_fc1, w_out, w_fc2, ln_gain, ln_bias, b_qkv, b_out, b_fc1, b_fc2, own
    )
    w = lax.all_gather(w, fsdp, axis=0).reshape(FS, 2, 768, PIECE)
    vectors = small_gather(vectors, ("x", "z"))
    vectors, own_a, own_b = lax.optimization_barrier((vectors, own_a, own_b))
    a, b = join(
        place,
        [own_a] + [shift(own_a, "x", -by) for by in (1, 2, 3)],
        [own_b] + [shift(own_b, "z", -by) for by in (1, 2, 3)],
    )
    g = lax.all_gather(tie(own_grad, a), ("z", "x"), axis=0, tiled=True)
    left_a, right_a, left_b, right_b = shift(a, "z", 1), shift(a, "z", -1), shift(b, "x", 1), shift(b, "x", -1)
    far = halves(place, left_a, right_a, left_b, right_b)
    x_a = [a, right_a, shift(far[0], "z", 1), shift(far[1], "z", -1), left_a]
    x_b = [b, right_b, shift(far[2], "x", 1), shift(far[3], "x", -1), left_b]
    vectors = small_gather(vectors, ("y", "core"))
    table, start, first = angles(tie(doc_starts, far[0]))
    vectors = vectors.transpose(1, 0, 2, 3, 4, 5).reshape(128, 8, 128)

    sizes = [16, 16, 48, 16, 64, 16]
    gain, bias, bq, bo, b1, b2 = [vectors[:, k, :n].reshape(1, -1) for k, n in enumerate(sizes)]
    b_in = jnp.concatenate(
        [
            lax.dynamic_slice_in_dim(bq, seq * QKV, QKV, 1).reshape(2, 3, 64).transpose(1, 0, 2).reshape(1, QKV),
            lax.dynamic_slice_in_dim(b1, seq * HID, HID, 1),
        ],
        axis=1,
    )

    normed, qkv, act, slope = project(place, x_a, x_b, gain, bias, w, b_in, table)
    att, lse = attend(first, qkv, start)
    out_part = emit(att, act, w)
    out_sum = lax.psum_scatter(out_part, ("z", "x"), scatter_dimension=0, tiled=True)
    output = (own.astype(F32) + out_sum.astype(F32) + bo + b2).astype(BF)

    ga, gh, b1_sum = emit_back(tie(g, out_part), w, slope)
    gqkv, bq_sum = attend_back(first, qkv, att, ga, lse, start, table)
    bq_sum = bq_sum.reshape(3, 2, 64).transpose(1, 0, 2).reshape(1, QKV)
    far_a0, far_a1, far_b0, far_b1, sums_far = input_back(((2, 6),), place, gqkv, gh, w, normed)
    got = [shift(far_a0, "z", 1), shift(far_a1, "z", -1), shift(far_b0, "x", 1), shift(far_b1, "x", -1)]
    grads = weight_grads(att, act, gh, tie(gqkv, far_a0), g, normed)
    right_a, right_b, left_a, left_b, own_a, own_b, sums = input_back(
        ((1, 5), (3, 7), (0, 4)), place, gqkv, gh, w, tie(normed, grads), got
    )
    sums = sums + sums_far
    wide_grad = own_grad.astype(F32)
    bo_sum = jnp.sum(wide_grad, axis=0, keepdims=True)
    gain_sum = (sums[1:2] - bias * sums[0:1]) / gain
    bq_all = lax.dynamic_update_slice_in_dim(jnp.zeros((1, 16 * QKV), F32), bq_sum, seq * QKV, 1)
    b1_all = lax.dynamic_update_slice_in_dim(jnp.zeros((1, 16 * HID), F32), b1_sum, seq * HID, 1)
    packed = jnp.concatenate(
        [t.reshape(128, -1) for t in (gain_sum, sums[0:1], bq_all, bo_sum, b1_all)], axis=1
    )
    small = small_sum(packed.reshape(4, 2, 4, 4, -1), (("z", 4, 2), ("x", 4, 2)))
    small, right_a, right_b, left_a, left_b = lax.optimization_barrier((small, right_a, right_b, left_a, left_b))
    small = small.reshape(FS, 1, 160).astype(BF)
    grads = lax.dynamic_update_slice(grads, small, (0, ALLW, 0))
    grads = lax.psum_scatter(grads, fsdp, scatter_dimension=0, tiled=True)
    grad_qkv, grad_out, grad_fc1, grad_fc2, small = unpack(grads)
    small = small[0, :160]

    a = near_sum(own_a, right_a, left_a, "z").astype(BF)
    b = near_sum(own_b, right_b, left_b, "x").astype(BF)
    a = ring_sum(quarters(a), "x")
    b = ring_sum(quarters(b), "z")
    dn = jnp.concatenate([a, b], axis=0)
    wide = own.astype(F32)
    centered = wide - jnp.mean(wide, axis=1, keepdims=True)
    inv = lax.rsqrt(jnp.mean(centered * centered, axis=1, keepdims=True) + EPS)
    unit = centered * inv
    e = dn * gain
    input_grad = wide_grad + inv * (
        e - jnp.mean(e, axis=1, keepdims=True) - unit * jnp.mean(e * unit, axis=1, keepdims=True)
    )

    return (
        output[None],
        input_grad[None],
        small[0:16],
        small[16:32],
        grad_qkv,
        small[32:80],
        grad_out,
        small[80:96],
        grad_fc1,
        small[96:160],
        grad_fc2,
        small[80:96],
    )


def solution(mesh):
    split = Mesh(mesh.devices.reshape(4, 2, 4, 4), ("y", "core", "z", "x"))
    f, s = ("y", "core"), ("z", "x")
    both = f + s
    in_specs = (
        P(f, s, None), P(f, s, None), P(f, None), P(both), P(both), P(f, s), P(both), P(s, f), P(both),
        P(f, s), P(both), P(s, f), P(both),
    )
    out_specs = (
        P(f, s, None), P(f, s, None), P(both), P(both), P(f, s), P(both), P(s, f), P(both), P(f, s),
        P(both), P(s, f), P(both),
    )
    return jax.shard_map(on_device, mesh=split, in_specs=in_specs, out_specs=out_specs, check_vma=False)
```
